32 devices in a mesh: fsdp: 32 (over z, y, x, core).
Axes of the slice: x: 2, y: 2, z: 4, core: 2. Of those that a mesh axis runs over, the one named last changes fastest.
Arguments:
- tokens: bfloat16 [65536, 768], P('fsdp'), may hold values from -6 to 6
- mol_len: int32 [256], P('fsdp'), may hold values from 0 to 256, as said below
- cotangent: bfloat16 [65536, 768], P('fsdp'), may hold values from -6 to 6
- ln1_gain: bfloat16 [768], P('fsdp'), may hold values from 0.5 to 1.5
- ln1_bias: bfloat16 [768], P('fsdp'), may hold values from -1 to 1
- w_qkv: bfloat16 [768, 2304], P('fsdp'), may hold values from -0.21875 to 0.21875
- q_bias: bfloat16 [768], P('fsdp'), may hold values from -1 to 1
- v_bias: bfloat16 [768], P('fsdp'), may hold values from -1 to 1
- w_out: bfloat16 [768, 768], P('fsdp'), may hold values from -1.25 to 1.25
- out_bias: bfloat16 [768], P('fsdp'), may hold values from -1 to 1
- ln2_gain: bfloat16 [768], P('fsdp'), may hold values from 0.5 to 1.5
- ln2_bias: bfloat16 [768], P('fsdp'), may hold values from -1 to 1
- w_in: bfloat16 [768, 768], P('fsdp'), may hold values from -0.21875 to 0.21875
- in_bias: bfloat16 [768], P('fsdp'), may hold values from -1 to 1
- w_back: bfloat16 [768, 768], P('fsdp'), may hold values from -0.21875 to 0.21875
- back_bias: bfloat16 [768], P('fsdp'), may hold values from -1 to 1
Outputs:
- mixed_out: bfloat16 [65536, 768], P('fsdp')
- token_grad: bfloat16 [65536, 768], P('fsdp')
- grad_ln1_gain: float32 [768], P('fsdp')
- grad_ln1_bias: float32 [768], P('fsdp')
- grad_w_qkv: float32 [768, 2304], P('fsdp')
- grad_q_bias: float32 [768], P('fsdp')
- grad_v_bias: float32 [768], P('fsdp')
- grad_w_out: float32 [768, 768], P('fsdp')
- grad_out_bias: float32 [768], P('fsdp')
- grad_ln2_gain: float32 [768], P('fsdp')
- grad_ln2_bias: float32 [768], P('fsdp')
- grad_w_in: float32 [768, 768], P('fsdp')
- grad_in_bias: float32 [768], P('fsdp')
- grad_w_back: float32 [768, 768], P('fsdp')
- grad_back_bias: float32 [768], P('fsdp')
The draws below stay inside these ranges and needn't reach their ends.
Inputs may be any that keep to these rules, and one draw needn't show every extreme that they name: `mol_len`: each slot of 256 tokens holds one molecule or is empty; the first slot of every device is used; on one device every slot is used and one slot is full, on another only the first is used.
All inputs are finite; a program needn't handle non-finite values.
Results may differ from the reference program's by a relative error of at most 0.012.
Values may be sent and summed in bfloat16 or wider, within the bound.
A program may use at most 192 MiB of HBM per device.

```python
import jax
import jax.numpy as jnp
from jax import lax

D = 768
HEADS = 32
FF = 768
BLOCK = 256
BLOCKS_DEV = 8
BLOCKS = 256
TOKENS = 65536


def draw_mol_len(key, part):
    key = jax.random.fold_in(key, 11)
    devices = BLOCKS // BLOCKS_DEV
    count_key, length_key, pick_key = jax.random.split(key, 3)
    device_ids = jnp.arange(devices)
    counts = jax.random.randint(count_key, (devices,), 1, BLOCKS_DEV + 1)
    full_device = jax.random.randint(pick_key, (), 0, devices)
    counts = jnp.where(device_ids == full_device, BLOCKS_DEV, counts)
    counts = jnp.where(device_ids == (full_device + 1) % devices, 1, counts)
    lengths = jax.random.randint(length_key, (devices, BLOCKS_DEV), BLOCK // 16 + 1, BLOCK + 1)
    block_slots = jnp.arange(BLOCKS_DEV)
    lengths = jnp.where((device_ids[:, None] == full_device) & (block_slots[None, :] == 0), BLOCK, lengths)
    lengths = jnp.where(block_slots[None, :] < counts[:, None], lengths, 0)
    return lengths.reshape(BLOCKS).astype(jnp.int32)


def strengthened(entries, key, source, target, shards_of, factor):
    def block_of(dim):
        return (jnp.arange(entries.shape[dim]) // (entries.shape[dim] // shards_of)).reshape((-1,) + (1,) * (entries.ndim - 1 - dim))

    one_side = jax.random.permutation(key, shards_of)[block_of(target)]
    other_side = (block_of(target) + shards_of // 2) % shards_of
    return jnp.where((block_of(source) == one_side) | (block_of(source) == other_side), factor * entries, entries)


def steps_of(own_key, extent, cuts, smallest, largest):
    level = 1.0
    for axis_at, blocks in cuts:
        draws = jax.random.uniform(jax.random.fold_in(jax.random.fold_in(own_key, 6), axis_at), (blocks,), jnp.float32, smallest / len(cuts), largest / len(cuts))
        level = level * jnp.repeat(jnp.exp(draws), extent[axis_at] // blocks).reshape((-1,) + (1,) * (len(extent) - 1 - axis_at))
    return level


def noise(own_key, dims, width, limit, cuts=(), kind=jnp.bfloat16):
    values = jax.random.normal(own_key, dims, jnp.float32) * width
    if len(cuts) > 0:
        values = steps_of(own_key, dims, cuts, -0.22, 0.18) * values
    return jnp.clip(values, min=-limit, max=limit).astype(kind)


def bell_draw_with(stream_key, extent, width, reach, shards, heavy, kind=jnp.bfloat16):
    values = width * jax.random.normal(stream_key, extent, jnp.float32)
    if shards:
        values = values * steps_of(stream_key, extent, shards, -0.22, 0.18)
    return jnp.clip(strengthened(values, jax.random.fold_in(stream_key, 3), *heavy), -reach, reach).astype(kind)


def setup_inputs(seed: int = 0) -> dict:
    arg_keys = jax.random.split(jax.random.key(seed), 17)
    tokens = noise(arg_keys[0], (TOKENS, D), 1.0, 6.0, ((0, 32),))
    mol_len = draw_mol_len(jax.random.fold_in(arg_keys[16], 71), 0)
    cotangent = bell_draw_with(arg_keys[2], (TOKENS, D), 1.0, 6.0, ((0, 32),), (0, 1, 32, 2.75))
    ln1_gain = jnp.clip(1.0 + 0.1 * jax.random.normal(arg_keys[3], (D,), jnp.float32), 0.5, 1.5).astype(jnp.bfloat16)
    ln1_bias = noise(arg_keys[4], (D,), 0.2, 1.0, ((0, 32),))
    w_qkv = noise(arg_keys[5], (D, 3 * D), D ** -0.5, 0.21875, ((0, 32),))
    q_bias = noise(arg_keys[6], (D,), 0.2, 1.0, ((0, 32),))
    v_bias = noise(arg_keys[7], (D,), 0.2, 1.0, ((0, 32),))
    w_out = noise(arg_keys[8], (D, D), (D // 32) ** -0.5, 1.25, ((0, 32),))
    out_bias = noise(arg_keys[9], (D,), 0.2, 1.0, ((0, 32),))
    ln2_gain = jnp.clip(1.0 + 0.1 * jax.random.normal(arg_keys[10], (D,), jnp.float32), 0.5, 1.5).astype(jnp.bfloat16)
    ln2_bias = noise(arg_keys[11], (D,), 0.2, 1.0, ((0, 32),))
    w_in = noise(arg_keys[12], (D, FF), D ** -0.5, 0.21875, ((0, 32),))
    in_bias = noise(arg_keys[13], (FF,), 0.2, 1.0, ((0, 32),))
    w_back = noise(arg_keys[14], (FF, D), FF ** -0.5, 0.21875, ((0, 32),))
    back_bias = noise(arg_keys[15], (D,), 0.2, 1.0, ((0, 32),))
    return dict(tokens=tokens, mol_len=mol_len, cotangent=cotangent, ln1_gain=ln1_gain, ln1_bias=ln1_bias, w_qkv=w_qkv, q_bias=q_bias, v_bias=v_bias, w_out=w_out, out_bias=out_bias, ln2_gain=ln2_gain, ln2_bias=ln2_bias, w_in=w_in, in_bias=in_bias, w_back=w_back, back_bias=back_bias)


@jax.custom_vjp
def low(v):
    return lax.optimization_barrier(v.astype(jnp.bfloat16)).astype(jnp.float32)

@jax.custom_vjp
def low_back(v):
    return v

def low_keep(v):
    return (low(v), None)

def low_pass(kept, grad):
    return (grad,)

def back_keep(v):
    return (v, None)

def back_low(kept, grad):
    return (low(grad),)
low.defvjp(low_keep, low_pass)
low_back.defvjp(back_keep, back_low)
eps = 1e-05
masked_score = -1e+30
highest = lax.Precision.HIGHEST

def layer_norm(values, norm_gain, norm_shift):
    row_mean = lax.optimization_barrier(jnp.mean(values, axis=-1, keepdims=True))
    centred = values - row_mean
    spread = lax.optimization_barrier(jnp.mean(centred * centred, axis=-1, keepdims=True))
    return centred * lax.rsqrt(spread + eps) * norm_gain + norm_shift

def matmul(left, right):
    return jnp.dot(left, right, precision=highest, preferred_element_type=jnp.float32)

def tile_forward(params, inputs, row_valid, allowed):
    gain_one, bias_one, w_qkv, q_bias, v_bias, w_out, out_bias, gain_two, bias_two, w_in, in_bias, w_back, back_bias = params
    row_count = inputs.shape[0]
    head_dim = D // HEADS
    normed_one = low(layer_norm(inputs, gain_one, bias_one))
    qkv_full = matmul(normed_one, w_qkv)
    queries = low_back(low(qkv_full[:, :D] + q_bias)).reshape(row_count, HEADS, head_dim)
    keys_all = low_back(low(qkv_full[:, D:2 * D])).reshape(row_count, HEADS, head_dim)
    values_all = low_back(low(qkv_full[:, 2 * D:] + v_bias)).reshape(row_count, HEADS, head_dim)
    scores = jnp.einsum('qhd,khd->hqk', queries, keys_all, precision=highest) * head_dim ** (-0.5)
    scores = low_back(scores)
    masked = jnp.where(allowed[None], scores, masked_score)
    soft_probs = low(jax.nn.softmax(masked, axis=-1))
    context = jnp.einsum('hqk,khd->qhd', soft_probs, values_all, precision=highest).reshape(row_count, D)
    context = low_back(low(context))
    attn_out = low_back(matmul(context, w_out) + out_bias)
    mixed = inputs + row_valid * attn_out
    normed_two = low(layer_norm(mixed, gain_two, bias_two))
    pre_act = low_back(matmul(normed_two, w_in) + in_bias)
    activation = low(jax.nn.gelu(pre_act, approximate=False))
    branch = low_back(matmul(activation, w_back) + back_bias)
    return mixed + row_valid * branch

def reference(tokens, mol_len, cotangent, ln1_gain, ln1_bias, w_qkv, q_bias, v_bias, w_out, out_bias, ln2_gain, ln2_bias, w_in, in_bias, w_back, back_bias):
    params = tuple((weight.astype(jnp.float32) for weight in (ln1_gain, ln1_bias, w_qkv, q_bias, v_bias, w_out, out_bias, ln2_gain, ln2_bias, w_in, in_bias, w_back, back_bias)))
    tile_rows = 2 * BLOCK
    tile_count = TOKENS // tile_rows
    inputs = tokens.astype(jnp.float32).reshape(tile_count, tile_rows, D)
    upstream = cotangent.astype(jnp.float32).reshape(tile_count, tile_rows, D)
    tile_lengths = mol_len.reshape(tile_count, 2)
    positions = jnp.arange(BLOCK, dtype=jnp.int32)
    block_of = jnp.arange(tile_rows, dtype=jnp.int32) // BLOCK
    same_block = block_of[:, None] == block_of[None, :]

    def scan_step(totals, tile_item):
        tile_inputs, tile_upstream, lengths = tile_item
        live_keys = (positions[None, :] < lengths[:, None]).reshape(tile_rows)
        row_valid = live_keys.astype(jnp.float32)[:, None]
        allowed = same_block & live_keys[None, :]

        def forward(weights, values):
            return tile_forward(weights, values, row_valid, allowed)
        tile_out, pullback = jax.vjp(forward, params, tile_inputs)
        grad_params, grad_inputs = pullback(tile_upstream)
        totals = jax.tree.map(jnp.add, totals, grad_params)
        return (totals, (tile_out, grad_inputs))
    zero_grads = tuple((jnp.zeros_like(weight) for weight in params))
    grads, (outputs, input_grads) = lax.scan(scan_step, zero_grads, (inputs, upstream, tile_lengths))
    mixed_out = outputs.reshape(TOKENS, D).astype(jnp.bfloat16)
    token_grad = input_grads.reshape(TOKENS, D).astype(jnp.bfloat16)
    return (mixed_out, token_grad, grads[0], grads[1], grads[2], grads[3], grads[4], grads[5], grads[6], grads[7], grads[8], grads[9], grads[10], grads[11], grads[12])
```

```python
import functools

import jax
import jax.numpy as jnp
from jax import lax
from jax.experimental import pallas as pl
from jax.experimental.pallas import tpu as pltpu
from jax.sharding import PartitionSpec as P

HEADS = 32

bf16 = jnp.bfloat16
f32 = jnp.float32
eps = 1e-05
masked_score = -1e30
log2_e = 1.4426950408889634
MESH = pl.DeviceIdType.MESH
MIB = 1 << 20

PLANES = 4
CHIPS = 4 * PLANES
DEVICES = 2 * CHIPS
SHARD = 24


def dot(left, right, left_dim, right_dim):
    return lax.dot_general(
        left, right, (((left_dim,), (right_dim,)), ((), ())), preferred_element_type=f32
    )


def normalize(values):
    centred = values - jnp.mean(values, axis=-1, keepdims=True)
    factor = lax.rsqrt(jnp.mean(centred * centred, axis=-1, keepdims=True) + eps)
    return centred * factor, factor


def norm_backward(d_normed, gain, unit, factor):
    e = d_normed * gain
    inner = jnp.mean(e * unit, axis=-1, keepdims=True)
    return factor * (e - jnp.mean(e, axis=-1, keepdims=True) - unit * inner)


def fold_rows(values):
    rows, columns = values.shape
    return jnp.sum(values.reshape(rows // 8, 8, columns), axis=0)


class Place:
    def __init__(self):
        me = lax.axis_index("fsdp")
        self.me = me
        self.c = lax.rem(me, 2)
        self.x = lax.rem(me // 2, 2)
        self.y = lax.rem(me // 4, 2)
        self.z = me // 8
        self.sib = me + 1 - 2 * self.c
        self.xn = me + 2 - 4 * self.x
        self.yn = me + 4 - 8 * self.y
        self.up = me + 8
        self.down = me - 8

    def block(self, c, z, y, x):
        return ((c * PLANES + z) * 2 + y) * 2 + x

    def barrier(self):
        sem = pltpu.get_barrier_semaphore()

        def greet(device):
            pl.semaphore_signal(sem, inc=1, device_id=(device,), device_id_type=MESH)

        for device in (self.sib, self.xn, self.yn):
            greet(device)

        @pl.when(self.z < PLANES - 1)
        def _():
            greet(self.up)

        @pl.when(self.z > 0)
        def _():
            greet(self.down)

        inner = jnp.where((self.z > 0) & (self.z < PLANES - 1), 5, 4)
        pl.semaphore_wait(sem, inner)


def gather_kernel(
    small_ref,
    wq_ref,
    wo_ref,
    wi_ref,
    wb_ref,
    tok_ref,
    qkv_hbm,
    unit_hbm,
    fq_hbm,
    fo_hbm,
    fi_hbm,
    fb_hbm,
    vec_ref,
    gq,
    goi,
    gb,
    fq,
    fo,
    fi,
    fb,
    fq_t,
    unit,
    unit_t,
    qkv,
    bias,
    send_sem,
    recv_sem,
    copy_sem,
):
    at = Place()
    width = tok_ref.shape[1]
    slots, _, block = qkv.shape
    slabs = (gq, goi, gb)
    half_q = 3 * width // 2
    half = width // 2
    own = at.block(at.c, at.z, at.y, at.x)

    gq[own] = jnp.concatenate(
        [
            jnp.concatenate([wq_ref[:, :half_q], wq_ref[:, half_q:]], axis=0),
            jnp.concatenate([small_ref[...], jnp.zeros((2 * SHARD - 16, 128), bf16)], axis=0),
        ],
        axis=1,
    )
    goi[own] = jnp.concatenate([wo_ref[...], wi_ref[...]], axis=0)
    gb[own] = jnp.concatenate([wb_ref[:, :half], wb_ref[:, half:]], axis=0)

    pending = []

    def remote(k, first, count, target, kind):
        view = slabs[k].at[pl.ds(first, count)]
        return pltpu.make_async_remote_copy(
            src_ref=view,
            dst_ref=view,
            send_sem=send_sem.at[k, lax.rem(first, CHIPS), kind],
            recv_sem=recv_sem.at[k, first],
            device_id=(target,),
            device_id_type=MESH,
        )

    def send(k, first, target, kind, count=1, when=None):
        copy = remote(k, first, count, target, kind)
        pending.append((copy, when))

        if when is None:
            copy.start()
        else:
            pl.when(when)(copy.start)

    def arrived(k, first, count=1):
        remote(k, first, count, at.sib, 0).wait_recv()

    below = at.z > 0
    above = at.z < PLANES - 1

    def own_sends(k):
        send(k, own, at.xn, 1)
        send(k, own, at.yn, 2)
        send(k, own, at.up, 3, when=above)
        send(k, own, at.down, 4, when=below)
        send(k, own, at.sib, 0)

    def column(k, s):
        lower = at.z - s >= 0
        upper = at.z + s <= PLANES - 1
        for there, shift, onward, target, kind in (
            (lower, -s, above, at.up, 3),
            (upper, s, below, at.down, 4),
        ):
            b = own + 4 * shift

            @pl.when(there)
            def _():
                arrived(k, b)

            send(k, b, target, kind, when=there & onward)
            send(k, b, at.xn, 1, when=there)
            send(k, b, at.yn, 2, when=there)
            send(k, b, at.sib, 0, when=there)

    def plane(k, s):
        for shift in sorted({-s, s}):
            level = at.z + shift
            there = (level >= 0) & (level <= PLANES - 1)
            even = lax.rem(level, 2) == 0
            for b, target, kind, onward in (
                (at.block(at.c, level, at.y, 1 - at.x), at.yn, 2, even),
                (at.block(at.c, level, 1 - at.y, at.x), at.xn, 1, jnp.logical_not(even)),
            ):

                @pl.when(there)
                def _():
                    arrived(k, b)

                send(k, b, target, kind, when=there & onward)
                send(k, b, at.sib, 0, when=there)

    def corner(k, j):
        b = at.block(at.c, j, 1 - at.y, 1 - at.x)
        arrived(k, b)
        send(k, b, at.sib, 0)

    def others(k):
        for j in range(PLANES):
            for i in range(4):
                arrived(k, (1 - at.c) * CHIPS + 4 * j + i)

    def flat(k):
        even = lax.rem(at.z, 2) == 0
        x_block = at.block(at.c, at.z, at.y, 1 - at.x)
        y_block = at.block(at.c, at.z, 1 - at.y, at.x)
        z_block = at.block(at.c, at.z, 1 - at.y, 1 - at.x)
        arrived(k, x_block)
        send(k, x_block, at.yn, 2, when=even)
        arrived(k, y_block)
        send(k, y_block, at.xn, 1, when=jnp.logical_not(even))
        for b in (x_block, y_block):
            send(k, b, at.up, 3, when=above)
            send(k, b, at.down, 4, when=below)
            send(k, b, at.sib, 0)
        arrived(k, z_block)
        send(k, z_block, at.up, 3, when=above)
        send(k, z_block, at.down, 4, when=below)
        send(k, z_block, at.sib, 0)

    def rise(k, s):
        lower = at.z - s >= 0
        upper = at.z + s <= PLANES - 1
        for there, level, onward, target, kind in (
            (lower, at.z - s, above, at.up, 3),
            (upper, at.z + s, below, at.down, 4),
        ):
            for i in range(4):
                b = at.c * CHIPS + 4 * level + i

                @pl.when(there)
                def _():
                    arrived(k, b)

                send(k, b, target, kind, when=there & onward)
                send(k, b, at.sib, 0, when=there)

    def norm_step(m):
        rows = pl.ds(m * block, block)
        values, _ = normalize(tok_ref[rows].astype(f32))
        unit[rows] = values
        unit_t[:, rows] = values.astype(bf16).T

    at.barrier()
    own_sends(0)
    norm_step(0)
    norm_step(1)
    plane(0, 0)
    column(0, 1)
    norm_step(2)
    norm_step(3)
    plane(0, 1)
    column(0, 2)
    plane(0, 2)
    column(0, 3)
    own_sends(1)
    plane(0, 3)
    norm_step(4)
    norm_step(5)
    for j in range(PLANES):
        corner(0, j)
    own_sends(2)
    norm_step(6)
    norm_step(7)
    unit_copy = pltpu.make_async_copy(unit_t, unit_hbm, copy_sem.at[slots])
    unit_copy.start()
    others(0)

    def strip(i):
        return pl.ds(pl.multiple_of(i * 2 * SHARD, 2 * SHARD), 2 * SHARD)

    def build_q(i, carry):
        first = gq[i].astype(f32)
        second = gq[CHIPS + i].astype(f32)
        fq[strip(i), :half_q] = jnp.concatenate(
            [first[:SHARD, :half_q], second[:SHARD, :half_q]], axis=0
        ).astype(bf16)
        fq[strip(i), half_q:] = jnp.concatenate(
            [first[SHARD:, :half_q], second[SHARD:, :half_q]], axis=0
        ).astype(bf16)
        return carry

    def build_oi(i, carry):
        first = goi[i].astype(f32)
        second = goi[CHIPS + i].astype(f32)
        fo[strip(i)] = jnp.concatenate([first[:SHARD], second[:SHARD]], axis=0).astype(bf16)
        fi[strip(i)] = jnp.concatenate([first[SHARD:], second[SHARD:]], axis=0).astype(bf16)
        return carry

    def build_b(i, carry):
        first = gb[i].astype(f32)
        second = gb[CHIPS + i].astype(f32)
        fb[strip(i), :half] = jnp.concatenate([first[:SHARD], second[:SHARD]], axis=0).astype(bf16)
        fb[strip(i), half:] = jnp.concatenate([first[SHARD:], second[SHARD:]], axis=0).astype(bf16)
        return carry

    lax.fori_loop(0, CHIPS, build_q, 0)
    fq_copy = pltpu.make_async_copy(fq, fq_hbm, copy_sem.at[slots + 1])
    fq_copy.start()
    for part in range(3):
        columns = slice(part * width, (part + 1) * width)
        fq_t[columns] = fq[:, columns].T

    column_at = lax.broadcasted_iota(jnp.int32, (128, width), 1)
    entry = lax.broadcasted_iota(jnp.int32, (128, width), 0)
    spread = jnp.where(lax.rem(column_at, SHARD) == entry, 1.0, 0.0).astype(bf16)
    stacked = jnp.concatenate([gq[p, :16, half_q:] for p in range(DEVICES)], axis=0)
    wide = dot(stacked, spread, 1, 0)
    total = jnp.zeros((16, width), f32)
    column_at = lax.broadcasted_iota(jnp.int32, (16, width), 1)
    for p in range(DEVICES):
        first = SHARD * ((p % CHIPS) * 2 + p // CHIPS)
        mine = (column_at >= first) & (column_at < first + SHARD)
        total = total + jnp.where(mine, wide[16 * p : 16 * p + 16], 0.0)
    vec_ref[...] = total
    bias[:width] = jnp.broadcast_to(total[2:3], (128, width)).T
    bias[width : 2 * width] = jnp.zeros((width, 128), f32)
    bias[2 * width :] = jnp.broadcast_to(total[3:4], (128, width)).T
    gain, shift = total[0:1], total[1:2]

    copies = []

    def qkv_step(m):
        normed = (unit[m * block : (m + 1) * block] * gain + shift).astype(bf16)

        def part_step(part, carry):
            rows = pl.ds(pl.multiple_of(part * width, width), width)
            result = dot(fq_t[rows], normed, 1, 1)
            added = bias[rows]
            qkv[m, rows] = (result + jnp.concatenate([added] * (block // 128), axis=1)).astype(
                bf16
            )
            return carry

        lax.fori_loop(0, 3, part_step, 0)
        copy = pltpu.make_async_copy(qkv.at[m], qkv_hbm.at[m], copy_sem.at[m])
        copy.start()
        copies.append(copy)

    plane(1, 0)
    column(1, 1)
    qkv_step(0)
    plane(1, 1)
    column(1, 2)
    flat(2)
    qkv_step(1)
    plane(1, 2)
    column(1, 3)
    rise(2, 1)
    plane(1, 3)
    qkv_step(2)
    rise(2, 2)
    qkv_step(3)
    rise(2, 3)
    qkv_step(4)
    for j in range(PLANES):
        corner(1, j)
    qkv_step(5)
    qkv_step(6)
    qkv_step(7)
    others(1)
    lax.fori_loop(0, CHIPS, build_oi, 0)
    fo_copy = pltpu.make_async_copy(fo, fo_hbm, copy_sem.at[slots + 2])
    fo_copy.start()
    fi_copy = pltpu.make_async_copy(fi, fi_hbm, copy_sem.at[slots + 3])
    fi_copy.start()
    others(2)
    lax.fori_loop(0, CHIPS, build_b, 0)
    fb_copy = pltpu.make_async_copy(fb, fb_hbm, copy_sem.at[slots + 4])
    fb_copy.start()
    for copy, when in pending:
        if when is None:
            copy.wait_send()
        else:
            pl.when(when)(copy.wait_send)
    for copy in copies + [unit_copy, fq_copy, fo_copy, fi_copy, fb_copy]:
        copy.wait()


def gather_and_project(small, w_qkv, w_out, w_in, w_back, tokens, slots):
    rows, width = tokens.shape
    block = rows // slots
    wide = 3 * width
    vmem = pl.BlockSpec(memory_space=pltpu.VMEM)
    anywhere = pl.BlockSpec(memory_space=pl.ANY)
    square = (width, width)
    return pl.pallas_call(
        gather_kernel,
        out_shape=[
            jax.ShapeDtypeStruct((slots, wide, block), bf16),
            jax.ShapeDtypeStruct((width, rows), bf16),
            jax.ShapeDtypeStruct((width, wide), bf16),
            jax.ShapeDtypeStruct(square, bf16),
            jax.ShapeDtypeStruct(square, bf16),
            jax.ShapeDtypeStruct(square, bf16),
            jax.ShapeDtypeStruct((16, width), f32),
        ],
        in_specs=[vmem] * 6,
        out_specs=[anywhere] * 6 + [vmem],
        scratch_shapes=[
            pltpu.VMEM((DEVICES, 2 * SHARD, wide // 2 + 128), bf16),
            pltpu.VMEM((DEVICES, 2 * SHARD, width), bf16),
            pltpu.VMEM((DEVICES, 2 * SHARD, width // 2), bf16),
            pltpu.VMEM((width, wide), bf16),
            pltpu.VMEM(square, bf16),
            pltpu.VMEM(square, bf16),
            pltpu.VMEM(square, bf16),
            pltpu.VMEM((wide, width), bf16),
            pltpu.VMEM((rows, width), f32),
            pltpu.VMEM((width, rows), bf16),
            pltpu.VMEM((slots, wide, block), bf16),
            pltpu.VMEM((wide, 128), f32),
            pltpu.SemaphoreType.DMA((3, CHIPS, 5)),
            pltpu.SemaphoreType.DMA((3, DEVICES)),
            pltpu.SemaphoreType.DMA((slots + 5,)),
        ],
        compiler_params=pltpu.CompilerParams(
            collective_id=0, has_side_effects=True, vmem_limit_bytes=58 * MIB
        ),
    )(small, w_qkv, w_out, w_in, w_back, tokens)


def middle_kernel(
    packed,
    head_dim,
    len_ref,
    qkv_ref,
    tok_ref,
    cot_ref,
    wout_ref,
    win_ref,
    wback_ref,
    vec_ref,
    mixed_ref,
    dmix_ref,
    dqkv_ref,
    gvec_ref,
    *rest,
):
    if packed:
        soi_ref, sb_ref, gout_ref, gin_ref, gback_ref, probs, ctx_s, linv_s, dctx_s = rest
    else:
        gout_ref, gin_ref, gback_ref, probs, ctx_s, linv_s, dctx_s = rest
    step = pl.program_id(0)
    block, width = tok_ref.shape
    slot = 32
    group = 4
    heads = width // head_dim
    span = group * head_dim
    scale = head_dim ** (-0.5)
    length = len_ref[step]

    @pl.when(step == 0)
    def _():
        gout_ref[...] = jnp.zeros_like(gout_ref)
        gin_ref[...] = jnp.zeros_like(gin_ref)
        gback_ref[...] = jnp.zeros_like(gback_ref)
        gvec_ref[...] = jnp.zeros_like(gvec_ref)

    def run(size):
        extra = (slot - head_dim, size)
        sub = lax.broadcasted_iota(jnp.int32, extra, 0)
        lane = lax.broadcasted_iota(jnp.int32, extra, 1)
        one_row = jnp.where(sub == 0, 1.0, 0.0).astype(f32)
        two_rows = jnp.where(sub <= 1, 1.0, 0.0).astype(f32)
        mask_row = jnp.where((sub == 0) & (lane >= length), masked_score, 0.0).astype(f32)

        def group_rows(base, g):
            return pl.ds(pl.multiple_of(base + g * span, span), span)

        def load(base, g):
            return qkv_ref[group_rows(base, g), :size].astype(f32)

        def place(j, rows):
            parts = []
            if j > 0:
                parts.append(jnp.zeros((slot * j, size), bf16))
            parts.append(rows)
            if j < group - 1:
                parts.append(jnp.zeros((slot * (group - 1 - j), size), bf16))
            return jnp.concatenate(parts, axis=0)

        def pieces(values):
            return [values[head_dim * j : head_dim * (j + 1)] for j in range(group)]

        def padded(values, tail):
            return [jnp.concatenate([p, tail], axis=0).astype(bf16) for p in pieces(values)]

        def forward(g):
            q = padded(load(0, g), one_row)
            k = jnp.concatenate(padded(load(width, g), mask_row), axis=0).T
            v = padded(load(2 * width, g), one_row)
            scores = [dot(k, place(j, q[j]), 1, 0) for j in range(group)]
            ps = []
            for j in range(group):
                peak = jnp.max(scores[j], axis=0, keepdims=True)
                p = jnp.exp2((scores[j] - peak) * (scale * log2_e)).astype(bf16)
                probs[g * group + j, :size, :size] = p
                ps.append(p)
            outs = []
            for j in range(group):
                o = dot(v[j], ps[j], 1, 0)
                inverse = 1.0 / o[head_dim : head_dim + 1]
                linv_s[g * group + j, :, :size] = jnp.broadcast_to(inverse, (8, size))
                outs.append(o[:head_dim] * inverse)
            ctx_s[group_rows(0, g), :size] = jnp.concatenate(outs, axis=0)

        def forward_step(i, carry):
            forward(2 * i)
            forward(2 * i + 1)
            return carry

        lax.fori_loop(0, heads // group // 2, forward_step, 0)

        live = (lax.broadcasted_iota(jnp.int32, (size, 1), 0) < length).astype(f32)
        out_bias, gain, shift = vec_ref[4:5], vec_ref[5:6], vec_ref[6:7]
        in_bias, back_bias = vec_ref[7:8], vec_ref[8:9]
        x = tok_ref[:size].astype(f32)
        dy = cot_ref[:size].astype(f32)
        ctx_t = ctx_s[:, :size].astype(bf16)
        attn = dot(ctx_t.T, wout_ref[...], 1, 0) + out_bias
        mixed = x + live * attn
        unit, factor = normalize(mixed)
        normed = (unit * gain + shift).astype(bf16)
        pre = dot(normed, win_ref[...], 1, 0) + in_bias
        cdf = 0.5 * (1.0 + lax.erf(pre * 0.7071067811865476))
        act = (pre * cdf).astype(bf16)
        slope = cdf + pre * jnp.exp(-0.5 * pre * pre) * 0.3989422804014327
        branch = dot(act, wback_ref[...], 1, 0) + back_bias
        mixed_ref[:size] = (mixed + live * branch).astype(bf16)
        d_ffn = live * dy
        gvec_ref[4] += fold_rows(d_ffn)
        d_ffn = d_ffn.astype(bf16)
        gback_ref[...] += dot(act.T, d_ffn, 1, 0)
        d_act = dot(d_ffn, wback_ref[...], 1, 1)
        d_pre = (d_act * slope).astype(bf16)
        gvec_ref[3] += fold_rows(d_pre.astype(f32))
        gin_ref[...] += dot(normed.T, d_pre, 1, 0)
        d_normed = dot(d_pre, win_ref[...], 1, 1)
        gvec_ref[1] += fold_rows(d_normed * unit)
        gvec_ref[2] += fold_rows(d_normed)
        d_mixed = dy + norm_backward(d_normed, gain, unit, factor)
        dmix_ref[:size] = d_mixed
        d_attn = (live * d_mixed).astype(bf16)
        gvec_ref[0] += fold_rows(d_attn.astype(f32))
        gout_ref[...] += dot(ctx_t, d_attn, 1, 0)
        dctx_s[:, :size] = dot(wout_ref[...], d_attn, 1, 1).astype(bf16)

        def backward(g):
            q = padded(load(0, g), one_row)
            k = padded(load(width, g), one_row)
            v = jnp.concatenate(padded(load(2 * width, g), two_rows), axis=0).T
            d_out = pieces(dctx_s[group_rows(0, g), :size].astype(f32))
            out = pieces(ctx_s[group_rows(0, g), :size])
            ds = []
            for j in range(group):
                d = d_out[j] * linv_s[g * group + j, :1, :size]
                inner = -jnp.sum(d * out[j], axis=0, keepdims=True)
                high = inner.astype(bf16).astype(f32)
                rest_rows = jnp.zeros((slot - head_dim - 2, size), f32)
                tail = jnp.concatenate([high, inner - high, rest_rows], axis=0)
                ds.append(jnp.concatenate([d, tail], axis=0).astype(bf16))
            d_probs = [dot(v, place(j, ds[j]), 1, 0) for j in range(group)]
            ps = [probs[g * group + j, :size, :size] for j in range(group)]
            d_scores = [(ps[j].astype(f32) * d_probs[j]).astype(bf16) for j in range(group)]
            d_v = [dot(ds[j], ps[j], 1, 1)[:head_dim] for j in range(group)]
            d_q = [dot(k[j], d_scores[j], 1, 0)[:head_dim] * scale for j in range(group)]
            d_k = [dot(q[j], d_scores[j], 1, 1)[:head_dim] * scale for j in range(group)]
            for base, parts in ((0, d_q), (width, d_k), (2 * width, d_v)):
                rows = group_rows(base, g)
                dqkv_ref[rows, :size] = jnp.concatenate(parts, axis=0).astype(bf16)

        def backward_step(i, carry):
            backward(2 * i)
            backward(2 * i + 1)
            return carry

        lax.fori_loop(0, heads // group // 2, backward_step, 0)

        if size < block:
            mixed_ref[size:] = tok_ref[size:]
            dmix_ref[size:] = cot_ref[size:].astype(f32)
            dqkv_ref[:, size:] = jnp.zeros((3 * width, block - size), bf16)

    half = block // 2

    @pl.when(length == 0)
    def _():
        mixed_ref[...] = tok_ref[...]
        dmix_ref[...] = cot_ref[...].astype(f32)
        dqkv_ref[...] = jnp.zeros_like(dqkv_ref)

    @pl.when((length > 0) & (length <= half))
    def _():
        run(half)

    @pl.when(length > half)
    def _():
        run(block)

    if packed:

        @pl.when(step == pl.num_programs(0) - 1)
        def _():
            columns = width // 2
            for i in range(DEVICES):
                p = (i % 2) * CHIPS + i // 2
                rows = slice(SHARD * i, SHARD * (i + 1))
                soi_ref[p] = jnp.concatenate([gout_ref[rows], gin_ref[rows]], axis=0).astype(bf16)
                sb_ref[p] = jnp.concatenate(
                    [gback_ref[rows, :columns], gback_ref[rows, columns:]], axis=0
                ).astype(bf16)


def middle(mol_len, qkv, tokens, cotangent, w_out, w_in, w_back, vectors, packed):
    slots = mol_len.shape[0]
    rows, width = tokens.shape
    block = rows // slots
    square = (width, width)

    def whole(shape):
        return pl.BlockSpec(shape, lambda m, lengths: (0,) * len(shape))

    by_rows = pl.BlockSpec((block, width), lambda m, lengths: (m, 0))
    out_specs = [
        by_rows,
        by_rows,
        pl.BlockSpec((3 * width, block), lambda m, lengths: (0, m)),
        whole((5, 8, width)),
    ]
    out_shape = [
        jax.ShapeDtypeStruct((rows, width), bf16),
        jax.ShapeDtypeStruct((rows, width), f32),
        jax.ShapeDtypeStruct((3 * width, rows), bf16),
        jax.ShapeDtypeStruct((5, 8, width), f32),
    ]
    scratch = [
        pltpu.VMEM((HEADS, block, block), bf16),
        pltpu.VMEM((width, block), f32),
        pltpu.VMEM((HEADS, 8, block), f32),
        pltpu.VMEM((width, block), bf16),
    ]
    if packed:
        shapes = [(DEVICES, 2 * SHARD, width), (DEVICES, 2 * SHARD, width // 2)]
        out_specs += [whole(s) for s in shapes]
        out_shape += [jax.ShapeDtypeStruct(s, bf16) for s in shapes]
        scratch = [pltpu.VMEM(square, f32)] * 3 + scratch
    else:
        out_specs += [whole(square)] * 3
        out_shape += [jax.ShapeDtypeStruct(square, f32)] * 3
    return pl.pallas_call(
        functools.partial(middle_kernel, packed, width // HEADS),
        grid_spec=pltpu.PrefetchScalarGridSpec(
            num_scalar_prefetch=1,
            grid=(slots,),
            in_specs=[
                pl.BlockSpec((None, 3 * width, block), lambda m, lengths: (m, 0, 0)),
                by_rows,
                by_rows,
                whole(square),
                whole(square),
                whole(square),
                whole((16, width)),
            ],
            out_specs=out_specs,
            scratch_shapes=scratch,
        ),
        out_shape=out_shape,
        compiler_params=pltpu.CompilerParams(vmem_limit_bytes=58 * MIB),
    )(mol_len, qkv, tokens, cotangent, w_out, w_in, w_back, vectors)


def scatter_kernel(
    soi_hbm,
    sb_hbm,
    dqkv_hbm,
    unit_hbm,
    fq_hbm,
    tok_hbm,
    dmix_hbm,
    vec_ref,
    gvec_ref,
    grad_hbm,
    gq_ref,
    go_ref,
    gi_ref,
    gb_ref,
    gs_ref,
    sq,
    soi,
    sb,
    rq_sib,
    roi_sib,
    rb_sib,
    rq,
    roi,
    rb_flat,
    rb_up,
    rb_down,
    dqkv,
    unit_t,
    fq,
    tok,
    dmix,
    grad,
    gain_wide,
    shift_wide,
    small_wide,
    sums,
    send_sem,
    recv_sem,
    copy_sem,
):
    at = Place()
    rows, width = tok.shape
    wide = 3 * width
    half_q = wide // 2
    half = width // 2
    slots = 8
    block = rows // slots
    mine = at.c * CHIPS
    own = at.block(at.c, at.z, at.y, at.x)
    level_rows = 8 * SHARD

    def local(src, dst, i):
        copy = pltpu.make_async_copy(src, dst, copy_sem.at[i])
        copy.start()
        return copy

    oi_in = local(soi_hbm, soi, 0)
    b_in = local(sb_hbm, sb, 1)
    unit_in = local(unit_hbm, unit_t, 2)
    dqkv_in = local(dqkv_hbm, dqkv, 3)
    fq_in = local(fq_hbm, fq, 4)
    tok_in = local(tok_hbm, tok, 5)
    dmix_in = local(dmix_hbm, dmix, 6)

    pending = []

    def remote(src, dst, target, k, kind, j):
        return pltpu.make_async_remote_copy(
            src_ref=src,
            dst_ref=dst,
            send_sem=send_sem.at[k, kind, j],
            recv_sem=recv_sem.at[k, kind, j],
            device_id=(target,),
            device_id_type=MESH,
        )

    def send(copy, when=None):
        pending.append((copy, when))
        if when is None:
            copy.start()
        else:
            pl.when(when)(copy.start)

    def add(slab, p, other, q):
        slab[p] = (slab[p].astype(f32) + other[q].astype(f32)).astype(bf16)

    slabs = (sq, soi, sb)
    from_sib = (rq_sib, roi_sib, rb_sib)
    steps = (rq, roi)

    def x_type(z):
        return at.block(at.c, z, at.y, 1 - at.x)

    def y_type(z):
        return at.block(at.c, z, 1 - at.y, at.x)

    def corner_type(z):
        return at.block(at.c, z, 1 - at.y, 1 - at.x)

    def sib_copy(k, j):
        return remote(
            slabs[k].at[pl.ds((1 - at.c) * CHIPS + 4 * j, 4)],
            from_sib[k].at[pl.ds(4 * j, 4)],
            at.sib,
            k,
            0,
            j,
        )

    def sib_send(k, j):
        send(sib_copy(k, j))

    def sib_add(k, j):
        sib_copy(k, j).wait_recv()

        def body(i, carry):
            add(slabs[k], mine + 4 * j + i, from_sib[k], 4 * j + i)
            return carry

        lax.fori_loop(0, 4, body, 0)

    def step_copy(k, kind, j, src, target):
        return remote(
            slabs[k].at[pl.ds(src, 1)], steps[k].at[pl.ds(4 * (kind - 1) + j, 1)], target, k, kind, j
        )

    def corner_send(k, j):
        target = at.yn if j % 2 == 0 else at.xn
        send(step_copy(k, 1, j, corner_type(j), target))
        if j % 2 == 0:
            send(step_copy(k, 3, j, y_type(j), at.yn))
        else:
            send(step_copy(k, 2, j, x_type(j), at.xn))

    def corner_add(k, j):
        step_copy(k, 1, j, corner_type(j), at.yn).wait_recv()
        if j % 2 == 0:
            add(slabs[k], x_type(j), steps[k], j)
            send(step_copy(k, 2, j, x_type(j), at.xn))
        else:
            add(slabs[k], y_type(j), steps[k], j)
            send(step_copy(k, 3, j, y_type(j), at.yn))

    def plane_add(k, j):
        p = at.block(at.c, j, at.y, at.x)
        step_copy(k, 2, j, p, at.xn).wait_recv()
        step_copy(k, 3, j, p, at.yn).wait_recv()
        total = slabs[k][p].astype(f32) + steps[k][4 + j].astype(f32) + steps[k][8 + j].astype(f32)
        slabs[k][p] = total.astype(bf16)

    def climb(k, j, hop):
        p = at.block(at.c, j, at.y, at.x)
        for z, kind, target, further in (
            (j - hop, 4, at.up, j - hop - 1 >= 0),
            (j + hop, 5, at.down, j + hop + 1 <= PLANES - 1),
        ):
            if 0 <= z <= PLANES - 1:
                here = at.z == z
                if further:

                    @pl.when(here)
                    def _():
                        step_copy(k, kind, j, p, target).wait_recv()
                        add(slabs[k], p, steps[k], 4 * (kind - 1) + j)

                send(step_copy(k, kind, j, p, target), here)

    def land(k, j):
        p = at.block(at.c, j, at.y, at.x)
        for kind, target, there in ((4, at.up, j > 0), (5, at.down, j < PLANES - 1)):
            if there:

                @pl.when(at.z == j)
                def _():
                    step_copy(k, kind, j, p, target).wait_recv()
                    add(slabs[k], p, steps[k], 4 * (kind - 1) + j)

    def group_copy(kind, j, target):
        buffer = rb_up if kind == 4 else rb_down
        return remote(
            sb.at[pl.ds(mine + 4 * j, 4)], buffer.at[pl.ds(4 * j, 4)], target, 2, kind, j
        )

    def group_add(buffer, j):
        def body(i, carry):
            add(sb, mine + 4 * j + i, buffer, 4 * j + i)
            return carry

        lax.fori_loop(0, 4, body, 0)

    def group_climb(j, hop):
        for z, kind, target, further, buffer in (
            (j - hop, 4, at.up, j - hop - 1 >= 0, rb_up),
            (j + hop, 5, at.down, j + hop + 1 <= PLANES - 1, rb_down),
        ):
            if 0 <= z <= PLANES - 1:
                here = at.z == z
                if further:

                    @pl.when(here)
                    def _():
                        group_copy(kind, j, target).wait_recv()
                        group_add(buffer, j)

                send(group_copy(kind, j, target), here)

    def group_land(j):
        for kind, target, there, buffer in (
            (4, at.up, j > 0, rb_up),
            (5, at.down, j < PLANES - 1, rb_down),
        ):
            if there:

                @pl.when(at.z == j)
                def _():
                    group_copy(kind, j, target).wait_recv()
                    group_add(buffer, j)

    def flat_copy(kind, src, target):
        return remote(sb.at[pl.ds(src, 1)], rb_flat.at[pl.ds(kind - 1, 1)], target, 2, kind, 0)

    even = lax.rem(at.z, 2) == 0
    odd = jnp.logical_not(even)

    def flat_start():
        z = at.z
        send(flat_copy(1, corner_type(z), at.yn), even)
        send(flat_copy(1, corner_type(z), at.xn), odd)
        send(flat_copy(3, y_type(z), at.yn), even)
        send(flat_copy(2, x_type(z), at.xn), odd)

    def flat_corner():
        z = at.z
        flat_copy(1, own, at.yn).wait_recv()

        @pl.when(even)
        def _():
            add(sb, x_type(z), rb_flat, 0)

        @pl.when(odd)
        def _():
            add(sb, y_type(z), rb_flat, 0)

        send(flat_copy(2, x_type(z), at.xn), even)
        send(flat_copy(3, y_type(z), at.yn), odd)

    def flat_end():
        flat_copy(2, own, at.xn).wait_recv()
        flat_copy(3, own, at.yn).wait_recv()
        total = sb[own].astype(f32) + rb_flat[1].astype(f32) + rb_flat[2].astype(f32)
        gb_ref[:, :half] = total[:SHARD]
        gb_ref[:, half:] = total[SHARD:]

    def prepare():
        gain_wide[...] = jnp.broadcast_to(vec_ref[0:1], (128, width)).T
        shift_wide[...] = jnp.broadcast_to(vec_ref[1:2], (128, width)).T
        ones = jnp.ones((16, rows), bf16)
        for part in range(3):
            columns = slice(part * width, (part + 1) * width)
            sums[:, columns] = dot(ones, dqkv[columns], 1, 1)[:8]
        lines = [jnp.zeros((2, width), f32), sums[0:1, :width], sums[0:1, 2 * width :]]
        lines += [jnp.sum(gvec_ref[i], axis=0, keepdims=True) for i in range(5)]
        lines.append(jnp.zeros((128 - 9, width), f32))
        small_wide[...] = jnp.concatenate(lines, axis=0).T

    def weight_grad(j):
        lines = pl.ds(j * level_rows, level_rows)
        left = unit_t[lines]
        lane = lax.broadcasted_iota(jnp.int32, (level_rows, 128), 1)
        gain_sum = jnp.zeros((level_rows, 1), f32)
        shift_sum = jnp.zeros((level_rows, 1), f32)
        pieces = []
        for part in range(3):
            columns = slice(part * width, (part + 1) * width)
            product = dot(left, dqkv[columns], 1, 1)
            weight = fq[lines, columns].astype(f32)
            line = sums[0:1, columns]
            gain_sum += jnp.sum(weight * product, axis=1, keepdims=True)
            shift_sum += jnp.sum(weight * line, axis=1, keepdims=True)
            gain = jnp.concatenate([gain_wide[lines]] * (width // 128), axis=1)
            shift = jnp.concatenate([shift_wide[lines]] * (width // 128), axis=1)
            pieces.append(gain * product + shift * line)
        result = jnp.concatenate(pieces, axis=1)
        small = small_wide[lines]
        small = jnp.where(lane == 0, gain_sum, jnp.where(lane == 1, shift_sum, small))
        blank = jnp.zeros((SHARD, 128), f32)
        for i in range(8):
            p = (i % 2) * CHIPS + 4 * j + i // 2
            some = slice(SHARD * i, SHARD * (i + 1))
            top = jnp.concatenate([result[some, :half_q], small[some]], axis=1)
            bottom = jnp.concatenate([result[some, half_q:], blank], axis=1)
            sq[p] = jnp.concatenate([top, bottom], axis=0).astype(bf16)

    grads = []

    def input_grad(m):
        some = slice(m * block, (m + 1) * block)
        d_normed = dot(fq[...], dqkv[:, some], 1, 0).T
        unit, factor = normalize(tok[some].astype(f32))
        share = norm_backward(d_normed, vec_ref[0:1], unit, factor)
        grad[some] = (dmix[some] + share).astype(bf16)
        grads.append(local(grad.at[pl.ds(m * block, block)], grad_hbm.at[pl.ds(m * block, block)], 7 + m))

    at.barrier()
    oi_in.wait()
    for j in range(PLANES):
        sib_send(1, j)
    b_in.wait()
    for j in range(PLANES):
        sib_send(2, j)
    unit_in.wait()
    dqkv_in.wait()
    fq_in.wait()
    for j in range(PLANES):
        sib_add(1, j)
        corner_send(1, j)
    for j in range(PLANES):
        sib_add(2, j)
    for j in range(PLANES):
        group_climb(j, 3)
    prepare()
    for j in range(PLANES):
        corner_add(1, j)
    for j in range(PLANES):
        group_climb(j, 2)
    weight_grad(0)
    sib_send(0, 0)
    for j in range(PLANES):
        plane_add(1, j)
        climb(1, j, 3)
    for j in range(PLANES):
        group_climb(j, 1)
    weight_grad(3)
    sib_send(0, 3)
    sib_add(0, 0)
    corner_send(0, 0)
    for j in range(PLANES):
        climb(1, j, 2)
    for j in range(PLANES):
        group_land(j)
    flat_start()
    weight_grad(1)
    sib_send(0, 1)
    sib_add(0, 3)
    corner_send(0, 3)
    corner_add(0, 0)
    for j in range(PLANES):
        climb(1, j, 1)
    flat_corner()
    weight_grad(2)
    sib_send(0, 2)
    sib_add(0, 1)
    corner_send(0, 1)
    corner_add(0, 3)
    plane_add(0, 0)
    climb(0, 0, 3)
    tok_in.wait()
    dmix_in.wait()
    input_grad(0)
    sib_add(0, 2)
    corner_send(0, 2)
    corner_add(0, 1)
    plane_add(0, 3)
    climb(0, 3, 3)
    climb(0, 0, 2)
    input_grad(1)
    corner_add(0, 2)
    plane_add(0, 1)
    climb(0, 1, 2)
    climb(0, 3, 2)
    climb(0, 0, 1)
    input_grad(2)
    plane_add(0, 2)
    climb(0, 2, 2)
    climb(0, 1, 1)
    climb(0, 3, 1)
    input_grad(3)
    climb(0, 2, 1)
    for j in range(PLANES):
        land(1, j)
    input_grad(4)
    flat_end()
    input_grad(5)
    input_grad(6)
    input_grad(7)
    for j in range(PLANES):
        land(0, j)
    last = sq[own].astype(f32)
    gq_ref[:, :half_q] = last[:SHARD, :half_q]
    gq_ref[:, half_q:] = last[SHARD:, :half_q]
    gs_ref[...] = last[:SHARD, half_q:]
    last = soi[own].astype(f32)
    go_ref[...] = last[:SHARD]
    gi_ref[...] = last[SHARD:]
    for copy, when in pending:
        if when is None:
            copy.wait_send()
        else:
            pl.when(when)(copy.wait_send)
    for copy in grads:
        copy.wait()


def scatter(soi, sb, dqkv, unit_t, full_qkv, tokens, d_mixed, vectors, sums):
    rows, width = tokens.shape
    wide = 3 * width
    vmem = pl.BlockSpec(memory_space=pltpu.VMEM)
    anywhere = pl.BlockSpec(memory_space=pl.ANY)
    tall = 2 * SHARD
    widths = (wide // 2 + 128, width, width // 2)
    return pl.pallas_call(
        scatter_kernel,
        out_shape=[
            jax.ShapeDtypeStruct((rows, width), bf16),
            jax.ShapeDtypeStruct((SHARD, wide), f32),
            jax.ShapeDtypeStruct((SHARD, width), f32),
            jax.ShapeDtypeStruct((SHARD, width), f32),
            jax.ShapeDtypeStruct((SHARD, width), f32),
            jax.ShapeDtypeStruct((SHARD, 128), f32),
        ],
        in_specs=[anywhere] * 7 + [vmem] * 2,
        out_specs=[anywhere] + [vmem] * 5,
        scratch_shapes=[pltpu.VMEM((DEVICES, tall, w), bf16) for w in widths]
        + [pltpu.VMEM((CHIPS, tall, w), bf16) for w in widths]
        + [pltpu.VMEM((5 * PLANES, tall, w), bf16) for w in widths[:2]]
        + [
            pltpu.VMEM((3, tall, width // 2), bf16),
            pltpu.VMEM((CHIPS, tall, width // 2), bf16),
            pltpu.VMEM((CHIPS, tall, width // 2), bf16),
            pltpu.VMEM((wide, rows), bf16),
            pltpu.VMEM((width, rows), bf16),
            pltpu.VMEM((width, wide), bf16),
            pltpu.VMEM((rows, width), bf16),
            pltpu.VMEM((rows, width), f32),
            pltpu.VMEM((rows, width), bf16),
            pltpu.VMEM((width, 128), f32),
            pltpu.VMEM((width, 128), f32),
            pltpu.VMEM((width, 128), f32),
            pltpu.VMEM((8, wide), f32),
            pltpu.SemaphoreType.DMA((3, 6, PLANES)),
            pltpu.SemaphoreType.DMA((3, 6, PLANES)),
            pltpu.SemaphoreType.DMA((15,)),
        ],
        compiler_params=pltpu.CompilerParams(
            collective_id=1, has_side_effects=True, vmem_limit_bytes=60 * MIB
        ),
    )(soi, sb, dqkv, unit_t, full_qkv, tokens, d_mixed, vectors, sums)


def on_one_plan(tokens, mol_len, cotangent, vectors, w_qkv, w_out, w_in, w_back):
    slots = mol_len.shape[0]
    small = jnp.pad(jnp.stack(vectors), ((0, 16 - len(vectors)), (0, 128 - SHARD)))
    qkv, unit_t, full_qkv, full_out, full_in, full_back, lines = gather_and_project(
        small, w_qkv, w_out, w_in, w_back, tokens, slots
    )
    mixed_out, d_mixed, dqkv, sums, soi, sb = middle(
        mol_len, qkv, tokens, cotangent, full_out, full_in, full_back, lines, True
    )
    token_grad, g_qkv, g_out, g_in, g_back, g_small = scatter(
        soi, sb, dqkv, unit_t, full_qkv, tokens, d_mixed, lines, sums
    )
    g_small = g_small.T
    return mixed_out, token_grad, [g_small[i] for i in range(9)], g_qkv, g_out, g_in, g_back


def on_any_plan(tokens, mol_len, cotangent, vectors, w_qkv, w_out, w_in, w_back):
    slots = mol_len.shape[0]
    rows, width = tokens.shape

    def gather(array, axis):
        return lax.all_gather(array, "fsdp", axis=axis, tiled=True)

    lines = gather(jnp.stack(vectors), 1).astype(f32)
    lines = jnp.pad(lines, ((0, 16 - len(vectors)), (0, 0)))
    full_qkv, full_out, full_in, full_back = (
        gather(w, 0) for w in (w_qkv, w_out, w_in, w_back)
    )
    unit, factor = normalize(tokens.astype(f32))
    normed = (unit * lines[0] + lines[1]).astype(bf16)
    qkv = jnp.dot(normed, full_qkv, preferred_element_type=f32)
    qkv = (qkv + jnp.concatenate([lines[2], jnp.zeros_like(lines[2]), lines[3]])).astype(bf16)
    qkv = qkv.reshape(slots, rows // slots, 3 * width).transpose(0, 2, 1)
    mixed_out, d_mixed, dqkv, sums, g_out, g_in, g_back = middle(
        mol_len, qkv, tokens, cotangent, full_out, full_in, full_back, lines, False
    )
    g_qkv = jnp.einsum("rf,dr->fd", normed, dqkv, preferred_element_type=f32)
    d_normed = jnp.einsum("dr,fd->rf", dqkv, full_qkv, preferred_element_type=f32)
    totals = jnp.sum(dqkv.astype(f32), axis=1)
    small = [jnp.sum(d_normed * unit, axis=0), jnp.sum(d_normed, axis=0)]
    small += [totals[:width], totals[2 * width :]]
    small += [jnp.sum(sums[i], axis=0) for i in range(5)]
    share = norm_backward(d_normed, lines[0], unit, factor)
    token_grad = (d_mixed + share).astype(bf16)

    def scatter_sum(array, axis):
        return lax.psum_scatter(array, "fsdp", scatter_dimension=axis, tiled=True)

    small = scatter_sum(jnp.stack(small), 1)
    return (
        mixed_out,
        token_grad,
        [small[i] for i in range(9)],
        *(scatter_sum(g, 0) for g in (g_qkv, g_out, g_in, g_back)),
    )


def per_device(
    devices,
    tokens,
    mol_len,
    cotangent,
    ln1_gain,
    ln1_bias,
    w_qkv,
    q_bias,
    v_bias,
    w_out,
    out_bias,
    ln2_gain,
    ln2_bias,
    w_in,
    in_bias,
    w_back,
    back_bias,
):
    vectors = [
        ln1_gain,
        ln1_bias,
        q_bias,
        v_bias,
        out_bias,
        ln2_gain,
        ln2_bias,
        in_bias,
        back_bias,
    ]
    known = devices == DEVICES and w_qkv.shape[0] == SHARD
    plan = on_one_plan if known else on_any_plan
    mixed_out, token_grad, small, g_qkv, g_out, g_in, g_back = plan(
        tokens, mol_len, cotangent, vectors, w_qkv, w_out, w_in, w_back
    )
    return (
        mixed_out,
        token_grad,
        small[0],
        small[1],
        g_qkv,
        small[2],
        small[3],
        g_out,
        small[4],
        small[5],
        small[6],
        g_in,
        small[7],
        g_back,
        small[8],
    )


def solution(mesh):
    line, matrix = P("fsdp"), P("fsdp", None)
    return jax.shard_map(
        functools.partial(per_device, mesh.shape["fsdp"]),
        mesh=mesh,
        in_specs=(
            matrix,
            line,
            matrix,
            line,
            line,
            matrix,
            line,
            line,
            matrix,
            line,
            line,
            line,
            matrix,
            line,
            matrix,
            line,
        ),
        out_specs=(
            matrix,
            matrix,
            line,
            line,
            matrix,
            line,
            line,
            matrix,
            line,
            line,
            line,
            matrix,
            line,
            matrix,
            line,
        ),
        check_vma=False,
    )
```

```python
import functools

import jax
import jax.numpy as jnp
from jax import lax
from jax.experimental import pallas as pl
from jax.experimental.pallas import tpu as pltpu
from jax.sharding import PartitionSpec as P

HEADS = 32

bf16 = jnp.bfloat16
f32 = jnp.float32
eps = 1e-05
masked_score = -1e30
log2_e = 1.4426950408889634
MESH = pl.DeviceIdType.MESH
MIB = 1 << 20

PLANES = 4
CHIPS = 4 * PLANES
DEVICES = 2 * CHIPS
SHARD = 24


def dot(left, right, left_dim, right_dim):
    return lax.dot_general(
        left, right, (((left_dim,), (right_dim,)), ((), ())), preferred_element_type=f32
    )


def normalize(values):
    centred = values - jnp.mean(values, axis=-1, keepdims=True)
    factor = lax.rsqrt(jnp.mean(centred * centred, axis=-1, keepdims=True) + eps)
    return centred * factor, factor


def norm_backward(d_normed, gain, unit, factor):
    e = d_normed * gain
    inner = jnp.mean(e * unit, axis=-1, keepdims=True)
    return factor * (e - jnp.mean(e, axis=-1, keepdims=True) - unit * inner)


def fold_rows(values):
    rows, columns = values.shape
    return jnp.sum(values.reshape(rows // 8, 8, columns), axis=0)


class Place:
    def __init__(self):
        me = lax.axis_index("fsdp")
        self.me = me
        self.c = lax.rem(me, 2)
        self.x = lax.rem(me // 2, 2)
        self.y = lax.rem(me // 4, 2)
        self.z = me // 8
        self.sib = me + 1 - 2 * self.c
        self.xn = me + 2 - 4 * self.x
        self.yn = me + 4 - 8 * self.y

    def block(self, c, z, y, x):
        return ((c * PLANES + z) * 2 + y) * 2 + x

    def greet(self):
        sem = pltpu.get_barrier_semaphore()

        def signal(device):
            pl.semaphore_signal(sem, inc=1, device_id=(device,), device_id_type=MESH)

        for device in (self.sib, self.xn, self.yn):
            signal(device)
        for distance in range(1, PLANES):
            signal(lax.rem(self.me + 8 * distance, DEVICES))

    def await_all(self):
        pl.semaphore_wait(pltpu.get_barrier_semaphore(), 2 + PLANES)


def gather_kernel(
    small_ref,
    wq_ref,
    wo_ref,
    wi_ref,
    wb_ref,
    tok_ref,
    qkv_hbm,
    unit_hbm,
    fq_hbm,
    fo_hbm,
    fi_hbm,
    fb_hbm,
    vec_ref,
    gq,
    gr,
    fq,
    fo,
    fi,
    fb,
    fq_t,
    unit,
    unit_t,
    qkv,
    bias,
    send_sem,
    recv_sem,
    copy_sem,
):
    at = Place()
    at.greet()
    width = tok_ref.shape[1]
    slots, _, block = qkv.shape
    half_q = 3 * width // 2
    half = width // 2
    own = at.block(at.c, at.z, at.y, at.x)
    mine, theirs = at.c * CHIPS, (1 - at.c) * CHIPS
    slabs = ((gq, 0, 384), (gq, 384, 384), (gq, 768, 512), (gr, 0, 640), (gr, 640, 512))

    gq[own] = jnp.concatenate(
        [
            jnp.concatenate([wq_ref[:, :half_q], wq_ref[:, half_q:]], axis=0),
            jnp.concatenate([small_ref[...], jnp.zeros((2 * SHARD - 16, 128), bf16)], axis=0),
        ],
        axis=1,
    )
    gr[own] = jnp.concatenate(
        [
            jnp.concatenate([wo_ref[...], wi_ref[...]], axis=0),
            jnp.concatenate([wb_ref[:, :half], wb_ref[:, half:]], axis=0),
        ],
        axis=1,
    )

    def view(k, first, count):
        slab, column, columns = slabs[k]
        return slab.at[pl.ds(first, count), :, pl.ds(column, columns)]

    def remote(k, first, target, sem, count=1):
        return pltpu.make_async_remote_copy(
            src_ref=view(k, first, count),
            dst_ref=view(k, first, count),
            send_sem=send_sem.at[k],
            recv_sem=recv_sem.at[k, sem],
            device_id=(target,),
            device_id_type=MESH,
        )

    def send(k, b, target):
        remote(k, b, target, lax.rem(b, CHIPS)).start()

    def to_sib(k, b):
        remote(k, b, at.sib, CHIPS).start()

    def arrived(k, b):
        remote(k, b, at.sib, lax.rem(b, CHIPS)).wait_recv()

    def at_level(shift, body):
        level = at.z + shift
        if shift == 0:
            body(level)
        else:
            pl.when((level >= 0) & (level <= PLANES - 1))(lambda: body(level))

    def both(s):
        return (0,) if s == 0 else (-s, s)

    def own_plane(k):
        send(k, own, at.xn)
        send(k, own, at.yn)

    def own_column(k):
        for s in range(1, PLANES):
            for shift in both(s):
                at_level(shift, lambda level, shift=shift: send(k, own, at.me + 8 * shift))
        to_sib(k, own)

    def column(k, s):
        def body(level):
            b = at.block(at.c, level, at.y, at.x)
            arrived(k, b)
            send(k, b, at.xn)
            send(k, b, at.yn)
            to_sib(k, b)

        for shift in both(s):
            at_level(shift, body)

    def plane(k, s):
        def body(level):
            even = lax.rem(level, 2) == 0
            b = at.block(at.c, level, at.y, 1 - at.x)
            arrived(k, b)
            pl.when(even)(lambda: send(k, b, at.yn))
            to_sib(k, b)
            d = at.block(at.c, level, 1 - at.y, at.x)
            arrived(k, d)
            pl.when(jnp.logical_not(even))(lambda: send(k, d, at.xn))
            to_sib(k, d)

        for shift in both(s):
            at_level(shift, body)

    def corner(k):
        for j in range(PLANES):
            b = at.block(at.c, j, 1 - at.y, 1 - at.x)
            arrived(k, b)
            to_sib(k, b)

    def others(k):
        remote(k, theirs, at.sib, CHIPS, CHIPS).wait_recv()

    def norm_step(m):
        rows = pl.ds(m * block, block)
        values, _ = normalize(tok_ref[rows].astype(f32))
        unit[rows] = values
        unit_t[:, rows] = values.astype(bf16).T

    def strip(i):
        return pl.ds(pl.multiple_of(i * 2 * SHARD, 2 * SHARD), 2 * SHARD)

    def stack(first, second):
        return jnp.concatenate([first, second], axis=0).astype(bf16)

    def build_q():
        def body(i, carry):
            first = gq[i].astype(f32)
            second = gq[CHIPS + i].astype(f32)
            fq[strip(i), :half_q] = stack(first[:SHARD, :half_q], second[:SHARD, :half_q])
            fq[strip(i), half_q:] = stack(first[SHARD:, :half_q], second[SHARD:, :half_q])
            return carry

        lax.fori_loop(0, CHIPS, body, 0)
        out(fq, fq_hbm)

    def build_r():
        def body(i, carry):
            first = gr[i].astype(f32)
            second = gr[CHIPS + i].astype(f32)
            fo[strip(i)] = stack(first[:SHARD, :width], second[:SHARD, :width])
            fi[strip(i)] = stack(first[SHARD:, :width], second[SHARD:, :width])
            fb[strip(i), :half] = stack(first[:SHARD, width:], second[:SHARD, width:])
            fb[strip(i), half:] = stack(first[SHARD:, width:], second[SHARD:, width:])
            return carry

        lax.fori_loop(0, CHIPS, body, 0)
        out(fo, fo_hbm)
        out(fi, fi_hbm)
        out(fb, fb_hbm)

    copies = []

    def out(src, dst):
        copy = pltpu.make_async_copy(src, dst, copy_sem.at[len(copies)])
        copy.start()
        copies.append(copy)

    def turn(part):
        columns = slice(part * width, (part + 1) * width)
        fq_t[columns] = fq[:, columns].T

    def spread_vectors():
        column_at = lax.broadcasted_iota(jnp.int32, (128, width), 1)
        entry = lax.broadcasted_iota(jnp.int32, (128, width), 0)
        spread = jnp.where(lax.rem(column_at, SHARD) == entry, 1.0, 0.0).astype(bf16)
        stacked = jnp.concatenate([gq[p, :16, half_q:] for p in range(DEVICES)], axis=0)
        wide = dot(stacked, spread, 1, 0)
        total = jnp.zeros((16, width), f32)
        column_at = lax.broadcasted_iota(jnp.int32, (16, width), 1)
        for p in range(DEVICES):
            first = SHARD * ((p % CHIPS) * 2 + p // CHIPS)
            here = (column_at >= first) & (column_at < first + SHARD)
            total = total + jnp.where(here, wide[16 * p : 16 * p + 16], 0.0)
        vec_ref[...] = total
        bias[:width] = jnp.broadcast_to(total[2:3], (128, width)).T
        bias[width : 2 * width] = jnp.zeros((width, 128), f32)
        bias[2 * width :] = jnp.broadcast_to(total[3:4], (128, width)).T

    def qkv_part(m, part):
        normed = (unit[m * block : (m + 1) * block] * vec_ref[0:1] + vec_ref[1:2]).astype(bf16)
        lines = slice(part * width, (part + 1) * width)
        result = dot(fq_t[lines], normed, 1, 1)
        added = jnp.concatenate([bias[lines]] * (block // 128), axis=1)
        qkv[m, lines] = (result + added).astype(bf16)
        if part == 2:
            out(qkv.at[m], qkv_hbm.at[m])

    norm_step(0)
    norm_step(1)
    at.await_all()
    own_column(0)
    own_plane(4)
    own_column(1)
    own_plane(2)
    norm_step(2)
    own_plane(3)
    norm_step(3)
    own_plane(1)
    own_column(2)
    own_plane(0)
    own_column(3)
    column(0, 3)
    column(0, 1)
    own_column(4)
    plane(1, 0)
    column(0, 2)
    plane(0, 3)
    column(1, 3)
    plane(0, 1)
    norm_step(4)
    plane(0, 0)
    norm_step(5)
    column(1, 2)
    column(1, 1)
    plane(1, 3)
    plane(0, 2)
    column(2, 3)
    column(2, 1)
    column(2, 2)
    corner(0)
    plane(2, 0)
    plane(2, 3)
    plane(1, 1)
    plane(2, 1)
    plane(1, 2)
    plane(2, 2)
    norm_step(6)
    norm_step(7)
    column(3, 2)
    corner(1)
    plane(4, 0)
    corner(2)
    column(3, 3)
    plane(3, 0)
    others(0)
    others(1)
    column(3, 1)
    others(2)
    column(4, 3)
    build_q()
    column(4, 2)
    turn(0)
    turn(1)
    turn(2)
    spread_vectors()
    column(4, 1)
    qkv_part(0, 0)
    plane(3, 2)
    qkv_part(0, 1)
    qkv_part(0, 2)
    qkv_part(1, 0)
    qkv_part(1, 1)
    qkv_part(1, 2)
    qkv_part(2, 0)
    plane(3, 3)
    plane(4, 2)
    qkv_part(2, 1)
    plane(3, 1)
    plane(4, 3)
    plane(4, 1)
    qkv_part(2, 2)
    qkv_part(3, 0)
    qkv_part(3, 1)
    qkv_part(3, 2)
    qkv_part(4, 0)
    qkv_part(4, 1)
    qkv_part(4, 2)
    qkv_part(5, 0)
    corner(3)
    qkv_part(5, 1)
    qkv_part(5, 2)
    qkv_part(6, 0)
    corner(4)
    qkv_part(6, 1)
    qkv_part(6, 2)
    qkv_part(7, 0)
    others(3)
    qkv_part(7, 1)
    others(4)
    qkv_part(7, 2)
    build_r()
    out(unit_t, unit_hbm)
    for k in range(len(slabs)):
        remote(k, 0, at.sib, 0, DEVICES - 1).wait_send()
    for copy in copies:
        copy.wait()


def gather_and_project(small, w_qkv, w_out, w_in, w_back, tokens, slots):
    rows, width = tokens.shape
    block = rows // slots
    wide = 3 * width
    vmem = pl.BlockSpec(memory_space=pltpu.VMEM)
    anywhere = pl.BlockSpec(memory_space=pl.ANY)
    square = (width, width)
    return pl.pallas_call(
        gather_kernel,
        out_shape=[
            jax.ShapeDtypeStruct((slots, wide, block), bf16),
            jax.ShapeDtypeStruct((width, rows), bf16),
            jax.ShapeDtypeStruct((width, wide), bf16),
            jax.ShapeDtypeStruct(square, bf16),
            jax.ShapeDtypeStruct(square, bf16),
            jax.ShapeDtypeStruct(square, bf16),
            jax.ShapeDtypeStruct((16, width), f32),
        ],
        in_specs=[vmem] * 6,
        out_specs=[anywhere] * 6 + [vmem],
        scratch_shapes=[
            pltpu.VMEM((DEVICES, 2 * SHARD, wide // 2 + 128), bf16),
            pltpu.VMEM((DEVICES, 2 * SHARD, wide // 2), bf16),
            pltpu.VMEM((width, wide), bf16),
            pltpu.VMEM(square, bf16),
            pltpu.VMEM(square, bf16),
            pltpu.VMEM(square, bf16),
            pltpu.VMEM((wide, width), bf16),
            pltpu.VMEM((rows, width), f32),
            pltpu.VMEM((width, rows), bf16),
            pltpu.VMEM((slots, wide, block), bf16),
            pltpu.VMEM((wide, 128), f32),
            pltpu.SemaphoreType.DMA((5,)),
            pltpu.SemaphoreType.DMA((5, CHIPS + 1)),
            pltpu.SemaphoreType.DMA((slots + 5,)),
        ],
        compiler_params=pltpu.CompilerParams(
            collective_id=0, has_side_effects=True, vmem_limit_bytes=58 * MIB
        ),
    )(small, w_qkv, w_out, w_in, w_back, tokens)


def middle_kernel(
    packed,
    head_dim,
    len_ref,
    qkv_ref,
    tok_ref,
    cot_ref,
    wout_ref,
    win_ref,
    wback_ref,
    vec_ref,
    mixed_ref,
    dmix_ref,
    dqkv_ref,
    gvec_ref,
    *rest,
):
    if packed:
        packed_ref, gout_ref, gin_ref, gback_ref, probs, ctx_s, linv_s, dctx_s = rest
    else:
        gout_ref, gin_ref, gback_ref, probs, ctx_s, linv_s, dctx_s = rest
    step = pl.program_id(0)
    block, width = tok_ref.shape
    slot = 32
    group = 4
    heads = width // head_dim
    span = group * head_dim
    scale = head_dim ** (-0.5)
    length = len_ref[step]

    @pl.when(step == 0)
    def _():
        gout_ref[...] = jnp.zeros_like(gout_ref)
        gin_ref[...] = jnp.zeros_like(gin_ref)
        gback_ref[...] = jnp.zeros_like(gback_ref)
        gvec_ref[...] = jnp.zeros_like(gvec_ref)

    def run(size):
        extra = (slot - head_dim, size)
        sub = lax.broadcasted_iota(jnp.int32, extra, 0)
        lane = lax.broadcasted_iota(jnp.int32, extra, 1)
        one_row = jnp.where(sub == 0, 1.0, 0.0).astype(f32)
        two_rows = jnp.where(sub <= 1, 1.0, 0.0).astype(f32)
        mask_row = jnp.where((sub == 0) & (lane >= length), masked_score, 0.0).astype(f32)

        def group_rows(base, g):
            return slice(base + g * span, base + (g + 1) * span)

        def load(base, g):
            return qkv_ref[group_rows(base, g), :size].astype(f32)

        def place(j, rows):
            parts = []
            if j > 0:
                parts.append(jnp.zeros((slot * j, size), bf16))
            parts.append(rows)
            if j < group - 1:
                parts.append(jnp.zeros((slot * (group - 1 - j), size), bf16))
            return jnp.concatenate(parts, axis=0)

        def pieces(values):
            return [values[head_dim * j : head_dim * (j + 1)] for j in range(group)]

        def padded(values, tail):
            return [jnp.concatenate([p, tail], axis=0).astype(bf16) for p in pieces(values)]

        ahead = 3 if size > 128 else 6

        def forward():
            q, k, v, scores, weights, outs = {}, {}, {}, {}, {}, {}
            for t in range(heads + 2 * ahead):
                if t < heads:
                    g, j = divmod(t, group)
                    if j == 0:
                        q[g] = padded(load(0, g), one_row)
                        k[g] = jnp.concatenate(padded(load(width, g), mask_row), axis=0).T
                        v[g] = padded(load(2 * width, g), one_row)
                    scores[t] = dot(k[g], place(j, q[g][j]), 1, 0)
                h = t - ahead
                if 0 <= h < heads:
                    s = scores.pop(h)
                    peak = jnp.max(s, axis=0, keepdims=True)
                    weights[h] = jnp.exp2((s - peak) * (scale * log2_e)).astype(bf16)
                    probs[h, :size, :size] = weights[h]
                h = t - 2 * ahead
                if 0 <= h < heads:
                    g, j = divmod(h, group)
                    o = dot(v[g][j], weights.pop(h), 1, 0)
                    inverse = 1.0 / o[head_dim : head_dim + 1]
                    linv_s[h, :, :size] = jnp.broadcast_to(inverse, (8, size))
                    outs[h] = o[:head_dim] * inverse
                    if j == group - 1:
                        parts = [outs.pop(h - group + 1 + i) for i in range(group)]
                        ctx_s[group_rows(0, g), :size] = jnp.concatenate(parts, axis=0)

        forward()

        live = (lax.broadcasted_iota(jnp.int32, (size, 1), 0) < length).astype(f32)
        out_bias, gain, shift = vec_ref[4:5], vec_ref[5:6], vec_ref[6:7]
        in_bias, back_bias = vec_ref[7:8], vec_ref[8:9]
        x = tok_ref[:size].astype(f32)
        dy = cot_ref[:size].astype(f32)
        ctx_t = ctx_s[:, :size].astype(bf16)
        attn = dot(ctx_t.T, wout_ref[...], 1, 0) + out_bias
        mixed = x + live * attn
        unit, factor = normalize(mixed)
        normed = (unit * gain + shift).astype(bf16)
        pre = dot(normed, win_ref[...], 1, 0) + in_bias
        cdf = 0.5 * (1.0 + lax.erf(pre * 0.7071067811865476))
        act = (pre * cdf).astype(bf16)
        slope = cdf + pre * jnp.exp(-0.5 * pre * pre) * 0.3989422804014327
        branch = dot(act, wback_ref[...], 1, 0) + back_bias
        mixed_ref[:size] = (mixed + live * branch).astype(bf16)
        d_ffn = live * dy
        gvec_ref[4] += fold_rows(d_ffn)
        d_ffn = d_ffn.astype(bf16)
        gback_ref[...] += dot(act.T, d_ffn, 1, 0)
        d_act = dot(d_ffn, wback_ref[...], 1, 1)
        d_pre = (d_act * slope).astype(bf16)
        gvec_ref[3] += fold_rows(d_pre.astype(f32))
        gin_ref[...] += dot(normed.T, d_pre, 1, 0)
        d_normed = dot(d_pre, win_ref[...], 1, 1)
        gvec_ref[1] += fold_rows(d_normed * unit)
        gvec_ref[2] += fold_rows(d_normed)
        d_mixed = dy + norm_backward(d_normed, gain, unit, factor)
        dmix_ref[:size] = d_mixed
        d_attn = (live * d_mixed).astype(bf16)
        gvec_ref[0] += fold_rows(d_attn.astype(f32))
        gout_ref[...] += dot(ctx_t, d_attn, 1, 0)
        dctx_s[:, :size] = dot(wout_ref[...], d_attn, 1, 1).astype(bf16)

        behind = 3 if size > 128 else 6

        def backward():
            q, k, v, d, d_probs, d_scores = {}, {}, {}, {}, {}, {}
            d_q, d_k, d_v = {}, {}, {}
            for t in range(heads + 2 * behind):
                if t < heads:
                    g, j = divmod(t, group)
                    if j == 0:
                        q[g] = padded(load(0, g), one_row)
                        k[g] = padded(load(width, g), one_row)
                        v[g] = jnp.concatenate(padded(load(2 * width, g), two_rows), axis=0).T
                        d_out = pieces(dctx_s[group_rows(0, g), :size].astype(f32))
                        out = pieces(ctx_s[group_rows(0, g), :size])
                        for i in range(group):
                            here = d_out[i] * linv_s[g * group + i, :1, :size]
                            inner = -jnp.sum(here * out[i], axis=0, keepdims=True)
                            high = inner.astype(bf16).astype(f32)
                            blank = jnp.zeros((slot - head_dim - 2, size), f32)
                            tail = [here, high, inner - high, blank]
                            d[g * group + i] = jnp.concatenate(tail, axis=0).astype(bf16)
                    d_probs[t] = dot(v[g], place(j, d[t]), 1, 0)
                h = t - behind
                if 0 <= h < heads:
                    p = probs[h, :size, :size]
                    d_scores[h] = (p.astype(f32) * d_probs.pop(h)).astype(bf16)
                h = t - 2 * behind
                if 0 <= h < heads:
                    g, j = divmod(h, group)
                    ds = d_scores.pop(h)
                    d_v[h] = dot(d.pop(h), probs[h, :size, :size], 1, 1)[:head_dim]
                    d_q[h] = dot(k[g][j], ds, 1, 0)[:head_dim] * scale
                    d_k[h] = dot(q[g][j], ds, 1, 1)[:head_dim] * scale
                    if j == group - 1:
                        for base, parts in ((0, d_q), (width, d_k), (2 * width, d_v)):
                            some = [parts.pop(h - group + 1 + i) for i in range(group)]
                            dqkv_ref[group_rows(base, g), :size] = jnp.concatenate(
                                some, axis=0
                            ).astype(bf16)

        backward()

        if size < block:
            mixed_ref[size:] = tok_ref[size:]
            dmix_ref[size:] = cot_ref[size:].astype(f32)
            dqkv_ref[:, size:] = jnp.zeros((3 * width, block - size), bf16)

    half = block // 2

    @pl.when(length == 0)
    def _():
        mixed_ref[...] = tok_ref[...]
        dmix_ref[...] = cot_ref[...].astype(f32)
        dqkv_ref[...] = jnp.zeros_like(dqkv_ref)

    @pl.when((length > 0) & (length <= half))
    def _():
        run(half)

    @pl.when(length > half)
    def _():
        run(block)

    if packed:

        @pl.when(step == pl.num_programs(0) - 1)
        def _():
            columns = width // 2
            for i in range(DEVICES):
                p = (i % 2) * CHIPS + i // 2
                rows = slice(SHARD * i, SHARD * (i + 1))
                top = jnp.concatenate([gout_ref[rows], gback_ref[rows, :columns]], axis=1)
                bottom = jnp.concatenate([gin_ref[rows], gback_ref[rows, columns:]], axis=1)
                packed_ref[p] = jnp.concatenate([top, bottom], axis=0).astype(bf16)


def middle(mol_len, qkv, tokens, cotangent, w_out, w_in, w_back, vectors, packed):
    slots = mol_len.shape[0]
    rows, width = tokens.shape
    block = rows // slots
    square = (width, width)

    def whole(shape):
        return pl.BlockSpec(shape, lambda m, lengths: (0,) * len(shape))

    by_rows = pl.BlockSpec((block, width), lambda m, lengths: (m, 0))
    out_specs = [
        by_rows,
        by_rows,
        pl.BlockSpec((3 * width, block), lambda m, lengths: (0, m)),
        whole((5, 8, width)),
    ]
    out_shape = [
        jax.ShapeDtypeStruct((rows, width), bf16),
        jax.ShapeDtypeStruct((rows, width), f32),
        jax.ShapeDtypeStruct((3 * width, rows), bf16),
        jax.ShapeDtypeStruct((5, 8, width), f32),
    ]
    scratch = [
        pltpu.VMEM((HEADS, block, block), bf16),
        pltpu.VMEM((width, block), f32),
        pltpu.VMEM((HEADS, 8, block), f32),
        pltpu.VMEM((width, block), bf16),
    ]
    if packed:
        shape = (DEVICES, 2 * SHARD, width + width // 2)
        out_specs.append(whole(shape))
        out_shape.append(jax.ShapeDtypeStruct(shape, bf16))
        scratch = [pltpu.VMEM(square, f32)] * 3 + scratch
    else:
        out_specs += [whole(square)] * 3
        out_shape += [jax.ShapeDtypeStruct(square, f32)] * 3
    return pl.pallas_call(
        functools.partial(middle_kernel, packed, width // HEADS),
        grid_spec=pltpu.PrefetchScalarGridSpec(
            num_scalar_prefetch=1,
            grid=(slots,),
            in_specs=[
                pl.BlockSpec((None, 3 * width, block), lambda m, lengths: (m, 0, 0)),
                by_rows,
                by_rows,
                whole(square),
                whole(square),
                whole(square),
                whole((16, width)),
            ],
            out_specs=out_specs,
            scratch_shapes=scratch,
        ),
        out_shape=out_shape,
        compiler_params=pltpu.CompilerParams(vmem_limit_bytes=58 * MIB),
    )(mol_len, qkv, tokens, cotangent, w_out, w_in, w_back, vectors)


def scatter_kernel(
    sr_hbm,
    dqkv_hbm,
    unit_hbm,
    fq_hbm,
    tok_hbm,
    dmix_hbm,
    vec_ref,
    gvec_ref,
    grad_hbm,
    gq_ref,
    gr_ref,
    sq,
    sr,
    rq_sib,
    rr_sib,
    rq,
    rr,
    dqkv,
    unit_t,
    fq,
    tok,
    dmix,
    grad,
    gain_wide,
    shift_wide,
    small_wide,
    sums,
    result,
    send_sem,
    recv_sem,
    copy_sem,
):
    at = Place()
    at.greet()
    rows, width = tok.shape
    wide = 3 * width
    half_q = wide // 2
    slots = 8
    block = rows // slots
    mine, theirs = at.c * CHIPS, (1 - at.c) * CHIPS
    own = at.block(at.c, at.z, at.y, at.x)
    level_rows = 8 * SHARD

    def local(src, dst, i):
        copy = pltpu.make_async_copy(src, dst, copy_sem.at[i])
        copy.start()
        return copy

    sr_in = local(sr_hbm, sr, 0)
    unit_in = local(unit_hbm, unit_t, 1)
    dqkv_in = local(dqkv_hbm, dqkv, 2)
    fq_in = local(fq_hbm, fq, 3)
    tok_in = local(tok_hbm, tok, 4)
    dmix_in = local(dmix_hbm, dmix, 5)

    slabs = (
        (sq, rq_sib, rq, 0, 640),
        (sq, rq_sib, rq, 640, 640),
        (sr, rr_sib, rr, 0, 1152),
    )

    def cut(ref, k, first, count):
        return ref.at[pl.ds(first, count), :, pl.ds(slabs[k][3], slabs[k][4])]

    def piece(ref, k, p):
        _, _, _, column, columns = slabs[k]
        return ref[p, :, column : column + columns].astype(f32)

    def put(k, p, value):
        slab, _, _, column, columns = slabs[k]
        slab[p, :, column : column + columns] = value.astype(bf16)

    def remote(k, src, dst, target, sem):
        return pltpu.make_async_remote_copy(
            src_ref=src,
            dst_ref=dst,
            send_sem=send_sem.at[k],
            recv_sem=recv_sem.at[k, sem],
            device_id=(target,),
            device_id_type=MESH,
        )

    def x_type(j):
        return at.block(at.c, j, at.y, 1 - at.x)

    def y_type(j):
        return at.block(at.c, j, 1 - at.y, at.x)

    def corner_type(j):
        return at.block(at.c, j, 1 - at.y, 1 - at.x)

    def column_type(j):
        return at.block(at.c, j, at.y, at.x)

    def sib_copy(k, j):
        src = cut(slabs[k][0], k, theirs + 4 * j, 4)
        return remote(k, src, cut(slabs[k][1], k, 4 * j, 4), at.sib, j)

    def sib_send(k, j):
        sib_copy(k, j).start()

    def step_copy(k, src, slot, target):
        src = cut(slabs[k][0], k, src, 1)
        return remote(k, src, cut(slabs[k][2], k, slot, 1), target, PLANES + slot)

    def x_send(k, j):
        step_copy(k, x_type(j), 4 + j, at.xn).start()

    def y_send(k, j):
        step_copy(k, y_type(j), 8 + j, at.yn).start()

    def sib_add(k, j):
        sib_copy(k, j).wait_recv()

        def body(i, carry):
            p = mine + 4 * j + i
            put(k, p, piece(slabs[k][0], k, p) + piece(slabs[k][1], k, 4 * j + i))
            return carry

        lax.fori_loop(0, 4, body, 0)
        step_copy(k, corner_type(j), j, at.yn if j % 2 == 0 else at.xn).start()
        (y_send if j % 2 == 0 else x_send)(k, j)

    def corner_add(k, j):
        step_copy(k, own, j, at.sib).wait_recv()
        p = x_type(j) if j % 2 == 0 else y_type(j)
        put(k, p, piece(slabs[k][0], k, p) + piece(slabs[k][2], k, j))
        (x_send if j % 2 == 0 else y_send)(k, j)

    def plane_add(k, j):
        p = column_type(j)
        step_copy(k, own, 4 + j, at.sib).wait_recv()
        step_copy(k, own, 8 + j, at.sib).wait_recv()
        received = piece(slabs[k][2], k, 4 + j) + piece(slabs[k][2], k, 8 + j)
        put(k, p, piece(slabs[k][0], k, p) + received)

        @pl.when(at.z != j)
        def _():
            step_copy(k, p, 12 + at.z, at.me + 8 * (j - at.z)).start()

    def land(k):
        total = gq_ref if slabs[k][0] is sq else gr_ref
        columns = slice(slabs[k][3], slabs[k][3] + slabs[k][4])
        total[:, columns] = piece(slabs[k][0], k, own)
        for j in range(PLANES):

            @pl.when(at.z != j)
            def _():
                step_copy(k, own, 12 + j, at.sib).wait_recv()
                total[:, columns] += piece(slabs[k][2], k, 12 + j)

    def prepare():
        gain_wide[...] = jnp.broadcast_to(vec_ref[0:1], (128, width)).T
        shift_wide[...] = jnp.broadcast_to(vec_ref[1:2], (128, width)).T
        ones = jnp.ones((16, rows), bf16)
        for part in range(3):
            columns = slice(part * width, (part + 1) * width)
            sums[:, columns] = dot(ones, dqkv[columns], 1, 1)[:8]
        lines = [jnp.zeros((2, width), f32), sums[0:1, :width], sums[0:1, 2 * width :]]
        lines += [jnp.sum(gvec_ref[i], axis=0, keepdims=True) for i in range(5)]
        lines.append(jnp.zeros((128 - 9, width), f32))
        small_wide[...] = jnp.concatenate(lines, axis=0).T

    def weight_grad(j, part):
        lines = pl.ds(j * level_rows, level_rows)
        columns = slice(part * width, (part + 1) * width)
        product = dot(unit_t[lines], dqkv[columns], 1, 1)
        weight = fq[lines, columns].astype(f32)
        line = sums[0:1, columns]
        gain_sum = jnp.sum(weight * product, axis=1, keepdims=True)
        shift_sum = jnp.sum(weight * line, axis=1, keepdims=True)
        lane = lax.broadcasted_iota(jnp.int32, (level_rows, 128), 1)
        small_wide[lines] += jnp.where(
            lane == 0, gain_sum, jnp.where(lane == 1, shift_sum, 0.0)
        )
        gain = jnp.concatenate([gain_wide[lines]] * (width // 128), axis=1)
        shift = jnp.concatenate([shift_wide[lines]] * (width // 128), axis=1)
        result[:, columns] = gain * product + shift * line
        if part < 2:
            return
        small = small_wide[lines]
        blank = jnp.zeros((SHARD, 128), f32)
        for i in range(8):
            p = (i % 2) * CHIPS + 4 * j + i // 2
            some = slice(SHARD * i, SHARD * (i + 1))
            top = jnp.concatenate([result[some, :half_q], small[some]], axis=1)
            bottom = jnp.concatenate([result[some, half_q:], blank], axis=1)
            sq[p] = jnp.concatenate([top, bottom], axis=0).astype(bf16)

    grads = []

    def input_grad(m):
        some = slice(m * block, (m + 1) * block)
        d_normed = dot(fq[...], dqkv[:, some], 1, 0).T
        unit, factor = normalize(tok[some].astype(f32))
        share = norm_backward(d_normed, vec_ref[0:1], unit, factor)
        grad[some] = (dmix[some] + share).astype(bf16)
        grads.append(local(grad.at[pl.ds(m * block, block)], grad_hbm.at[pl.ds(m * block, block)], 6 + m))

    sr_in.wait()
    at.await_all()
    sib_send(2, 0)
    sib_send(2, 1)
    sib_send(2, 2)
    sib_add(2, 0)
    sib_send(2, 3)
    sib_add(2, 1)
    sib_add(2, 2)
    sib_add(2, 3)
    unit_in.wait()
    dqkv_in.wait()
    fq_in.wait()
    prepare()
    weight_grad(0, 0)
    weight_grad(0, 1)
    weight_grad(0, 2)
    weight_grad(3, 0)
    corner_add(2, 1)
    sib_send(1, 0)
    corner_add(2, 0)
    corner_add(2, 3)
    weight_grad(3, 1)
    sib_send(0, 0)
    corner_add(2, 2)
    weight_grad(3, 2)
    sib_send(1, 3)
    sib_send(0, 3)
    sib_add(0, 0)
    sib_add(1, 0)
    weight_grad(2, 0)
    plane_add(2, 1)
    plane_add(2, 0)
    sib_add(1, 3)
    weight_grad(2, 1)
    sib_add(0, 3)
    plane_add(2, 3)
    weight_grad(2, 2)
    sib_send(1, 2)
    weight_grad(1, 0)
    sib_add(1, 2)
    corner_add(0, 0)
    plane_add(2, 2)
    sib_send(0, 2)
    corner_add(1, 0)
    weight_grad(1, 1)
    corner_add(0, 3)
    weight_grad(1, 2)
    sib_send(1, 1)
    sib_send(0, 1)
    corner_add(1, 2)
    plane_add(0, 0)
    tok_in.wait()
    dmix_in.wait()
    sib_add(0, 2)
    corner_add(1, 3)
    sib_add(1, 1)
    sib_add(0, 1)
    plane_add(0, 3)
    plane_add(1, 0)
    input_grad(0)
    plane_add(1, 2)
    corner_add(0, 2)
    corner_add(1, 1)
    input_grad(1)
    input_grad(2)
    corner_add(0, 1)
    plane_add(1, 3)
    plane_add(1, 1)
    input_grad(3)
    input_grad(4)
    plane_add(0, 2)
    plane_add(0, 1)
    input_grad(5)
    input_grad(6)
    land(1)
    input_grad(7)
    land(2)
    land(0)
    for k in range(len(slabs)):
        every = cut(slabs[k][0], k, 0, DEVICES - 1)
        remote(k, every, every, at.sib, 0).wait_send()
    for copy in grads:
        copy.wait()


def scatter(packed, dqkv, unit_t, full_qkv, tokens, d_mixed, vectors, sums):
    rows, width = tokens.shape
    wide = 3 * width
    vmem = pl.BlockSpec(memory_space=pltpu.VMEM)
    anywhere = pl.BlockSpec(memory_space=pl.ANY)
    tall = 2 * SHARD
    widths = (wide // 2 + 128, wide // 2)
    return pl.pallas_call(
        scatter_kernel,
        out_shape=[jax.ShapeDtypeStruct((rows, width), bf16)]
        + [jax.ShapeDtypeStruct((tall, w), f32) for w in widths],
        in_specs=[anywhere] * 6 + [vmem] * 2,
        out_specs=[anywhere] + [vmem] * 2,
        scratch_shapes=[pltpu.VMEM((DEVICES, tall, w), bf16) for w in widths]
        + [pltpu.VMEM((CHIPS, tall, w), bf16) for w in widths]
        + [pltpu.VMEM((4 * PLANES, tall, w), bf16) for w in widths]
        + [
            pltpu.VMEM((wide, rows), bf16),
            pltpu.VMEM((width, rows), bf16),
            pltpu.VMEM((width, wide), bf16),
            pltpu.VMEM((rows, width), bf16),
            pltpu.VMEM((rows, width), f32),
            pltpu.VMEM((rows, width), bf16),
            pltpu.VMEM((width, 128), f32),
            pltpu.VMEM((width, 128), f32),
            pltpu.VMEM((width, 128), f32),
            pltpu.VMEM((8, wide), f32),
            pltpu.VMEM((8 * SHARD, wide), f32),
            pltpu.SemaphoreType.DMA((3,)),
            pltpu.SemaphoreType.DMA((3, 5 * PLANES)),
            pltpu.SemaphoreType.DMA((14,)),
        ],
        compiler_params=pltpu.CompilerParams(
            collective_id=1, has_side_effects=True, vmem_limit_bytes=60 * MIB
        ),
    )(packed, dqkv, unit_t, full_qkv, tokens, d_mixed, vectors, sums)


def finish_kernel(grad_ref, q_ref, r_ref, out_ref, g_qkv, g_out, g_in, g_back, *lines):
    out_ref[...] = grad_ref[...]

    @pl.when(pl.program_id(0) == 0)
    def _():
        width = g_out.shape[1]
        half_q = 3 * width // 2
        half = width // 2
        g_qkv[:, :half_q] = q_ref[:SHARD, :half_q]
        g_qkv[:, half_q:] = q_ref[SHARD:, :half_q]
        g_out[...] = r_ref[:SHARD, :width]
        g_in[...] = r_ref[SHARD:, :width]
        g_back[:, :half] = r_ref[:SHARD, width:]
        g_back[:, half:] = r_ref[SHARD:, width:]
        small = q_ref[:SHARD, half_q:].T
        for i, line in enumerate(lines):
            line[...] = small[i, :SHARD]


def finish(token_grad, q_part, r_part):
    rows, width = token_grad.shape
    pieces = 4
    by_rows = pl.BlockSpec((rows // pieces, width), lambda i: (i, 0))

    def whole(shape):
        return pl.BlockSpec(shape, lambda i: (0,) * len(shape))

    shapes = [(SHARD, 3 * width)] + [(SHARD, width)] * 3 + [(SHARD,)] * 9
    return pl.pallas_call(
        finish_kernel,
        grid=(pieces,),
        out_shape=[jax.ShapeDtypeStruct(token_grad.shape, bf16)]
        + [jax.ShapeDtypeStruct(s, f32) for s in shapes],
        in_specs=[by_rows, whole(q_part.shape), whole(r_part.shape)],
        out_specs=[by_rows] + [whole(s) for s in shapes],
    )(token_grad, q_part, r_part)


def on_one_plan(tokens, mol_len, cotangent, vectors, w_qkv, w_out, w_in, w_back):
    slots = mol_len.shape[0]
    small = jnp.pad(jnp.stack(vectors), ((0, 16 - len(vectors)), (0, 128 - SHARD)))
    qkv, unit_t, full_qkv, full_out, full_in, full_back, lines = gather_and_project(
        small, w_qkv, w_out, w_in, w_back, tokens, slots
    )
    mixed_out, d_mixed, dqkv, sums, packed = middle(
        mol_len, qkv, tokens, cotangent, full_out, full_in, full_back, lines, True
    )
    token_grad, q_part, r_part = scatter(
        packed, dqkv, unit_t, full_qkv, tokens, d_mixed, lines, sums
    )
    token_grad, g_qkv, g_out, g_in, g_back, *small = finish(token_grad, q_part, r_part)
    return mixed_out, token_grad, small, g_qkv, g_out, g_in, g_back


def on_any_plan(tokens, mol_len, cotangent, vectors, w_qkv, w_out, w_in, w_back):
    slots = mol_len.shape[0]
    rows, width = tokens.shape

    def gather(array, axis):
        return lax.all_gather(array, "fsdp", axis=axis, tiled=True)

    lines = gather(jnp.stack(vectors), 1).astype(f32)
    lines = jnp.pad(lines, ((0, 16 - len(vectors)), (0, 0)))
    full_qkv, full_out, full_in, full_back = (
        gather(w, 0) for w in (w_qkv, w_out, w_in, w_back)
    )
    unit, factor = normalize(tokens.astype(f32))
    normed = (unit * lines[0] + lines[1]).astype(bf16)
    qkv = jnp.dot(normed, full_qkv, preferred_element_type=f32)
    qkv = (qkv + jnp.concatenate([lines[2], jnp.zeros_like(lines[2]), lines[3]])).astype(bf16)
    qkv = qkv.reshape(slots, rows // slots, 3 * width).transpose(0, 2, 1)
    mixed_out, d_mixed, dqkv, sums, g_out, g_in, g_back = middle(
        mol_len, qkv, tokens, cotangent, full_out, full_in, full_back, lines, False
    )
    g_qkv = jnp.einsum("rf,dr->fd", normed, dqkv, preferred_element_type=f32)
    d_normed = jnp.einsum("dr,fd->rf", dqkv, full_qkv, preferred_element_type=f32)
    totals = jnp.sum(dqkv.astype(f32), axis=1)
    small = [jnp.sum(d_normed * unit, axis=0), jnp.sum(d_normed, axis=0)]
    small += [totals[:width], totals[2 * width :]]
    small += [jnp.sum(sums[i], axis=0) for i in range(5)]
    share = norm_backward(d_normed, lines[0], unit, factor)
    token_grad = (d_mixed + share).astype(bf16)

    def scatter_sum(array, axis):
        return lax.psum_scatter(array, "fsdp", scatter_dimension=axis, tiled=True)

    small = scatter_sum(jnp.stack(small), 1)
    return (
        mixed_out,
        token_grad,
        [small[i] for i in range(9)],
        *(scatter_sum(g, 0) for g in (g_qkv, g_out, g_in, g_back)),
    )


def per_device(
    devices,
    tokens,
    mol_len,
    cotangent,
    ln1_gain,
    ln1_bias,
    w_qkv,
    q_bias,
    v_bias,
    w_out,
    out_bias,
    ln2_gain,
    ln2_bias,
    w_in,
    in_bias,
    w_back,
    back_bias,
):
    vectors = [
        ln1_gain,
        ln1_bias,
        q_bias,
        v_bias,
        out_bias,
        ln2_gain,
        ln2_bias,
        in_bias,
        back_bias,
    ]
    known = devices == DEVICES and w_qkv.shape[0] == SHARD
    plan = on_one_plan if known else on_any_plan
    mixed_out, token_grad, small, g_qkv, g_out, g_in, g_back = plan(
        tokens, mol_len, cotangent, vectors, w_qkv, w_out, w_in, w_back
    )
    return (
        mixed_out,
        token_grad,
        small[0],
        small[1],
        g_qkv,
        small[2],
        small[3],
        g_out,
        small[4],
        small[5],
        small[6],
        g_in,
        small[7],
        g_back,
        small[8],
    )


def solution(mesh):
    line, matrix = P("fsdp"), P("fsdp", None)
    return jax.shard_map(
        functools.partial(per_device, mesh.shape["fsdp"]),
        mesh=mesh,
        in_specs=(
            matrix,
            line,
            matrix,
            line,
            line,
            matrix,
            line,
            line,
            matrix,
            line,
            line,
            line,
            matrix,
            line,
            matrix,
            line,
        ),
        out_specs=(
            matrix,
            matrix,
            line,
            line,
            matrix,
            line,
            line,
            matrix,
            line,
            line,
            line,
            matrix,
            line,
            matrix,
            line,
        ),
        check_vma=False,
    )
```

```python
import functools

import jax
import jax.numpy as jnp
from jax import lax
from jax.experimental import pallas as pl
from jax.experimental.pallas import tpu as pltpu
from jax.sharding import PartitionSpec as P

HEADS = 32

bf16 = jnp.bfloat16
f32 = jnp.float32
eps = 1e-05
masked_score = -1e30
log2_e = 1.4426950408889634
MESH = pl.DeviceIdType.MESH
MIB = 1 << 20

PLANES = 4
CHIPS = 4 * PLANES
DEVICES = 2 * CHIPS
SHARD = 24


def dot(left, right, left_dim, right_dim):
    return lax.dot_general(
        left, right, (((left_dim,), (right_dim,)), ((), ())), preferred_element_type=f32
    )


def normalize(values):
    centred = values - jnp.mean(values, axis=-1, keepdims=True)
    factor = lax.rsqrt(jnp.mean(centred * centred, axis=-1, keepdims=True) + eps)
    return centred * factor, factor


def norm_backward(d_normed, gain, unit, factor):
    e = d_normed * gain
    inner = jnp.mean(e * unit, axis=-1, keepdims=True)
    return factor * (e - jnp.mean(e, axis=-1, keepdims=True) - unit * inner)


def fold_rows(values):
    rows, columns = values.shape
    return jnp.sum(values.reshape(rows // 8, 8, columns), axis=0)


class Place:
    def __init__(self):
        me = lax.axis_index("fsdp")
        self.me = me
        self.c = lax.rem(me, 2)
        self.x = lax.rem(me // 2, 2)
        self.y = lax.rem(me // 4, 2)
        self.z = me // 8
        self.sib = me + 1 - 2 * self.c
        self.xn = me + 2 - 4 * self.x
        self.yn = me + 4 - 8 * self.y

    def block(self, c, z, y, x):
        return ((c * PLANES + z) * 2 + y) * 2 + x

    def greet(self):
        sem = pltpu.get_barrier_semaphore()

        def signal(device):
            pl.semaphore_signal(sem, inc=1, device_id=(device,), device_id_type=MESH)

        for device in (self.sib, self.xn, self.yn):
            signal(device)
        for distance in range(1, PLANES):
            signal(lax.rem(self.me + 8 * distance, DEVICES))

    def await_all(self):
        pl.semaphore_wait(pltpu.get_barrier_semaphore(), 2 + PLANES)


def gather_kernel(
    len_ref,
    small_ref,
    wq_ref,
    wo_ref,
    wi_ref,
    wb_ref,
    tok_ref,
    cot_hbm,
    qkv_hbm,
    unit_hbm,
    fq_hbm,
    fo_hbm,
    fi_hbm,
    fb_hbm,
    tok_hbm,
    cot_out,
    vec_ref,
    work_ref,
    gq,
    gr,
    fq,
    fo,
    fi,
    fb,
    fq_t,
    unit,
    unit_t,
    qkv,
    bias,
    tok_odd,
    cot_odd,
    len_send,
    len_recv,
    send_sem,
    recv_sem,
    swap_send,
    swap_recv,
    copy_sem,
):
    at = Place()
    at.greet()
    width = tok_ref.shape[1]
    slots, _, block = qkv.shape
    shared = slots // 2
    half_q = 3 * width // 2
    half = width // 2
    own = at.block(at.c, at.z, at.y, at.x)
    mine, theirs = at.c * CHIPS, (1 - at.c) * CHIPS
    slabs = ((gq, 0, 384), (gq, 384, 384), (gq, 768, 512), (gr, 0, 640), (gr, 640, 512))

    gq[own] = jnp.concatenate(
        [
            jnp.concatenate([wq_ref[:, :half_q], wq_ref[:, half_q:]], axis=0),
            jnp.concatenate([small_ref[...], jnp.zeros((2 * SHARD - 16, 128), bf16)], axis=0),
        ],
        axis=1,
    )
    gr[own] = jnp.concatenate(
        [
            jnp.concatenate([wo_ref[...], wi_ref[...]], axis=0),
            jnp.concatenate([wb_ref[:, :half], wb_ref[:, half:]], axis=0),
        ],
        axis=1,
    )

    def view(k, first, count):
        slab, column, columns = slabs[k]
        return slab.at[pl.ds(first, count), :, pl.ds(column, columns)]

    def remote(k, first, target, sem, count=1):
        return pltpu.make_async_remote_copy(
            src_ref=view(k, first, count),
            dst_ref=view(k, first, count),
            send_sem=send_sem.at[k],
            recv_sem=recv_sem.at[k, sem],
            device_id=(target,),
            device_id_type=MESH,
        )

    def send(k, b, target):
        remote(k, b, target, lax.rem(b, CHIPS)).start()

    def to_sib(k, b):
        remote(k, b, at.sib, CHIPS).start()

    def arrived(k, b):
        remote(k, b, at.sib, lax.rem(b, CHIPS)).wait_recv()

    def at_level(shift, body):
        level = at.z + shift
        if shift == 0:
            body(level)
        else:
            pl.when((level >= 0) & (level <= PLANES - 1))(lambda: body(level))

    def both(s):
        return (0,) if s == 0 else (-s, s)

    def own_plane(k):
        send(k, own, at.xn)
        send(k, own, at.yn)

    def own_column(k):
        for s in range(1, PLANES):
            for shift in both(s):
                at_level(shift, lambda level, shift=shift: send(k, own, at.me + 8 * shift))
        to_sib(k, own)

    def column(k, s):
        def body(level):
            b = at.block(at.c, level, at.y, at.x)
            arrived(k, b)
            send(k, b, at.xn)
            send(k, b, at.yn)
            to_sib(k, b)

        for shift in both(s):
            at_level(shift, body)

    def plane(k, s):
        def body(level):
            even = lax.rem(level, 2) == 0
            b = at.block(at.c, level, at.y, 1 - at.x)
            arrived(k, b)
            pl.when(even)(lambda: send(k, b, at.yn))
            to_sib(k, b)
            d = at.block(at.c, level, 1 - at.y, at.x)
            arrived(k, d)
            pl.when(jnp.logical_not(even))(lambda: send(k, d, at.xn))
            to_sib(k, d)

        for shift in both(s):
            at_level(shift, body)

    def corner(k):
        for j in range(PLANES):
            b = at.block(at.c, j, 1 - at.y, 1 - at.x)
            arrived(k, b)
            to_sib(k, b)

    def others(k):
        remote(k, theirs, at.sib, CHIPS, CHIPS).wait_recv()

    def rows_of(i):
        return pl.ds(i * block, block)

    cot_in = [
        pltpu.make_async_copy(
            cot_hbm.at[rows_of(2 * i + 1)], cot_odd.at[rows_of(i)], swap_recv.at[6 + i]
        )
        for i in range(shared)
    ]

    def swap_copy(src, dst, send, recv):
        return pltpu.make_async_remote_copy(
            src_ref=src,
            dst_ref=dst,
            send_sem=swap_send.at[send],
            recv_sem=swap_recv.at[recv],
            device_id=(at.sib,),
            device_id_type=MESH,
        )

    def tok_copy(i):
        return swap_copy(tok_ref.at[rows_of(2 * i + 1)], tok_odd.at[rows_of(i)], 0, i)

    def swap_start():
        swap_copy(len_send, len_recv, 2, 5).start()
        for i in range(shared):
            tok_copy(i).start()
        for i in range(shared):
            cot_in[i].wait()
            swap_copy(cot_odd.at[rows_of(i)], cot_out.at[rows_of(i)], 1, 4).start()

    def swap_end():
        swap_copy(len_send, len_recv, 2, 5).wait()
        swap_copy(tok_odd, tok_odd, 0, 0).wait_send()
        swap_copy(cot_odd, cot_out, 1, 4).wait()
        place = lax.broadcasted_iota(jnp.int32, (shared, 128), 0)
        own_lengths = jnp.zeros((shared, 128), jnp.int32)
        odd_lengths = jnp.zeros((shared, 128), jnp.int32)
        for i in range(shared):
            own_lengths = jnp.where(place == i, len_send[2 * i : 2 * i + 1], own_lengths)
            odd_lengths = jnp.where(place == i, len_recv[2 * i + 1 : 2 * i + 2], odd_lengths)
        work_ref[:shared] = own_lengths
        work_ref[shared:] = odd_lengths

    for i in range(slots):
        len_send[i : i + 1] = jnp.full((1, 128), len_ref[i], jnp.int32)
    for copy in cot_in:
        copy.start()

    def norm_step(m):
        rows = rows_of(m)
        if m < shared:
            here = tok_ref[rows_of(2 * m)]
        else:
            tok_copy(m - shared).wait_recv()
            here = tok_odd[rows_of(m - shared)]
        values, _ = normalize(here.astype(f32))
        unit[rows] = values
        unit_t[:, rows] = values.astype(bf16).T

    def strip(i):
        return pl.ds(pl.multiple_of(i * 2 * SHARD, 2 * SHARD), 2 * SHARD)

    def stack(first, second):
        return jnp.concatenate([first, second], axis=0).astype(bf16)

    def build_q():
        def body(i, carry):
            first = gq[i].astype(f32)
            second = gq[CHIPS + i].astype(f32)
            fq[strip(i), :half_q] = stack(first[:SHARD, :half_q], second[:SHARD, :half_q])
            fq[strip(i), half_q:] = stack(first[SHARD:, :half_q], second[SHARD:, :half_q])
            return carry

        lax.fori_loop(0, CHIPS, body, 0)
        out(fq, fq_hbm)

    def build_r():
        def body(i, carry):
            first = gr[i].astype(f32)
            second = gr[CHIPS + i].astype(f32)
            fo[strip(i)] = stack(first[:SHARD, :width], second[:SHARD, :width])
            fi[strip(i)] = stack(first[SHARD:, :width], second[SHARD:, :width])
            fb[strip(i), :half] = stack(first[:SHARD, width:], second[:SHARD, width:])
            fb[strip(i), half:] = stack(first[SHARD:, width:], second[SHARD:, width:])
            return carry

        lax.fori_loop(0, CHIPS, body, 0)
        out(fo, fo_hbm)
        out(fi, fi_hbm)
        out(fb, fb_hbm)

    copies = []

    def out(src, dst):
        copy = pltpu.make_async_copy(src, dst, copy_sem.at[len(copies)])
        copy.start()
        copies.append(copy)

    def turn(part):
        columns = slice(part * width, (part + 1) * width)
        fq_t[columns] = fq[:, columns].T

    def spread_vectors():
        column_at = lax.broadcasted_iota(jnp.int32, (128, width), 1)
        entry = lax.broadcasted_iota(jnp.int32, (128, width), 0)
        spread = jnp.where(lax.rem(column_at, SHARD) == entry, 1.0, 0.0).astype(bf16)
        stacked = jnp.concatenate([gq[p, :16, half_q:] for p in range(DEVICES)], axis=0)
        wide = dot(stacked, spread, 1, 0)
        total = jnp.zeros((16, width), f32)
        column_at = lax.broadcasted_iota(jnp.int32, (16, width), 1)
        for p in range(DEVICES):
            first = SHARD * ((p % CHIPS) * 2 + p // CHIPS)
            here = (column_at >= first) & (column_at < first + SHARD)
            total = total + jnp.where(here, wide[16 * p : 16 * p + 16], 0.0)
        vec_ref[...] = total
        bias[:width] = jnp.broadcast_to(total[2:3], (128, width)).T
        bias[width : 2 * width] = jnp.zeros((width, 128), f32)
        bias[2 * width :] = jnp.broadcast_to(total[3:4], (128, width)).T

    def qkv_part(m, part):
        normed = (unit[m * block : (m + 1) * block] * vec_ref[0:1] + vec_ref[1:2]).astype(bf16)
        lines = slice(part * width, (part + 1) * width)
        result = dot(fq_t[lines], normed, 1, 1)
        added = jnp.concatenate([bias[lines]] * (block // 128), axis=1)
        qkv[m, lines] = (result + added).astype(bf16)
        if part == 2:
            out(qkv.at[m], qkv_hbm.at[m])

    norm_step(0)
    norm_step(1)
    at.await_all()
    swap_start()
    own_column(0)
    own_plane(4)
    own_column(1)
    own_plane(2)
    norm_step(2)
    own_plane(3)
    norm_step(3)
    own_plane(1)
    own_column(2)
    own_plane(0)
    own_column(3)
    column(0, 3)
    column(0, 1)
    own_column(4)
    plane(1, 0)
    column(0, 2)
    plane(0, 3)
    column(1, 3)
    plane(0, 1)
    norm_step(4)
    plane(0, 0)
    norm_step(5)
    column(1, 2)
    column(1, 1)
    plane(1, 3)
    plane(0, 2)
    column(2, 3)
    column(2, 1)
    column(2, 2)
    corner(0)
    plane(2, 0)
    plane(2, 3)
    plane(1, 1)
    plane(2, 1)
    plane(1, 2)
    plane(2, 2)
    norm_step(6)
    norm_step(7)
    column(3, 2)
    corner(1)
    plane(4, 0)
    corner(2)
    column(3, 3)
    plane(3, 0)
    others(0)
    others(1)
    column(3, 1)
    others(2)
    column(4, 3)
    build_q()
    column(4, 2)
    turn(0)
    turn(1)
    turn(2)
    spread_vectors()
    column(4, 1)
    qkv_part(0, 0)
    plane(3, 2)
    qkv_part(0, 1)
    qkv_part(0, 2)
    qkv_part(1, 0)
    qkv_part(1, 1)
    qkv_part(1, 2)
    qkv_part(2, 0)
    plane(3, 3)
    plane(4, 2)
    qkv_part(2, 1)
    plane(3, 1)
    plane(4, 3)
    plane(4, 1)
    qkv_part(2, 2)
    qkv_part(3, 0)
    qkv_part(3, 1)
    qkv_part(3, 2)
    qkv_part(4, 0)
    qkv_part(4, 1)
    qkv_part(4, 2)
    qkv_part(5, 0)
    corner(3)
    qkv_part(5, 1)
    qkv_part(5, 2)
    qkv_part(6, 0)
    corner(4)
    qkv_part(6, 1)
    qkv_part(6, 2)
    qkv_part(7, 0)
    others(3)
    qkv_part(7, 1)
    others(4)
    qkv_part(7, 2)
    build_r()
    out(unit_t, unit_hbm)
    out(tok_odd, tok_hbm)
    swap_end()
    for k in range(len(slabs)):
        remote(k, 0, at.sib, 0, DEVICES - 1).wait_send()
    for copy in copies:
        copy.wait()


def gather_and_project(mol_len, small, w_qkv, w_out, w_in, w_back, tokens, cotangent):
    slots = mol_len.shape[0]
    rows, width = tokens.shape
    block = rows // slots
    wide = 3 * width
    vmem = pl.BlockSpec(memory_space=pltpu.VMEM)
    anywhere = pl.BlockSpec(memory_space=pl.ANY)
    square = (width, width)
    return pl.pallas_call(
        gather_kernel,
        out_shape=[
            jax.ShapeDtypeStruct((slots, wide, block), bf16),
            jax.ShapeDtypeStruct((width, rows), bf16),
            jax.ShapeDtypeStruct((width, wide), bf16),
            jax.ShapeDtypeStruct(square, bf16),
            jax.ShapeDtypeStruct(square, bf16),
            jax.ShapeDtypeStruct(square, bf16),
            jax.ShapeDtypeStruct((rows // 2, width), bf16),
            jax.ShapeDtypeStruct((rows // 2, width), bf16),
            jax.ShapeDtypeStruct((16, width), f32),
            jax.ShapeDtypeStruct((slots, 128), jnp.int32),
        ],
        in_specs=[pl.BlockSpec(memory_space=pltpu.SMEM)] + [vmem] * 6 + [anywhere],
        out_specs=[anywhere] * 8 + [vmem] * 2,
        scratch_shapes=[
            pltpu.VMEM((DEVICES, 2 * SHARD, wide // 2 + 128), bf16),
            pltpu.VMEM((DEVICES, 2 * SHARD, wide // 2), bf16),
            pltpu.VMEM((width, wide), bf16),
            pltpu.VMEM(square, bf16),
            pltpu.VMEM(square, bf16),
            pltpu.VMEM(square, bf16),
            pltpu.VMEM((wide, width), bf16),
            pltpu.VMEM((rows, width), f32),
            pltpu.VMEM((width, rows), bf16),
            pltpu.VMEM((slots, wide, block), bf16),
            pltpu.VMEM((wide, 128), f32),
            pltpu.VMEM((rows // 2, width), bf16),
            pltpu.VMEM((rows // 2, width), bf16),
            pltpu.VMEM((slots, 128), jnp.int32),
            pltpu.VMEM((slots, 128), jnp.int32),
            pltpu.SemaphoreType.DMA((5,)),
            pltpu.SemaphoreType.DMA((5, CHIPS + 1)),
            pltpu.SemaphoreType.DMA((3,)),
            pltpu.SemaphoreType.DMA((6 + slots // 2,)),
            pltpu.SemaphoreType.DMA((slots + 6,)),
        ],
        compiler_params=pltpu.CompilerParams(
            collective_id=0, has_side_effects=True, vmem_limit_bytes=60 * MIB
        ),
    )(mol_len, small, w_qkv, w_out, w_in, w_back, tokens, cotangent)


def middle_kernel(
    packed,
    head_dim,
    len_ref,
    qkv_ref,
    tok_first,
    tok_second,
    cot_first,
    cot_second,
    wout_ref,
    win_ref,
    wback_ref,
    vec_ref,
    mixed_ref,
    dmix_ref,
    dqkv_ref,
    gvec_ref,
    *rest,
):
    if packed:
        packed_ref, gout_ref, gin_ref, gback_ref, *rest = rest
    else:
        gout_ref, gin_ref, gback_ref, *rest = rest
    probs, ctx_s, linv_s, dctx_s, tok_ref, cot_ref = rest
    step = pl.program_id(0)
    block, width = tok_ref.shape
    slot = 32
    group = 4
    heads = width // head_dim
    span = group * head_dim
    scale = head_dim ** (-0.5)
    length = len_ref[step, 0]
    first = step < pl.num_programs(0) // 2
    tok_ref[...] = jnp.where(first, tok_first[...], tok_second[...])
    cot_ref[...] = jnp.where(first, cot_first[...], cot_second[...])

    @pl.when(step == 0)
    def _():
        gout_ref[...] = jnp.zeros_like(gout_ref)
        gin_ref[...] = jnp.zeros_like(gin_ref)
        gback_ref[...] = jnp.zeros_like(gback_ref)
        gvec_ref[...] = jnp.zeros_like(gvec_ref)

    def run(size):
        extra = (slot - head_dim, size)
        sub = lax.broadcasted_iota(jnp.int32, extra, 0)
        lane = lax.broadcasted_iota(jnp.int32, extra, 1)
        one_row = jnp.where(sub == 0, 1.0, 0.0).astype(f32)
        two_rows = jnp.where(sub <= 1, 1.0, 0.0).astype(f32)
        mask_row = jnp.where((sub == 0) & (lane >= length), masked_score, 0.0).astype(f32)

        def group_rows(base, g):
            return slice(base + g * span, base + (g + 1) * span)

        def load(base, g):
            return qkv_ref[group_rows(base, g), :size].astype(f32)

        def place(j, rows):
            parts = []
            if j > 0:
                parts.append(jnp.zeros((slot * j, size), bf16))
            parts.append(rows)
            if j < group - 1:
                parts.append(jnp.zeros((slot * (group - 1 - j), size), bf16))
            return jnp.concatenate(parts, axis=0)

        def pieces(values):
            return [values[head_dim * j : head_dim * (j + 1)] for j in range(group)]

        def padded(values, tail):
            return [jnp.concatenate([p, tail], axis=0).astype(bf16) for p in pieces(values)]

        ahead = 3 if size > 128 else 6

        def forward():
            q, k, v, scores, weights, outs = {}, {}, {}, {}, {}, {}
            for t in range(heads + 2 * ahead):
                if t < heads:
                    g, j = divmod(t, group)
                    if j == 0:
                        q[g] = padded(load(0, g), one_row)
                        k[g] = jnp.concatenate(padded(load(width, g), mask_row), axis=0).T
                        v[g] = padded(load(2 * width, g), one_row)
                    scores[t] = dot(k[g], place(j, q[g][j]), 1, 0)
                h = t - ahead
                if 0 <= h < heads:
                    s = scores.pop(h)
                    peak = jnp.max(s, axis=0, keepdims=True)
                    weights[h] = jnp.exp2((s - peak) * (scale * log2_e)).astype(bf16)
                    probs[h, :size, :size] = weights[h]
                h = t - 2 * ahead
                if 0 <= h < heads:
                    g, j = divmod(h, group)
                    o = dot(v[g][j], weights.pop(h), 1, 0)
                    inverse = 1.0 / o[head_dim : head_dim + 1]
                    linv_s[h, :, :size] = jnp.broadcast_to(inverse, (8, size))
                    outs[h] = o[:head_dim] * inverse
                    if j == group - 1:
                        parts = [outs.pop(h - group + 1 + i) for i in range(group)]
                        ctx_s[group_rows(0, g), :size] = jnp.concatenate(parts, axis=0)

        forward()

        live = (lax.broadcasted_iota(jnp.int32, (size, 1), 0) < length).astype(f32)
        out_bias, gain, shift = vec_ref[4:5], vec_ref[5:6], vec_ref[6:7]
        in_bias, back_bias = vec_ref[7:8], vec_ref[8:9]
        x = tok_ref[:size].astype(f32)
        dy = cot_ref[:size].astype(f32)
        ctx_t = ctx_s[:, :size].astype(bf16)
        attn = dot(ctx_t.T, wout_ref[...], 1, 0) + out_bias
        mixed = x + live * attn
        unit, factor = normalize(mixed)
        normed = (unit * gain + shift).astype(bf16)
        pre = dot(normed, win_ref[...], 1, 0) + in_bias
        cdf = 0.5 * (1.0 + lax.erf(pre * 0.7071067811865476))
        act = (pre * cdf).astype(bf16)
        slope = cdf + pre * jnp.exp(-0.5 * pre * pre) * 0.3989422804014327
        branch = dot(act, wback_ref[...], 1, 0) + back_bias
        mixed_ref[:size] = (mixed + live * branch).astype(bf16)
        d_ffn = live * dy
        gvec_ref[4] += fold_rows(d_ffn)
        d_ffn = d_ffn.astype(bf16)
        gback_ref[...] += dot(act.T, d_ffn, 1, 0)
        d_act = dot(d_ffn, wback_ref[...], 1, 1)
        d_pre = (d_act * slope).astype(bf16)
        gvec_ref[3] += fold_rows(d_pre.astype(f32))
        gin_ref[...] += dot(normed.T, d_pre, 1, 0)
        d_normed = dot(d_pre, win_ref[...], 1, 1)
        gvec_ref[1] += fold_rows(d_normed * unit)
        gvec_ref[2] += fold_rows(d_normed)
        d_mixed = dy + norm_backward(d_normed, gain, unit, factor)
        dmix_ref[:size] = d_mixed
        d_attn = (live * d_mixed).astype(bf16)
        gvec_ref[0] += fold_rows(d_attn.astype(f32))
        gout_ref[...] += dot(ctx_t, d_attn, 1, 0)
        dctx_s[:, :size] = dot(wout_ref[...], d_attn, 1, 1).astype(bf16)

        behind = 3 if size > 128 else 6

        def backward():
            q, k, v, d, d_probs, d_scores = {}, {}, {}, {}, {}, {}
            d_q, d_k, d_v = {}, {}, {}
            for t in range(heads + 2 * behind):
                if t < heads:
                    g, j = divmod(t, group)
                    if j == 0:
                        q[g] = padded(load(0, g), one_row)
                        k[g] = padded(load(width, g), one_row)
                        v[g] = jnp.concatenate(padded(load(2 * width, g), two_rows), axis=0).T
                        d_out = pieces(dctx_s[group_rows(0, g), :size].astype(f32))
                        out = pieces(ctx_s[group_rows(0, g), :size])
                        for i in range(group):
                            here = d_out[i] * linv_s[g * group + i, :1, :size]
                            inner = -jnp.sum(here * out[i], axis=0, keepdims=True)
                            high = inner.astype(bf16).astype(f32)
                            blank = jnp.zeros((slot - head_dim - 2, size), f32)
                            tail = [here, high, inner - high, blank]
                            d[g * group + i] = jnp.concatenate(tail, axis=0).astype(bf16)
                    d_probs[t] = dot(v[g], place(j, d[t]), 1, 0)
                h = t - behind
                if 0 <= h < heads:
                    p = probs[h, :size, :size]
                    d_scores[h] = (p.astype(f32) * d_probs.pop(h)).astype(bf16)
                h = t - 2 * behind
                if 0 <= h < heads:
                    g, j = divmod(h, group)
                    ds = d_scores.pop(h)
                    d_v[h] = dot(d.pop(h), probs[h, :size, :size], 1, 1)[:head_dim]
                    d_q[h] = dot(k[g][j], ds, 1, 0)[:head_dim] * scale
                    d_k[h] = dot(q[g][j], ds, 1, 1)[:head_dim] * scale
                    if j == group - 1:
                        for base, parts in ((0, d_q), (width, d_k), (2 * width, d_v)):
                            some = [parts.pop(h - group + 1 + i) for i in range(group)]
                            dqkv_ref[group_rows(base, g), :size] = jnp.concatenate(
                                some, axis=0
                            ).astype(bf16)

        backward()

        if size < block:
            mixed_ref[size:] = tok_ref[size:]
            dmix_ref[size:] = cot_ref[size:].astype(f32)
            dqkv_ref[:, size:] = jnp.zeros((3 * width, block - size), bf16)

    half = block // 2

    @pl.when(length == 0)
    def _():
        mixed_ref[...] = tok_ref[...]
        dmix_ref[...] = cot_ref[...].astype(f32)
        dqkv_ref[...] = jnp.zeros_like(dqkv_ref)

    @pl.when((length > 0) & (length <= half))
    def _():
        run(half)

    @pl.when(length > half)
    def _():
        run(block)

    if packed:

        @pl.when(step == pl.num_programs(0) - 1)
        def _():
            columns = width // 2
            for i in range(DEVICES):
                p = (i % 2) * CHIPS + i // 2
                rows = slice(SHARD * i, SHARD * (i + 1))
                top = jnp.concatenate([gout_ref[rows], gback_ref[rows, :columns]], axis=1)
                bottom = jnp.concatenate([gin_ref[rows], gback_ref[rows, columns:]], axis=1)
                packed_ref[p] = jnp.concatenate([top, bottom], axis=0).astype(bf16)


def middle(lengths, qkv, tokens, cotangent, w_out, w_in, w_back, vectors, packed):
    slots, wide, block = qkv.shape
    rows, width = slots * block, wide // 3
    square = (width, width)
    shared = slots // 2

    def whole(shape):
        return pl.BlockSpec(shape, lambda m: (0,) * len(shape))

    by_rows = pl.BlockSpec((block, width), lambda m: (m, 0))
    if packed:
        first = pl.BlockSpec((block, width), lambda m: (2 * jnp.minimum(m, shared - 1), 0))
        second = pl.BlockSpec((block, width), lambda m: (jnp.maximum(m - shared, 0), 0))
    else:
        first = pl.BlockSpec((block, width), lambda m: (jnp.minimum(m, shared - 1), 0))
        second = pl.BlockSpec((block, width), lambda m: (jnp.maximum(m, shared), 0))
    out_specs = [
        by_rows,
        by_rows,
        pl.BlockSpec((3 * width, block), lambda m: (0, m)),
        whole((5, 8, width)),
    ]
    out_shape = [
        jax.ShapeDtypeStruct((rows, width), bf16),
        jax.ShapeDtypeStruct((rows, width), f32),
        jax.ShapeDtypeStruct((3 * width, rows), bf16),
        jax.ShapeDtypeStruct((5, 8, width), f32),
    ]
    scratch = [
        pltpu.VMEM((HEADS, block, block), bf16),
        pltpu.VMEM((width, block), f32),
        pltpu.VMEM((HEADS, 8, block), f32),
        pltpu.VMEM((width, block), bf16),
        pltpu.VMEM((block, width), bf16),
        pltpu.VMEM((block, width), bf16),
    ]
    if packed:
        shape = (DEVICES, 2 * SHARD, width + width // 2)
        out_specs.append(whole(shape))
        out_shape.append(jax.ShapeDtypeStruct(shape, bf16))
        scratch = [pltpu.VMEM(square, f32)] * 3 + scratch
    else:
        out_specs += [whole(square)] * 3
        out_shape += [jax.ShapeDtypeStruct(square, f32)] * 3
    return pl.pallas_call(
        functools.partial(middle_kernel, packed, width // HEADS),
        grid=(slots,),
        in_specs=[
            pl.BlockSpec(memory_space=pltpu.SMEM),
            pl.BlockSpec((None, 3 * width, block), lambda m: (m, 0, 0)),
            first,
            second,
            first,
            second,
            whole(square),
            whole(square),
            whole(square),
            whole((16, width)),
        ],
        out_specs=out_specs,
        scratch_shapes=scratch,
        out_shape=out_shape,
        compiler_params=pltpu.CompilerParams(vmem_limit_bytes=58 * MIB),
    )(lengths, qkv, *tokens, *cotangent, w_out, w_in, w_back, vectors)


def scatter_kernel(
    sr_hbm,
    dqkv_hbm,
    unit_hbm,
    fq_hbm,
    tok_hbm,
    odd_hbm,
    dmix_hbm,
    mixed_hbm,
    vec_ref,
    gvec_ref,
    grad_hbm,
    grad_out,
    mixed_out,
    gq_ref,
    gr_ref,
    sq,
    sr,
    rq_sib,
    rr_sib,
    rq,
    rr,
    dqkv,
    unit_t,
    fq,
    tok,
    dmix,
    grad,
    mixed,
    gain_wide,
    shift_wide,
    small_wide,
    sums,
    result,
    send_sem,
    recv_sem,
    swap_send,
    swap_recv,
    copy_sem,
):
    at = Place()
    at.greet()
    rows, width = tok.shape
    wide = 3 * width
    half_q = wide // 2
    slots = 8
    block = rows // slots
    mine, theirs = at.c * CHIPS, (1 - at.c) * CHIPS
    own = at.block(at.c, at.z, at.y, at.x)
    level_rows = 8 * SHARD

    def local(src, dst, i):
        copy = pltpu.make_async_copy(src, dst, copy_sem.at[i])
        copy.start()
        return copy

    sr_in = local(sr_hbm, sr, 0)
    unit_in = local(unit_hbm, unit_t, 1)
    dqkv_in = local(dqkv_hbm, dqkv, 2)
    fq_in = local(fq_hbm, fq, 3)
    shared = slots // 2

    def rows_of(i, count=1):
        return pl.ds(i * block, count * block)

    mixed_in = local(mixed_hbm.at[rows_of(shared, shared)], mixed, 4)
    late = [local(dmix_hbm, dmix, 5), local(odd_hbm, tok.at[rows_of(shared, shared)], 6)]
    for i in range(shared):
        late.append(local(tok_hbm.at[rows_of(2 * i)], tok.at[rows_of(i)], 7 + i))

    def swap_copy(src, dst, i):
        return pltpu.make_async_remote_copy(
            src_ref=src,
            dst_ref=dst,
            send_sem=swap_send.at[i],
            recv_sem=swap_recv.at[i],
            device_id=(at.sib,),
            device_id_type=MESH,
        )

    slabs = (
        (sq, rq_sib, rq, 0, 640),
        (sq, rq_sib, rq, 640, 640),
        (sr, rr_sib, rr, 0, 1152),
    )

    def cut(ref, k, first, count):
        return ref.at[pl.ds(first, count), :, pl.ds(slabs[k][3], slabs[k][4])]

    def piece(ref, k, p):
        _, _, _, column, columns = slabs[k]
        return ref[p, :, column : column + columns].astype(f32)

    def put(k, p, value):
        slab, _, _, column, columns = slabs[k]
        slab[p, :, column : column + columns] = value.astype(bf16)

    def remote(k, src, dst, target, sem):
        return pltpu.make_async_remote_copy(
            src_ref=src,
            dst_ref=dst,
            send_sem=send_sem.at[k],
            recv_sem=recv_sem.at[k, sem],
            device_id=(target,),
            device_id_type=MESH,
        )

    def x_type(j):
        return at.block(at.c, j, at.y, 1 - at.x)

    def y_type(j):
        return at.block(at.c, j, 1 - at.y, at.x)

    def corner_type(j):
        return at.block(at.c, j, 1 - at.y, 1 - at.x)

    def column_type(j):
        return at.block(at.c, j, at.y, at.x)

    def sib_copy(k, j):
        src = cut(slabs[k][0], k, theirs + 4 * j, 4)
        return remote(k, src, cut(slabs[k][1], k, 4 * j, 4), at.sib, j)

    def sib_send(k, j):
        sib_copy(k, j).start()

    def step_copy(k, src, slot, target):
        src = cut(slabs[k][0], k, src, 1)
        return remote(k, src, cut(slabs[k][2], k, slot, 1), target, PLANES + slot)

    def x_send(k, j):
        step_copy(k, x_type(j), 4 + j, at.xn).start()

    def y_send(k, j):
        step_copy(k, y_type(j), 8 + j, at.yn).start()

    def sib_add(k, j):
        sib_copy(k, j).wait_recv()

        def body(i, carry):
            p = mine + 4 * j + i
            put(k, p, piece(slabs[k][0], k, p) + piece(slabs[k][1], k, 4 * j + i))
            return carry

        lax.fori_loop(0, 4, body, 0)
        step_copy(k, corner_type(j), j, at.yn if j % 2 == 0 else at.xn).start()
        (y_send if j % 2 == 0 else x_send)(k, j)

    def corner_add(k, j):
        step_copy(k, own, j, at.sib).wait_recv()
        p = x_type(j) if j % 2 == 0 else y_type(j)
        put(k, p, piece(slabs[k][0], k, p) + piece(slabs[k][2], k, j))
        (x_send if j % 2 == 0 else y_send)(k, j)

    def plane_add(k, j):
        p = column_type(j)
        step_copy(k, own, 4 + j, at.sib).wait_recv()
        step_copy(k, own, 8 + j, at.sib).wait_recv()
        received = piece(slabs[k][2], k, 4 + j) + piece(slabs[k][2], k, 8 + j)
        put(k, p, piece(slabs[k][0], k, p) + received)

        @pl.when(at.z != j)
        def _():
            step_copy(k, p, 12 + at.z, at.me + 8 * (j - at.z)).start()

    def land(k):
        total = gq_ref if slabs[k][0] is sq else gr_ref
        columns = slice(slabs[k][3], slabs[k][3] + slabs[k][4])
        total[:, columns] = piece(slabs[k][0], k, own)
        for j in range(PLANES):

            @pl.when(at.z != j)
            def _():
                step_copy(k, own, 12 + j, at.sib).wait_recv()
                total[:, columns] += piece(slabs[k][2], k, 12 + j)

    def prepare():
        gain_wide[...] = jnp.broadcast_to(vec_ref[0:1], (128, width)).T
        shift_wide[...] = jnp.broadcast_to(vec_ref[1:2], (128, width)).T
        ones = jnp.ones((16, rows), bf16)
        for part in range(3):
            columns = slice(part * width, (part + 1) * width)
            sums[:, columns] = dot(ones, dqkv[columns], 1, 1)[:8]
        lines = [jnp.zeros((2, width), f32), sums[0:1, :width], sums[0:1, 2 * width :]]
        lines += [jnp.sum(gvec_ref[i], axis=0, keepdims=True) for i in range(5)]
        lines.append(jnp.zeros((128 - 9, width), f32))
        small_wide[...] = jnp.concatenate(lines, axis=0).T

    def weight_grad(j, part):
        lines = pl.ds(j * level_rows, level_rows)
        columns = slice(part * width, (part + 1) * width)
        product = dot(unit_t[lines], dqkv[columns], 1, 1)
        weight = fq[lines, columns].astype(f32)
        line = sums[0:1, columns]
        gain_sum = jnp.sum(weight * product, axis=1, keepdims=True)
        shift_sum = jnp.sum(weight * line, axis=1, keepdims=True)
        lane = lax.broadcasted_iota(jnp.int32, (level_rows, 128), 1)
        small_wide[lines] += jnp.where(
            lane == 0, gain_sum, jnp.where(lane == 1, shift_sum, 0.0)
        )
        gain = jnp.concatenate([gain_wide[lines]] * (width // 128), axis=1)
        shift = jnp.concatenate([shift_wide[lines]] * (width // 128), axis=1)
        result[:, columns] = gain * product + shift * line
        if part < 2:
            return
        small = small_wide[lines]
        blank = jnp.zeros((SHARD, 128), f32)
        for i in range(8):
            p = (i % 2) * CHIPS + 4 * j + i // 2
            some = slice(SHARD * i, SHARD * (i + 1))
            top = jnp.concatenate([result[some, :half_q], small[some]], axis=1)
            bottom = jnp.concatenate([result[some, half_q:], blank], axis=1)
            sq[p] = jnp.concatenate([top, bottom], axis=0).astype(bf16)

    grads = []

    def input_grad(m):
        some = slice(m * block, (m + 1) * block)
        d_normed = dot(fq[...], dqkv[:, some], 1, 0).T
        unit, factor = normalize(tok[some].astype(f32))
        share = norm_backward(d_normed, vec_ref[0:1], unit, factor)
        grad[some] = (dmix[some] + share).astype(bf16)
        if m < shared:
            grads.append(local(grad.at[rows_of(m)], grad_hbm.at[rows_of(m)], 7 + shared + m))
        else:
            swap_copy(grad.at[rows_of(m)], grad_out.at[rows_of(m - shared)], 0).start()

    sr_in.wait()
    at.await_all()
    sib_send(2, 0)
    sib_send(2, 1)
    sib_send(2, 2)
    sib_add(2, 0)
    sib_send(2, 3)
    sib_add(2, 1)
    sib_add(2, 2)
    sib_add(2, 3)
    unit_in.wait()
    dqkv_in.wait()
    fq_in.wait()
    prepare()
    weight_grad(0, 0)
    weight_grad(0, 1)
    weight_grad(0, 2)
    weight_grad(3, 0)
    corner_add(2, 1)
    sib_send(1, 0)
    corner_add(2, 0)
    corner_add(2, 3)
    weight_grad(3, 1)
    sib_send(0, 0)
    corner_add(2, 2)
    weight_grad(3, 2)
    sib_send(1, 3)
    sib_send(0, 3)
    sib_add(0, 0)
    sib_add(1, 0)
    weight_grad(2, 0)
    plane_add(2, 1)
    plane_add(2, 0)
    sib_add(1, 3)
    weight_grad(2, 1)
    sib_add(0, 3)
    plane_add(2, 3)
    weight_grad(2, 2)
    sib_send(1, 2)
    weight_grad(1, 0)
    sib_add(1, 2)
    corner_add(0, 0)
    plane_add(2, 2)
    sib_send(0, 2)
    corner_add(1, 0)
    weight_grad(1, 1)
    corner_add(0, 3)
    weight_grad(1, 2)
    sib_send(1, 1)
    sib_send(0, 1)
    corner_add(1, 2)
    plane_add(0, 0)
    mixed_in.wait()
    swap_copy(mixed, mixed_out, 1).start()
    for copy in late:
        copy.wait()
    sib_add(0, 2)
    corner_add(1, 3)
    sib_add(1, 1)
    sib_add(0, 1)
    plane_add(0, 3)
    plane_add(1, 0)
    input_grad(0)
    plane_add(1, 2)
    corner_add(0, 2)
    corner_add(1, 1)
    input_grad(1)
    input_grad(2)
    corner_add(0, 1)
    plane_add(1, 3)
    plane_add(1, 1)
    input_grad(3)
    input_grad(4)
    plane_add(0, 2)
    plane_add(0, 1)
    input_grad(5)
    input_grad(6)
    land(1)
    input_grad(7)
    land(2)
    land(0)
    for k in range(len(slabs)):
        every = cut(slabs[k][0], k, 0, DEVICES - 1)
        remote(k, every, every, at.sib, 0).wait_send()
    for copy in grads:
        copy.wait()
    swap_copy(grad.at[rows_of(shared, shared)], grad_out, 0).wait()
    swap_copy(mixed, mixed_out, 1).wait()


def scatter(packed, dqkv, unit_t, full_qkv, tokens, odd_tokens, d_mixed, mixed, vectors, sums):
    rows, width = tokens.shape
    wide = 3 * width
    vmem = pl.BlockSpec(memory_space=pltpu.VMEM)
    anywhere = pl.BlockSpec(memory_space=pl.ANY)
    tall = 2 * SHARD
    widths = (wide // 2 + 128, wide // 2)
    return pl.pallas_call(
        scatter_kernel,
        out_shape=[jax.ShapeDtypeStruct((rows // 2, width), bf16)] * 3
        + [jax.ShapeDtypeStruct((tall, w), f32) for w in widths],
        in_specs=[anywhere] * 8 + [vmem] * 2,
        out_specs=[anywhere] * 3 + [vmem] * 2,
        scratch_shapes=[pltpu.VMEM((DEVICES, tall, w), bf16) for w in widths]
        + [pltpu.VMEM((CHIPS, tall, w), bf16) for w in widths]
        + [pltpu.VMEM((4 * PLANES, tall, w), bf16) for w in widths]
        + [
            pltpu.VMEM((wide, rows), bf16),
            pltpu.VMEM((width, rows), bf16),
            pltpu.VMEM((width, wide), bf16),
            pltpu.VMEM((rows, width), bf16),
            pltpu.VMEM((rows, width), f32),
            pltpu.VMEM((rows, width), bf16),
            pltpu.VMEM((rows // 2, width), bf16),
            pltpu.VMEM((width, 128), f32),
            pltpu.VMEM((width, 128), f32),
            pltpu.VMEM((width, 128), f32),
            pltpu.VMEM((8, wide), f32),
            pltpu.VMEM((8 * SHARD, wide), f32),
            pltpu.SemaphoreType.DMA((3,)),
            pltpu.SemaphoreType.DMA((3, 5 * PLANES)),
            pltpu.SemaphoreType.DMA((2,)),
            pltpu.SemaphoreType.DMA((2,)),
            pltpu.SemaphoreType.DMA((15,)),
        ],
        compiler_params=pltpu.CompilerParams(
            collective_id=1, has_side_effects=True, vmem_limit_bytes=60 * MIB
        ),
    )(packed, dqkv, unit_t, full_qkv, tokens, odd_tokens, d_mixed, mixed, vectors, sums)


def finish_kernel(
    mixed_even, mixed_odd, grad_even, grad_odd, q_ref, r_ref, mixed, grad, g_qkv, g_out, g_in, g_back, *lines
):
    block = mixed_even.shape[0]
    mixed[:block] = mixed_even[...]
    mixed[block:] = mixed_odd[...]
    grad[:block] = grad_even[...]
    grad[block:] = grad_odd[...]

    @pl.when(pl.program_id(0) == 0)
    def _():
        width = g_out.shape[1]
        half_q = 3 * width // 2
        half = width // 2
        g_qkv[:, :half_q] = q_ref[:SHARD, :half_q]
        g_qkv[:, half_q:] = q_ref[SHARD:, :half_q]
        g_out[...] = r_ref[:SHARD, :width]
        g_in[...] = r_ref[SHARD:, :width]
        g_back[:, :half] = r_ref[:SHARD, width:]
        g_back[:, half:] = r_ref[SHARD:, width:]
        small = q_ref[:SHARD, half_q:].T
        for i, line in enumerate(lines):
            line[...] = small[i, :SHARD]


def finish(mixed, mixed_odd, grad, grad_odd, q_part, r_part, slots):
    rows, width = mixed.shape
    block = rows // slots
    single = pl.BlockSpec((block, width), lambda i: (i, 0))
    double = pl.BlockSpec((2 * block, width), lambda i: (i, 0))

    def whole(shape):
        return pl.BlockSpec(shape, lambda i: (0,) * len(shape))

    shapes = [(SHARD, 3 * width)] + [(SHARD, width)] * 3 + [(SHARD,)] * 9
    return pl.pallas_call(
        finish_kernel,
        grid=(slots // 2,),
        out_shape=[jax.ShapeDtypeStruct((rows, width), bf16)] * 2
        + [jax.ShapeDtypeStruct(s, f32) for s in shapes],
        in_specs=[single] * 4 + [whole(q_part.shape), whole(r_part.shape)],
        out_specs=[double] * 2 + [whole(s) for s in shapes],
    )(mixed, mixed_odd, grad, grad_odd, q_part, r_part)


def on_one_plan(tokens, mol_len, cotangent, vectors, w_qkv, w_out, w_in, w_back):
    slots = mol_len.shape[0]
    small = jnp.pad(jnp.stack(vectors), ((0, 16 - len(vectors)), (0, 128 - SHARD)))
    (
        qkv,
        unit_t,
        full_qkv,
        full_out,
        full_in,
        full_back,
        odd_tokens,
        odd_cotangent,
        lines,
        lengths,
    ) = gather_and_project(mol_len, small, w_qkv, w_out, w_in, w_back, tokens, cotangent)
    mixed, d_mixed, dqkv, sums, packed = middle(
        lengths,
        qkv,
        (tokens, odd_tokens),
        (cotangent, odd_cotangent),
        full_out,
        full_in,
        full_back,
        lines,
        True,
    )
    grad, grad_odd, mixed_odd, q_part, r_part = scatter(
        packed, dqkv, unit_t, full_qkv, tokens, odd_tokens, d_mixed, mixed, lines, sums
    )
    mixed_out, token_grad, g_qkv, g_out, g_in, g_back, *small = finish(
        mixed, mixed_odd, grad, grad_odd, q_part, r_part, slots
    )
    return mixed_out, token_grad, small, g_qkv, g_out, g_in, g_back


def on_any_plan(tokens, mol_len, cotangent, vectors, w_qkv, w_out, w_in, w_back):
    slots = mol_len.shape[0]
    rows, width = tokens.shape

    def gather(array, axis):
        return lax.all_gather(array, "fsdp", axis=axis, tiled=True)

    lines = gather(jnp.stack(vectors), 1).astype(f32)
    lines = jnp.pad(lines, ((0, 16 - len(vectors)), (0, 0)))
    full_qkv, full_out, full_in, full_back = (
        gather(w, 0) for w in (w_qkv, w_out, w_in, w_back)
    )
    unit, factor = normalize(tokens.astype(f32))
    normed = (unit * lines[0] + lines[1]).astype(bf16)
    qkv = jnp.dot(normed, full_qkv, preferred_element_type=f32)
    qkv = (qkv + jnp.concatenate([lines[2], jnp.zeros_like(lines[2]), lines[3]])).astype(bf16)
    qkv = qkv.reshape(slots, rows // slots, 3 * width).transpose(0, 2, 1)
    mixed_out, d_mixed, dqkv, sums, g_out, g_in, g_back = middle(
        jnp.broadcast_to(mol_len[:, None], (slots, 128)),
        qkv,
        (tokens, tokens),
        (cotangent, cotangent),
        full_out,
        full_in,
        full_back,
        lines,
        False,
    )
    g_qkv = jnp.einsum("rf,dr->fd", normed, dqkv, preferred_element_type=f32)
    d_normed = jnp.einsum("dr,fd->rf", dqkv, full_qkv, preferred_element_type=f32)
    totals = jnp.sum(dqkv.astype(f32), axis=1)
    small = [jnp.sum(d_normed * unit, axis=0), jnp.sum(d_normed, axis=0)]
    small += [totals[:width], totals[2 * width :]]
    small += [jnp.sum(sums[i], axis=0) for i in range(5)]
    share = norm_backward(d_normed, lines[0], unit, factor)
    token_grad = (d_mixed + share).astype(bf16)

    def scatter_sum(array, axis):
        return lax.psum_scatter(array, "fsdp", scatter_dimension=axis, tiled=True)

    small = scatter_sum(jnp.stack(small), 1)
    return (
        mixed_out,
        token_grad,
        [small[i] for i in range(9)],
        *(scatter_sum(g, 0) for g in (g_qkv, g_out, g_in, g_back)),
    )


def per_device(
    devices,
    tokens,
    mol_len,
    cotangent,
    ln1_gain,
    ln1_bias,
    w_qkv,
    q_bias,
    v_bias,
    w_out,
    out_bias,
    ln2_gain,
    ln2_bias,
    w_in,
    in_bias,
    w_back,
    back_bias,
):
    vectors = [
        ln1_gain,
        ln1_bias,
        q_bias,
        v_bias,
        out_bias,
        ln2_gain,
        ln2_bias,
        in_bias,
        back_bias,
    ]
    known = devices == DEVICES and w_qkv.shape[0] == SHARD
    plan = on_one_plan if known else on_any_plan
    mixed_out, token_grad, small, g_qkv, g_out, g_in, g_back = plan(
        tokens, mol_len, cotangent, vectors, w_qkv, w_out, w_in, w_back
    )
    return (
        mixed_out,
        token_grad,
        small[0],
        small[1],
        g_qkv,
        small[2],
        small[3],
        g_out,
        small[4],
        small[5],
        small[6],
        g_in,
        small[7],
        g_back,
        small[8],
    )


def solution(mesh):
    line, matrix = P("fsdp"), P("fsdp", None)
    return jax.shard_map(
        functools.partial(per_device, mesh.shape["fsdp"]),
        mesh=mesh,
        in_specs=(
            matrix,
            line,
            matrix,
            line,
            line,
            matrix,
            line,
            line,
            matrix,
            line,
            line,
            line,
            matrix,
            line,
            matrix,
            line,
        ),
        out_specs=(
            matrix,
            matrix,
            line,
            line,
            matrix,
            line,
            line,
            matrix,
            line,
            line,
            line,
            matrix,
            line,
            matrix,
            line,
        ),
        check_vma=False,
    )
```

```python
import functools

import jax
import jax.numpy as jnp
from jax import lax
from jax.experimental import pallas as pl
from jax.experimental.pallas import tpu as pltpu
from jax.sharding import PartitionSpec as P

HEADS = 32

bf16 = jnp.bfloat16
f32 = jnp.float32
eps = 1e-05
masked_score = -1e30
log2_e = 1.4426950408889634
MESH = pl.DeviceIdType.MESH
MIB = 1 << 20

PLANES = 4
CHIPS = 4 * PLANES
DEVICES = 2 * CHIPS
SHARD = 24
VECTORS = 9


def dot(left, right, left_dim, right_dim):
    return lax.dot_general(
        left, right, (((left_dim,), (right_dim,)), ((), ())), preferred_element_type=f32
    )


def normalize(values):
    centred = values - jnp.mean(values, axis=-1, keepdims=True)
    factor = lax.rsqrt(jnp.mean(centred * centred, axis=-1, keepdims=True) + eps)
    return centred * factor, factor


def norm_backward(d_normed, gain, unit, factor):
    e = d_normed * gain
    inner = jnp.mean(e * unit, axis=-1, keepdims=True)
    return factor * (e - jnp.mean(e, axis=-1, keepdims=True) - unit * inner)


def fold_rows(values):
    rows, columns = values.shape
    return jnp.sum(values.reshape(rows // 8, 8, columns), axis=0)


class Place:
    def __init__(self):
        me = lax.axis_index("fsdp")
        self.me = me
        self.c = lax.rem(me, 2)
        self.x = lax.rem(me // 2, 2)
        self.y = lax.rem(me // 4, 2)
        self.z = me // 8
        self.sib = me + 1 - 2 * self.c
        self.xn = me + 2 - 4 * self.x
        self.yn = me + 4 - 8 * self.y

    def block(self, c, z, y, x):
        return ((c * PLANES + z) * 2 + y) * 2 + x

    def greet(self):
        sem = pltpu.get_barrier_semaphore()

        def signal(device):
            pl.semaphore_signal(sem, inc=1, device_id=(device,), device_id_type=MESH)

        for device in (self.sib, self.xn, self.yn):
            signal(device)
        for distance in range(1, PLANES):
            signal(lax.rem(self.me + 8 * distance, DEVICES))

    def await_all(self):
        pl.semaphore_wait(pltpu.get_barrier_semaphore(), 2 + PLANES)


def gather_kernel(
    len_ref,
    *refs,
):
    lines, refs = refs[:VECTORS], refs[VECTORS:]
    gather_body(len_ref, lines, *refs)


def gather_body(
    len_ref,
    lines,
    wq_ref,
    wo_ref,
    wi_ref,
    wb_ref,
    tok_ref,
    cot_hbm,
    qkv_hbm,
    unit_hbm,
    fq_hbm,
    fo_hbm,
    fi_hbm,
    fb_hbm,
    tok_hbm,
    cot_out,
    vec_ref,
    work_ref,
    gq,
    gr,
    fq,
    fo,
    fi,
    fb,
    fq_t,
    unit,
    unit_t,
    qkv,
    bias,
    tok_odd,
    cot_odd,
    len_send,
    len_recv,
    send_sem,
    recv_sem,
    swap_send,
    swap_recv,
    copy_sem,
):
    at = Place()
    at.greet()
    width = tok_ref.shape[1]
    slots, _, block = qkv.shape
    shared = slots // 2
    half_q = 3 * width // 2
    half = width // 2
    own = at.block(at.c, at.z, at.y, at.x)
    mine, theirs = at.c * CHIPS, (1 - at.c) * CHIPS
    slabs = ((gq, 0, 384), (gq, 384, 384), (gq, 768, 512), (gr, 0, 640), (gr, 640, 512))

    small = [line[...].astype(f32).reshape(1, SHARD) for line in lines]
    small = jnp.concatenate(small + [jnp.zeros((2 * SHARD - VECTORS, SHARD), f32)], axis=0)
    small = jnp.concatenate([small, jnp.zeros((2 * SHARD, 128 - SHARD), f32)], axis=1).astype(bf16)
    gq[own] = jnp.concatenate(
        [
            jnp.concatenate([wq_ref[:, :half_q], wq_ref[:, half_q:]], axis=0),
            small,
        ],
        axis=1,
    )
    gr[own] = jnp.concatenate(
        [
            jnp.concatenate([wo_ref[...], wi_ref[...]], axis=0),
            jnp.concatenate([wb_ref[:, :half], wb_ref[:, half:]], axis=0),
        ],
        axis=1,
    )

    def view(k, first, count):
        slab, column, columns = slabs[k]
        return slab.at[pl.ds(first, count), :, pl.ds(column, columns)]

    def remote(k, first, target, sem, count=1):
        return pltpu.make_async_remote_copy(
            src_ref=view(k, first, count),
            dst_ref=view(k, first, count),
            send_sem=send_sem.at[k],
            recv_sem=recv_sem.at[k, sem],
            device_id=(target,),
            device_id_type=MESH,
        )

    def send(k, b, target):
        remote(k, b, target, lax.rem(b, CHIPS)).start()

    def to_sib(k, b):
        remote(k, b, at.sib, CHIPS).start()

    def arrived(k, b):
        remote(k, b, at.sib, lax.rem(b, CHIPS)).wait_recv()

    def at_level(shift, body):
        level = at.z + shift
        if shift == 0:
            body(level)
        else:
            pl.when((level >= 0) & (level <= PLANES - 1))(lambda: body(level))

    def both(s):
        return (0,) if s == 0 else (-s, s)

    def own_plane(k):
        send(k, own, at.xn)
        send(k, own, at.yn)

    def own_column(k):
        for s in range(1, PLANES):
            for shift in both(s):
                at_level(shift, lambda level, shift=shift: send(k, own, at.me + 8 * shift))
        to_sib(k, own)

    def column(k, s):
        def body(level):
            b = at.block(at.c, level, at.y, at.x)
            arrived(k, b)
            send(k, b, at.xn)
            send(k, b, at.yn)
            to_sib(k, b)

        for shift in both(s):
            at_level(shift, body)

    def plane(k, s):
        def body(level):
            even = lax.rem(level, 2) == 0
            b = at.block(at.c, level, at.y, 1 - at.x)
            arrived(k, b)
            pl.when(even)(lambda: send(k, b, at.yn))
            to_sib(k, b)
            d = at.block(at.c, level, 1 - at.y, at.x)
            arrived(k, d)
            pl.when(jnp.logical_not(even))(lambda: send(k, d, at.xn))
            to_sib(k, d)

        for shift in both(s):
            at_level(shift, body)

    def corner(k):
        for j in range(PLANES):
            b = at.block(at.c, j, 1 - at.y, 1 - at.x)
            arrived(k, b)
            to_sib(k, b)

    def others(k):
        remote(k, theirs, at.sib, CHIPS, CHIPS).wait_recv()

    def rows_of(i):
        return pl.ds(i * block, block)

    cot_in = [
        pltpu.make_async_copy(
            cot_hbm.at[rows_of(2 * i + 1)], cot_odd.at[rows_of(i)], swap_recv.at[6 + i]
        )
        for i in range(shared)
    ]

    def swap_copy(src, dst, send, recv):
        return pltpu.make_async_remote_copy(
            src_ref=src,
            dst_ref=dst,
            send_sem=swap_send.at[send],
            recv_sem=swap_recv.at[recv],
            device_id=(at.sib,),
            device_id_type=MESH,
        )

    def tok_copy(i):
        return swap_copy(tok_ref.at[rows_of(2 * i + 1)], tok_odd.at[rows_of(i)], 0, i)

    def swap_start():
        swap_copy(len_send, len_recv, 2, 5).start()
        for i in range(shared):
            tok_copy(i).start()
        for i in range(shared):
            cot_in[i].wait()
            swap_copy(cot_odd.at[rows_of(i)], cot_out.at[rows_of(i)], 1, 4).start()

    def swap_end():
        swap_copy(len_send, len_recv, 2, 5).wait()
        swap_copy(tok_odd, tok_odd, 0, 0).wait_send()
        swap_copy(cot_odd, cot_out, 1, 4).wait()
        place = lax.broadcasted_iota(jnp.int32, (shared, 128), 0)
        own_lengths = jnp.zeros((shared, 128), jnp.int32)
        odd_lengths = jnp.zeros((shared, 128), jnp.int32)
        for i in range(shared):
            own_lengths = jnp.where(place == i, len_send[2 * i : 2 * i + 1], own_lengths)
            odd_lengths = jnp.where(place == i, len_recv[2 * i + 1 : 2 * i + 2], odd_lengths)
        work_ref[:shared] = own_lengths
        work_ref[shared:] = odd_lengths

    for i in range(slots):
        len_send[i : i + 1] = jnp.full((1, 128), len_ref[i], jnp.int32)
    for copy in cot_in:
        copy.start()

    def norm_step(m):
        rows = rows_of(m)
        if m < shared:
            here = tok_ref[rows_of(2 * m)]
        else:
            tok_copy(m - shared).wait_recv()
            here = tok_odd[rows_of(m - shared)]
        values, _ = normalize(here.astype(f32))
        unit[rows] = values
        unit_t[:, rows] = values.astype(bf16).T

    def strip(i):
        return pl.ds(pl.multiple_of(i * 2 * SHARD, 2 * SHARD), 2 * SHARD)

    def stack(first, second):
        return jnp.concatenate([first, second], axis=0).astype(bf16)

    def build_q():
        def body(i, carry):
            first = gq[i].astype(f32)
            second = gq[CHIPS + i].astype(f32)
            fq[strip(i), :half_q] = stack(first[:SHARD, :half_q], second[:SHARD, :half_q])
            fq[strip(i), half_q:] = stack(first[SHARD:, :half_q], second[SHARD:, :half_q])
            return carry

        lax.fori_loop(0, CHIPS, body, 0)
        out(fq, fq_hbm)

    def build_r():
        def body(i, carry):
            first = gr[i].astype(f32)
            second = gr[CHIPS + i].astype(f32)
            fo[strip(i)] = stack(first[:SHARD, :width], second[:SHARD, :width])
            fi[strip(i)] = stack(first[SHARD:, :width], second[SHARD:, :width])
            fb[strip(i), :half] = stack(first[:SHARD, width:], second[:SHARD, width:])
            fb[strip(i), half:] = stack(first[SHARD:, width:], second[SHARD:, width:])
            return carry

        lax.fori_loop(0, CHIPS, body, 0)
        out(fo, fo_hbm)
        out(fi, fi_hbm)
        out(fb, fb_hbm)

    copies = []

    def out(src, dst):
        copy = pltpu.make_async_copy(src, dst, copy_sem.at[len(copies)])
        copy.start()
        copies.append(copy)

    def turn(part):
        columns = slice(part * width, (part + 1) * width)
        fq_t[columns] = fq[:, columns].T

    def spread_vectors():
        column_at = lax.broadcasted_iota(jnp.int32, (128, width), 1)
        entry = lax.broadcasted_iota(jnp.int32, (128, width), 0)
        spread = jnp.where(lax.rem(column_at, SHARD) == entry, 1.0, 0.0).astype(bf16)
        stacked = jnp.concatenate([gq[p, :16, half_q:] for p in range(DEVICES)], axis=0)
        wide = dot(stacked, spread, 1, 0)
        total = jnp.zeros((16, width), f32)
        column_at = lax.broadcasted_iota(jnp.int32, (16, width), 1)
        for p in range(DEVICES):
            first = SHARD * ((p % CHIPS) * 2 + p // CHIPS)
            here = (column_at >= first) & (column_at < first + SHARD)
            total = total + jnp.where(here, wide[16 * p : 16 * p + 16], 0.0)
        vec_ref[...] = total
        bias[:width] = jnp.broadcast_to(total[2:3], (128, width)).T
        bias[width : 2 * width] = jnp.zeros((width, 128), f32)
        bias[2 * width :] = jnp.broadcast_to(total[3:4], (128, width)).T

    def qkv_part(m, part):
        normed = (unit[m * block : (m + 1) * block] * vec_ref[0:1] + vec_ref[1:2]).astype(bf16)
        lines = slice(part * width, (part + 1) * width)
        result = dot(fq_t[lines], normed, 1, 1)
        added = jnp.concatenate([bias[lines]] * (block // 128), axis=1)
        qkv[m, lines] = (result + added).astype(bf16)
        if part == 2:
            out(qkv.at[m], qkv_hbm.at[m])

    norm_step(0)
    norm_step(1)
    at.await_all()
    swap_start()
    own_column(0)
    own_plane(4)
    own_column(1)
    own_plane(2)
    norm_step(2)
    own_plane(3)
    norm_step(3)
    own_plane(1)
    own_column(2)
    own_plane(0)
    own_column(3)
    column(0, 3)
    column(0, 1)
    own_column(4)
    plane(1, 0)
    column(0, 2)
    plane(0, 3)
    column(1, 3)
    plane(0, 1)
    norm_step(4)
    plane(0, 0)
    norm_step(5)
    column(1, 2)
    column(1, 1)
    plane(1, 3)
    plane(0, 2)
    column(2, 3)
    column(2, 1)
    column(2, 2)
    corner(0)
    plane(2, 0)
    plane(2, 3)
    plane(1, 1)
    plane(2, 1)
    plane(1, 2)
    plane(2, 2)
    norm_step(6)
    norm_step(7)
    column(3, 2)
    corner(1)
    plane(4, 0)
    corner(2)
    column(3, 3)
    plane(3, 0)
    others(0)
    others(1)
    column(3, 1)
    others(2)
    column(4, 3)
    build_q()
    column(4, 2)
    turn(0)
    turn(1)
    turn(2)
    spread_vectors()
    column(4, 1)
    qkv_part(0, 0)
    plane(3, 2)
    qkv_part(0, 1)
    qkv_part(0, 2)
    qkv_part(1, 0)
    qkv_part(1, 1)
    qkv_part(1, 2)
    qkv_part(2, 0)
    plane(3, 3)
    plane(4, 2)
    qkv_part(2, 1)
    plane(3, 1)
    plane(4, 3)
    plane(4, 1)
    qkv_part(2, 2)
    qkv_part(3, 0)
    qkv_part(3, 1)
    qkv_part(3, 2)
    qkv_part(4, 0)
    qkv_part(4, 1)
    qkv_part(4, 2)
    qkv_part(5, 0)
    corner(3)
    qkv_part(5, 1)
    qkv_part(5, 2)
    qkv_part(6, 0)
    corner(4)
    qkv_part(6, 1)
    qkv_part(6, 2)
    qkv_part(7, 0)
    others(3)
    qkv_part(7, 1)
    others(4)
    qkv_part(7, 2)
    build_r()
    out(unit_t, unit_hbm)
    out(tok_odd, tok_hbm)
    swap_end()
    for k in range(len(slabs)):
        remote(k, 0, at.sib, 0, DEVICES - 1).wait_send()
    for copy in copies:
        copy.wait()


def gather_and_project(mol_len, vectors, w_qkv, w_out, w_in, w_back, tokens, cotangent):
    slots = mol_len.shape[0]
    rows, width = tokens.shape
    block = rows // slots
    wide = 3 * width
    vmem = pl.BlockSpec(memory_space=pltpu.VMEM)
    anywhere = pl.BlockSpec(memory_space=pl.ANY)
    square = (width, width)
    return pl.pallas_call(
        gather_kernel,
        out_shape=[
            jax.ShapeDtypeStruct((slots, wide, block), bf16),
            jax.ShapeDtypeStruct((width, rows), bf16),
            jax.ShapeDtypeStruct((width, wide), bf16),
            jax.ShapeDtypeStruct(square, bf16),
            jax.ShapeDtypeStruct(square, bf16),
            jax.ShapeDtypeStruct(square, bf16),
            jax.ShapeDtypeStruct((rows // 2, width), bf16),
            jax.ShapeDtypeStruct((rows // 2, width), bf16),
            jax.ShapeDtypeStruct((16, width), f32),
            jax.ShapeDtypeStruct((slots, 128), jnp.int32),
        ],
        in_specs=[pl.BlockSpec(memory_space=pltpu.SMEM)] + [vmem] * (VECTORS + 5) + [anywhere],
        out_specs=[anywhere] * 8 + [vmem] * 2,
        scratch_shapes=[
            pltpu.VMEM((DEVICES, 2 * SHARD, wide // 2 + 128), bf16),
            pltpu.VMEM((DEVICES, 2 * SHARD, wide // 2), bf16),
            pltpu.VMEM((width, wide), bf16),
            pltpu.VMEM(square, bf16),
            pltpu.VMEM(square, bf16),
            pltpu.VMEM(square, bf16),
            pltpu.VMEM((wide, width), bf16),
            pltpu.VMEM((rows, width), f32),
            pltpu.VMEM((width, rows), bf16),
            pltpu.VMEM((slots, wide, block), bf16),
            pltpu.VMEM((wide, 128), f32),
            pltpu.VMEM((rows // 2, width), bf16),
            pltpu.VMEM((rows // 2, width), bf16),
            pltpu.VMEM((slots, 128), jnp.int32),
            pltpu.VMEM((slots, 128), jnp.int32),
            pltpu.SemaphoreType.DMA((5,)),
            pltpu.SemaphoreType.DMA((5, CHIPS + 1)),
            pltpu.SemaphoreType.DMA((3,)),
            pltpu.SemaphoreType.DMA((6 + slots // 2,)),
            pltpu.SemaphoreType.DMA((slots + 6,)),
        ],
        compiler_params=pltpu.CompilerParams(
            collective_id=0, has_side_effects=True, vmem_limit_bytes=60 * MIB
        ),
    )(mol_len, *vectors, w_qkv, w_out, w_in, w_back, tokens, cotangent)


def middle_kernel(
    packed,
    head_dim,
    len_ref,
    qkv_ref,
    tok_first,
    tok_second,
    cot_first,
    cot_second,
    wout_ref,
    win_ref,
    wback_ref,
    vec_ref,
    mixed_ref,
    dmix_ref,
    dqkv_ref,
    gvec_ref,
    *rest,
):
    if packed:
        packed_ref, gout_ref, gin_ref, gback_ref, *rest = rest
    else:
        gout_ref, gin_ref, gback_ref, *rest = rest
    probs, ctx_s, linv_s, dctx_s, tok_ref, cot_ref = rest
    step = pl.program_id(0)
    block, width = tok_ref.shape
    slot = 32
    group = 4
    heads = width // head_dim
    span = group * head_dim
    scale = head_dim ** (-0.5)
    length = len_ref[step, 0]
    first = step < pl.num_programs(0) // 2
    tok_ref[...] = jnp.where(first, tok_first[...], tok_second[...])
    cot_ref[...] = jnp.where(first, cot_first[...], cot_second[...])

    @pl.when(step == 0)
    def _():
        gout_ref[...] = jnp.zeros_like(gout_ref)
        gin_ref[...] = jnp.zeros_like(gin_ref)
        gback_ref[...] = jnp.zeros_like(gback_ref)
        gvec_ref[...] = jnp.zeros_like(gvec_ref)

    def run(size):
        extra = (slot - head_dim, size)
        sub = lax.broadcasted_iota(jnp.int32, extra, 0)
        lane = lax.broadcasted_iota(jnp.int32, extra, 1)
        one_row = jnp.where(sub == 0, 1.0, 0.0).astype(f32)
        two_rows = jnp.where(sub <= 1, 1.0, 0.0).astype(f32)
        mask_row = jnp.where((sub == 0) & (lane >= length), masked_score, 0.0).astype(f32)

        def group_rows(base, g):
            return slice(base + g * span, base + (g + 1) * span)

        def load(base, g):
            return qkv_ref[group_rows(base, g), :size].astype(f32)

        def place(j, rows):
            parts = []
            if j > 0:
                parts.append(jnp.zeros((slot * j, size), bf16))
            parts.append(rows)
            if j < group - 1:
                parts.append(jnp.zeros((slot * (group - 1 - j), size), bf16))
            return jnp.concatenate(parts, axis=0)

        def pieces(values):
            return [values[head_dim * j : head_dim * (j + 1)] for j in range(group)]

        def padded(values, tail):
            return [jnp.concatenate([p, tail], axis=0).astype(bf16) for p in pieces(values)]

        ahead = 3 if size > 128 else 6

        def forward():
            q, k, v, scores, weights, outs = {}, {}, {}, {}, {}, {}
            for t in range(heads + 2 * ahead):
                if t < heads:
                    g, j = divmod(t, group)
                    if j == 0:
                        q[g] = padded(load(0, g), one_row)
                        k[g] = jnp.concatenate(padded(load(width, g), mask_row), axis=0).T
                        v[g] = padded(load(2 * width, g), one_row)
                    scores[t] = dot(k[g], place(j, q[g][j]), 1, 0)
                h = t - ahead
                if 0 <= h < heads:
                    s = scores.pop(h)
                    peak = jnp.max(s, axis=0, keepdims=True)
                    weights[h] = jnp.exp2((s - peak) * (scale * log2_e)).astype(bf16)
                    probs[h, :size, :size] = weights[h]
                h = t - 2 * ahead
                if 0 <= h < heads:
                    g, j = divmod(h, group)
                    o = dot(v[g][j], weights.pop(h), 1, 0)
                    inverse = 1.0 / o[head_dim : head_dim + 1]
                    linv_s[h, :, :size] = jnp.broadcast_to(inverse, (8, size))
                    outs[h] = o[:head_dim] * inverse
                    if j == group - 1:
                        parts = [outs.pop(h - group + 1 + i) for i in range(group)]
                        ctx_s[group_rows(0, g), :size] = jnp.concatenate(parts, axis=0)

        forward()

        live = (lax.broadcasted_iota(jnp.int32, (size, 1), 0) < length).astype(f32)
        out_bias, gain, shift = vec_ref[4:5], vec_ref[5:6], vec_ref[6:7]
        in_bias, back_bias = vec_ref[7:8], vec_ref[8:9]

        strips = [slice(c, c + 256) for c in range(0, width, 256)]

        def row_mean(parts):
            return sum(jnp.sum(p, axis=1, keepdims=True) for p in parts) * (1.0 / width)

        def join(parts):
            return jnp.concatenate(parts, axis=1)

        d_ffn = cot_ref[:size].astype(f32) * live
        gvec_ref[4] += fold_rows(d_ffn)
        d_ffn = d_ffn.astype(bf16)
        ctx_t = ctx_s[:, :size].astype(bf16)
        ctx = ctx_t.T
        mixed = []
        for c in strips:
            attn = dot(ctx, wout_ref[:, c], 1, 0) + out_bias[:, c]
            mixed.append(tok_ref[:size, c].astype(f32) + live * attn)
        d_act = [dot(d_ffn, wback_ref[c], 1, 1) for c in strips[:1]]
        mean = row_mean(mixed)
        centred = [m - mean for m in mixed]
        factor = lax.rsqrt(row_mean([v * v for v in centred]) + eps)
        unit = [v * factor for v in centred]
        normed = join(
            [(u * gain[:, c] + shift[:, c]).astype(bf16) for u, c in zip(unit, strips)]
        )
        act, d_pre = [], []

        def project(c):
            return dot(normed, win_ref[:, c], 1, 0) + in_bias[:, c]

        ahead_pre = [project(strips[0])]
        for i, c in enumerate(strips):
            if i + 1 < len(strips):
                ahead_pre.append(project(strips[i + 1]))
                d_act.append(dot(d_ffn, wback_ref[strips[i + 1]], 1, 1))
            pre = ahead_pre[i]
            cdf = 0.5 * (1.0 + lax.erf(pre * 0.7071067811865476))
            act.append((pre * cdf).astype(bf16))
            slope = cdf + pre * jnp.exp(-0.5 * pre * pre) * 0.3989422804014327
            low = (d_act[i] * slope).astype(bf16)
            gvec_ref[3, :, c] += fold_rows(low.astype(f32))
            d_pre.append(low)
        act, d_pre = join(act), join(d_pre)
        d_normed = [dot(d_pre, win_ref[c], 1, 1) for c in strips]
        for m, c in zip(mixed, strips):
            branch = dot(act, wback_ref[:, c], 1, 0) + back_bias[:, c]
            mixed_ref[:size, c] = (m + live * branch).astype(bf16)
        act_t, normed_t = act.T, normed.T
        e = []
        for i, c in enumerate(strips):
            gback_ref[:, c] += dot(act_t, d_ffn[:, c], 1, 0)
            gvec_ref[1, :, c] += fold_rows(d_normed[i] * unit[i])
            gvec_ref[2, :, c] += fold_rows(d_normed[i])
            e.append(d_normed[i] * gain[:, c])
        mean = row_mean(e)
        inner = row_mean([v * u for v, u in zip(e, unit)])
        d_attn = []
        for i, c in enumerate(strips):
            gin_ref[:, c] += dot(normed_t, d_pre[:, c], 1, 0)
            d_mixed = cot_ref[:size, c].astype(f32) + factor * (e[i] - mean - unit[i] * inner)
            dmix_ref[:size, c] = d_mixed
            low = (live * d_mixed).astype(bf16)
            gvec_ref[0, :, c] += fold_rows(low.astype(f32))
            d_attn.append(low)
        d_attn = join(d_attn)
        for c in strips:
            dctx_s[c, :size] = dot(wout_ref[c], d_attn, 1, 1).astype(bf16)
        for c in strips:
            gout_ref[:, c] += dot(ctx_t, d_attn[:, c], 1, 0)

        behind = 3 if size > 128 else 6

        def backward():
            q, k, v, d, d_probs, d_scores = {}, {}, {}, {}, {}, {}
            d_q, d_k, d_v = {}, {}, {}
            for t in range(heads + 2 * behind):
                if t < heads:
                    g, j = divmod(t, group)
                    if j == 0:
                        q[g] = padded(load(0, g), one_row)
                        k[g] = padded(load(width, g), one_row)
                        v[g] = jnp.concatenate(padded(load(2 * width, g), two_rows), axis=0).T
                        d_out = pieces(dctx_s[group_rows(0, g), :size].astype(f32))
                        out = pieces(ctx_s[group_rows(0, g), :size])
                        for i in range(group):
                            here = d_out[i] * linv_s[g * group + i, :1, :size]
                            inner = -jnp.sum(here * out[i], axis=0, keepdims=True)
                            high = inner.astype(bf16).astype(f32)
                            blank = jnp.zeros((slot - head_dim - 2, size), f32)
                            tail = [here, high, inner - high, blank]
                            d[g * group + i] = jnp.concatenate(tail, axis=0).astype(bf16)
                    d_probs[t] = dot(v[g], place(j, d[t]), 1, 0)
                h = t - behind
                if 0 <= h < heads:
                    p = probs[h, :size, :size]
                    d_scores[h] = (p.astype(f32) * d_probs.pop(h)).astype(bf16)
                h = t - 2 * behind
                if 0 <= h < heads:
                    g, j = divmod(h, group)
                    ds = d_scores.pop(h)
                    d_v[h] = dot(d.pop(h), probs[h, :size, :size], 1, 1)[:head_dim]
                    d_q[h] = dot(k[g][j], ds, 1, 0)[:head_dim] * scale
                    d_k[h] = dot(q[g][j], ds, 1, 1)[:head_dim] * scale
                    if j == group - 1:
                        for base, parts in ((0, d_q), (width, d_k), (2 * width, d_v)):
                            some = [parts.pop(h - group + 1 + i) for i in range(group)]
                            dqkv_ref[group_rows(base, g), :size] = jnp.concatenate(
                                some, axis=0
                            ).astype(bf16)

        backward()

        if size < block:
            mixed_ref[size:] = tok_ref[size:]
            dmix_ref[size:] = cot_ref[size:].astype(f32)
            dqkv_ref[:, size:] = jnp.zeros((3 * width, block - size), bf16)

    half = block // 2

    @pl.when(length == 0)
    def _():
        mixed_ref[...] = tok_ref[...]
        dmix_ref[...] = cot_ref[...].astype(f32)
        dqkv_ref[...] = jnp.zeros_like(dqkv_ref)

    @pl.when((length > 0) & (length <= half))
    def _():
        run(half)

    @pl.when(length > half)
    def _():
        run(block)

    if packed:

        @pl.when(step == pl.num_programs(0) - 1)
        def _():
            columns = width // 2
            for i in range(DEVICES):
                p = (i % 2) * CHIPS + i // 2
                rows = slice(SHARD * i, SHARD * (i + 1))
                top = jnp.concatenate([gout_ref[rows], gback_ref[rows, :columns]], axis=1)
                bottom = jnp.concatenate([gin_ref[rows], gback_ref[rows, columns:]], axis=1)
                packed_ref[p] = jnp.concatenate([top, bottom], axis=0).astype(bf16)


def middle(lengths, qkv, tokens, cotangent, w_out, w_in, w_back, vectors, packed):
    slots, wide, block = qkv.shape
    rows, width = slots * block, wide // 3
    square = (width, width)
    shared = slots // 2

    def whole(shape):
        return pl.BlockSpec(shape, lambda m: (0,) * len(shape))

    by_rows = pl.BlockSpec((block, width), lambda m: (m, 0))
    if packed:
        first = pl.BlockSpec((block, width), lambda m: (2 * jnp.minimum(m, shared - 1), 0))
        second = pl.BlockSpec((block, width), lambda m: (jnp.maximum(m - shared, 0), 0))
    else:
        first = pl.BlockSpec((block, width), lambda m: (jnp.minimum(m, shared - 1), 0))
        second = pl.BlockSpec((block, width), lambda m: (jnp.maximum(m, shared), 0))
    out_specs = [
        by_rows,
        by_rows,
        pl.BlockSpec((3 * width, block), lambda m: (0, m)),
        whole((5, 8, width)),
    ]
    out_shape = [
        jax.ShapeDtypeStruct((rows, width), bf16),
        jax.ShapeDtypeStruct((rows, width), f32),
        jax.ShapeDtypeStruct((3 * width, rows), bf16),
        jax.ShapeDtypeStruct((5, 8, width), f32),
    ]
    scratch = [
        pltpu.VMEM((HEADS, block, block), bf16),
        pltpu.VMEM((width, block), f32),
        pltpu.VMEM((HEADS, 8, block), f32),
        pltpu.VMEM((width, block), bf16),
        pltpu.VMEM((block, width), bf16),
        pltpu.VMEM((block, width), bf16),
    ]
    if packed:
        shape = (DEVICES, 2 * SHARD, width + width // 2)
        out_specs.append(whole(shape))
        out_shape.append(jax.ShapeDtypeStruct(shape, bf16))
        scratch = [pltpu.VMEM(square, f32)] * 3 + scratch
    else:
        out_specs += [whole(square)] * 3
        out_shape += [jax.ShapeDtypeStruct(square, f32)] * 3
    return pl.pallas_call(
        functools.partial(middle_kernel, packed, width // HEADS),
        grid=(slots,),
        in_specs=[
            pl.BlockSpec(memory_space=pltpu.SMEM),
            pl.BlockSpec((None, 3 * width, block), lambda m: (m, 0, 0)),
            first,
            second,
            first,
            second,
            whole(square),
            whole(square),
            whole(square),
            whole((16, width)),
        ],
        out_specs=out_specs,
        scratch_shapes=scratch,
        out_shape=out_shape,
        compiler_params=pltpu.CompilerParams(vmem_limit_bytes=58 * MIB),
    )(lengths, qkv, *tokens, *cotangent, w_out, w_in, w_back, vectors)


def scatter_kernel(
    sr_hbm,
    dqkv_hbm,
    unit_hbm,
    fq_hbm,
    tok_hbm,
    odd_hbm,
    dmix_hbm,
    mixed_hbm,
    vec_ref,
    gvec_ref,
    grad_hbm,
    grad_out,
    mixed_out,
    gq_ref,
    gr_ref,
    sq,
    sr,
    rq_sib,
    rr_sib,
    rq,
    rr,
    dqkv,
    unit_t,
    fq,
    tok,
    dmix,
    grad,
    mixed,
    gain_wide,
    shift_wide,
    small_wide,
    sums,
    result,
    send_sem,
    recv_sem,
    swap_send,
    swap_recv,
    copy_sem,
):
    at = Place()
    at.greet()
    rows, width = tok.shape
    wide = 3 * width
    half_q = wide // 2
    slots = 8
    block = rows // slots
    mine, theirs = at.c * CHIPS, (1 - at.c) * CHIPS
    own = at.block(at.c, at.z, at.y, at.x)
    level_rows = 8 * SHARD

    def local(src, dst, i):
        copy = pltpu.make_async_copy(src, dst, copy_sem.at[i])
        copy.start()
        return copy

    sr_in = local(sr_hbm, sr, 0)
    unit_in = local(unit_hbm, unit_t, 1)
    dqkv_in = local(dqkv_hbm, dqkv, 2)
    fq_in = local(fq_hbm, fq, 3)
    shared = slots // 2

    def rows_of(i, count=1):
        return pl.ds(i * block, count * block)

    mixed_in = local(mixed_hbm.at[rows_of(shared, shared)], mixed, 4)
    late = [local(dmix_hbm, dmix, 5), local(odd_hbm, tok.at[rows_of(shared, shared)], 6)]
    for i in range(shared):
        late.append(local(tok_hbm.at[rows_of(2 * i)], tok.at[rows_of(i)], 7 + i))

    def swap_copy(src, dst, i):
        return pltpu.make_async_remote_copy(
            src_ref=src,
            dst_ref=dst,
            send_sem=swap_send.at[i],
            recv_sem=swap_recv.at[i],
            device_id=(at.sib,),
            device_id_type=MESH,
        )

    slabs = (
        (sq, rq_sib, rq, 0, 640),
        (sq, rq_sib, rq, 640, 640),
        (sr, rr_sib, rr, 0, 1152),
    )

    def cut(ref, k, first, count):
        return ref.at[pl.ds(first, count), :, pl.ds(slabs[k][3], slabs[k][4])]

    def piece(ref, k, p):
        _, _, _, column, columns = slabs[k]
        return ref[p, :, column : column + columns].astype(f32)

    def put(k, p, value):
        slab, _, _, column, columns = slabs[k]
        slab[p, :, column : column + columns] = value.astype(bf16)

    def remote(k, src, dst, target, sem):
        return pltpu.make_async_remote_copy(
            src_ref=src,
            dst_ref=dst,
            send_sem=send_sem.at[k],
            recv_sem=recv_sem.at[k, sem],
            device_id=(target,),
            device_id_type=MESH,
        )

    def x_type(j):
        return at.block(at.c, j, at.y, 1 - at.x)

    def y_type(j):
        return at.block(at.c, j, 1 - at.y, at.x)

    def corner_type(j):
        return at.block(at.c, j, 1 - at.y, 1 - at.x)

    def column_type(j):
        return at.block(at.c, j, at.y, at.x)

    def sib_copy(k, j):
        src = cut(slabs[k][0], k, theirs + 4 * j, 4)
        return remote(k, src, cut(slabs[k][1], k, 4 * j, 4), at.sib, j)

    def sib_send(k, j):
        sib_copy(k, j).start()

    def step_copy(k, src, slot, target):
        src = cut(slabs[k][0], k, src, 1)
        return remote(k, src, cut(slabs[k][2], k, slot, 1), target, PLANES + slot)

    def x_send(k, j):
        step_copy(k, x_type(j), 4 + j, at.xn).start()

    def y_send(k, j):
        step_copy(k, y_type(j), 8 + j, at.yn).start()

    def sib_add(k, j):
        sib_copy(k, j).wait_recv()

        def body(i, carry):
            p = mine + 4 * j + i
            put(k, p, piece(slabs[k][0], k, p) + piece(slabs[k][1], k, 4 * j + i))
            return carry

        lax.fori_loop(0, 4, body, 0)
        step_copy(k, corner_type(j), j, at.yn if j % 2 == 0 else at.xn).start()
        (y_send if j % 2 == 0 else x_send)(k, j)

    def corner_add(k, j):
        step_copy(k, own, j, at.sib).wait_recv()
        p = x_type(j) if j % 2 == 0 else y_type(j)
        put(k, p, piece(slabs[k][0], k, p) + piece(slabs[k][2], k, j))
        (x_send if j % 2 == 0 else y_send)(k, j)

    def plane_add(k, j):
        p = column_type(j)
        step_copy(k, own, 4 + j, at.sib).wait_recv()
        step_copy(k, own, 8 + j, at.sib).wait_recv()
        received = piece(slabs[k][2], k, 4 + j) + piece(slabs[k][2], k, 8 + j)
        put(k, p, piece(slabs[k][0], k, p) + received)

        @pl.when(at.z != j)
        def _():
            step_copy(k, p, 12 + at.z, at.me + 8 * (j - at.z)).start()

    def land(k):
        total = gq_ref if slabs[k][0] is sq else gr_ref
        columns = slice(slabs[k][3], slabs[k][3] + slabs[k][4])
        total[:, columns] = piece(slabs[k][0], k, own)
        for j in range(PLANES):

            @pl.when(at.z != j)
            def _():
                step_copy(k, own, 12 + j, at.sib).wait_recv()
                total[:, columns] += piece(slabs[k][2], k, 12 + j)

    def prepare():
        gain_wide[...] = jnp.broadcast_to(vec_ref[0:1], (128, width)).T
        shift_wide[...] = jnp.broadcast_to(vec_ref[1:2], (128, width)).T
        ones = jnp.ones((16, rows), bf16)
        for part in range(3):
            columns = slice(part * width, (part + 1) * width)
            sums[:, columns] = dot(ones, dqkv[columns], 1, 1)[:8]
        lines = [jnp.zeros((2, width), f32), sums[0:1, :width], sums[0:1, 2 * width :]]
        lines += [jnp.sum(gvec_ref[i], axis=0, keepdims=True) for i in range(5)]
        lines.append(jnp.zeros((128 - 9, width), f32))
        small_wide[...] = jnp.concatenate(lines, axis=0).T

    def weight_grad(j, part):
        lines = pl.ds(j * level_rows, level_rows)
        columns = slice(part * width, (part + 1) * width)
        product = dot(unit_t[lines], dqkv[columns], 1, 1)
        weight = fq[lines, columns].astype(f32)
        line = sums[0:1, columns]
        gain_sum = jnp.sum(weight * product, axis=1, keepdims=True)
        shift_sum = jnp.sum(weight * line, axis=1, keepdims=True)
        lane = lax.broadcasted_iota(jnp.int32, (level_rows, 128), 1)
        small_wide[lines] += jnp.where(
            lane == 0, gain_sum, jnp.where(lane == 1, shift_sum, 0.0)
        )
        gain = jnp.concatenate([gain_wide[lines]] * (width // 128), axis=1)
        shift = jnp.concatenate([shift_wide[lines]] * (width // 128), axis=1)
        result[:, columns] = gain * product + shift * line
        if part < 2:
            return
        small = small_wide[lines]
        blank = jnp.zeros((SHARD, 128), f32)
        for i in range(8):
            p = (i % 2) * CHIPS + 4 * j + i // 2
            some = slice(SHARD * i, SHARD * (i + 1))
            top = jnp.concatenate([result[some, :half_q], small[some]], axis=1)
            bottom = jnp.concatenate([result[some, half_q:], blank], axis=1)
            sq[p] = jnp.concatenate([top, bottom], axis=0).astype(bf16)

    grads = []

    def input_grad(m):
        some = slice(m * block, (m + 1) * block)
        d_normed = dot(fq[...], dqkv[:, some], 1, 0).T
        unit, factor = normalize(tok[some].astype(f32))
        share = norm_backward(d_normed, vec_ref[0:1], unit, factor)
        grad[some] = (dmix[some] + share).astype(bf16)
        if m < shared:
            grads.append(local(grad.at[rows_of(m)], grad_hbm.at[rows_of(m)], 7 + shared + m))
        else:
            swap_copy(grad.at[rows_of(m)], grad_out.at[rows_of(m - shared)], 0).start()

    sr_in.wait()
    at.await_all()
    sib_send(2, 0)
    sib_send(2, 1)
    sib_send(2, 2)
    sib_add(2, 0)
    sib_send(2, 3)
    sib_add(2, 1)
    sib_add(2, 2)
    sib_add(2, 3)
    unit_in.wait()
    dqkv_in.wait()
    fq_in.wait()
    prepare()
    weight_grad(0, 0)
    weight_grad(0, 1)
    weight_grad(0, 2)
    weight_grad(3, 0)
    corner_add(2, 1)
    sib_send(1, 0)
    corner_add(2, 0)
    corner_add(2, 3)
    weight_grad(3, 1)
    sib_send(0, 0)
    corner_add(2, 2)
    weight_grad(3, 2)
    sib_send(1, 3)
    sib_send(0, 3)
    sib_add(0, 0)
    sib_add(1, 0)
    weight_grad(2, 0)
    plane_add(2, 1)
    plane_add(2, 0)
    sib_add(1, 3)
    weight_grad(2, 1)
    sib_add(0, 3)
    plane_add(2, 3)
    weight_grad(2, 2)
    sib_send(1, 2)
    weight_grad(1, 0)
    sib_add(1, 2)
    corner_add(0, 0)
    plane_add(2, 2)
    sib_send(0, 2)
    corner_add(1, 0)
    weight_grad(1, 1)
    corner_add(0, 3)
    weight_grad(1, 2)
    sib_send(1, 1)
    sib_send(0, 1)
    corner_add(1, 2)
    plane_add(0, 0)
    mixed_in.wait()
    swap_copy(mixed, mixed_out, 1).start()
    for copy in late:
        copy.wait()
    sib_add(0, 2)
    corner_add(1, 3)
    sib_add(1, 1)
    sib_add(0, 1)
    plane_add(0, 3)
    plane_add(1, 0)
    input_grad(0)
    plane_add(1, 2)
    corner_add(0, 2)
    corner_add(1, 1)
    input_grad(1)
    input_grad(2)
    corner_add(0, 1)
    plane_add(1, 3)
    plane_add(1, 1)
    input_grad(3)
    input_grad(4)
    plane_add(0, 2)
    plane_add(0, 1)
    input_grad(5)
    input_grad(6)
    land(1)
    input_grad(7)
    land(2)
    land(0)
    for k in range(len(slabs)):
        every = cut(slabs[k][0], k, 0, DEVICES - 1)
        remote(k, every, every, at.sib, 0).wait_send()
    for copy in grads:
        copy.wait()
    swap_copy(grad.at[rows_of(shared, shared)], grad_out, 0).wait()
    swap_copy(mixed, mixed_out, 1).wait()


def scatter(packed, dqkv, unit_t, full_qkv, tokens, odd_tokens, d_mixed, mixed, vectors, sums):
    rows, width = tokens.shape
    wide = 3 * width
    vmem = pl.BlockSpec(memory_space=pltpu.VMEM)
    anywhere = pl.BlockSpec(memory_space=pl.ANY)
    tall = 2 * SHARD
    widths = (wide // 2 + 128, wide // 2)
    return pl.pallas_call(
        scatter_kernel,
        out_shape=[jax.ShapeDtypeStruct((rows // 2, width), bf16)] * 3
        + [jax.ShapeDtypeStruct((tall, w), f32) for w in widths],
        in_specs=[anywhere] * 8 + [vmem] * 2,
        out_specs=[anywhere] * 3 + [vmem] * 2,
        scratch_shapes=[pltpu.VMEM((DEVICES, tall, w), bf16) for w in widths]
        + [pltpu.VMEM((CHIPS, tall, w), bf16) for w in widths]
        + [pltpu.VMEM((4 * PLANES, tall, w), bf16) for w in widths]
        + [
            pltpu.VMEM((wide, rows), bf16),
            pltpu.VMEM((width, rows), bf16),
            pltpu.VMEM((width, wide), bf16),
            pltpu.VMEM((rows, width), bf16),
            pltpu.VMEM((rows, width), f32),
            pltpu.VMEM((rows, width), bf16),
            pltpu.VMEM((rows // 2, width), bf16),
            pltpu.VMEM((width, 128), f32),
            pltpu.VMEM((width, 128), f32),
            pltpu.VMEM((width, 128), f32),
            pltpu.VMEM((8, wide), f32),
            pltpu.VMEM((8 * SHARD, wide), f32),
            pltpu.SemaphoreType.DMA((3,)),
            pltpu.SemaphoreType.DMA((3, 5 * PLANES)),
            pltpu.SemaphoreType.DMA((2,)),
            pltpu.SemaphoreType.DMA((2,)),
            pltpu.SemaphoreType.DMA((15,)),
        ],
        compiler_params=pltpu.CompilerParams(
            collective_id=1, has_side_effects=True, vmem_limit_bytes=60 * MIB
        ),
    )(packed, dqkv, unit_t, full_qkv, tokens, odd_tokens, d_mixed, mixed, vectors, sums)


def finish_kernel(
    mixed_even, mixed_odd, grad_even, grad_odd, q_ref, r_ref, mixed, grad, g_qkv, g_out, g_in, g_back, *lines
):
    block = mixed_even.shape[0]
    mixed[:block] = mixed_even[...]
    mixed[block:] = mixed_odd[...]
    grad[:block] = grad_even[...]
    grad[block:] = grad_odd[...]

    @pl.when(pl.program_id(0) == 0)
    def _():
        width = g_out.shape[1]
        half_q = 3 * width // 2
        half = width // 2
        g_qkv[:, :half_q] = q_ref[:SHARD, :half_q]
        g_qkv[:, half_q:] = q_ref[SHARD:, :half_q]
        g_out[...] = r_ref[:SHARD, :width]
        g_in[...] = r_ref[SHARD:, :width]
        g_back[:, :half] = r_ref[:SHARD, width:]
        g_back[:, half:] = r_ref[SHARD:, width:]
        small = q_ref[:SHARD, half_q:].T
        for i, line in enumerate(lines):
            line[...] = small[i, :SHARD]


def finish(mixed, mixed_odd, grad, grad_odd, q_part, r_part, slots):
    rows, width = mixed.shape
    block = rows // slots
    single = pl.BlockSpec((block, width), lambda i: (i, 0))
    double = pl.BlockSpec((2 * block, width), lambda i: (i, 0))

    def whole(shape):
        return pl.BlockSpec(shape, lambda i: (0,) * len(shape))

    shapes = [(SHARD, 3 * width)] + [(SHARD, width)] * 3 + [(SHARD,)] * 9
    return pl.pallas_call(
        finish_kernel,
        grid=(slots // 2,),
        out_shape=[jax.ShapeDtypeStruct((rows, width), bf16)] * 2
        + [jax.ShapeDtypeStruct(s, f32) for s in shapes],
        in_specs=[single] * 4 + [whole(q_part.shape), whole(r_part.shape)],
        out_specs=[double] * 2 + [whole(s) for s in shapes],
    )(mixed, mixed_odd, grad, grad_odd, q_part, r_part)


def on_one_plan(tokens, mol_len, cotangent, vectors, w_qkv, w_out, w_in, w_back):
    slots = mol_len.shape[0]
    (
        qkv,
        unit_t,
        full_qkv,
        full_out,
        full_in,
        full_back,
        odd_tokens,
        odd_cotangent,
        lines,
        lengths,
    ) = gather_and_project(mol_len, vectors, w_qkv, w_out, w_in, w_back, tokens, cotangent)
    mixed, d_mixed, dqkv, sums, packed = middle(
        lengths,
        qkv,
        (tokens, odd_tokens),
        (cotangent, odd_cotangent),
        full_out,
        full_in,
        full_back,
        lines,
        True,
    )
    grad, grad_odd, mixed_odd, q_part, r_part = scatter(
        packed, dqkv, unit_t, full_qkv, tokens, odd_tokens, d_mixed, mixed, lines, sums
    )
    mixed_out, token_grad, g_qkv, g_out, g_in, g_back, *small = finish(
        mixed, mixed_odd, grad, grad_odd, q_part, r_part, slots
    )
    return mixed_out, token_grad, small, g_qkv, g_out, g_in, g_back


def on_any_plan(tokens, mol_len, cotangent, vectors, w_qkv, w_out, w_in, w_back):
    slots = mol_len.shape[0]
    rows, width = tokens.shape

    def gather(array, axis):
        return lax.all_gather(array, "fsdp", axis=axis, tiled=True)

    lines = gather(jnp.stack(vectors), 1).astype(f32)
    lines = jnp.pad(lines, ((0, 16 - len(vectors)), (0, 0)))
    full_qkv, full_out, full_in, full_back = (
        gather(w, 0) for w in (w_qkv, w_out, w_in, w_back)
    )
    unit, factor = normalize(tokens.astype(f32))
    normed = (unit * lines[0] + lines[1]).astype(bf16)
    qkv = jnp.dot(normed, full_qkv, preferred_element_type=f32)
    qkv = (qkv + jnp.concatenate([lines[2], jnp.zeros_like(lines[2]), lines[3]])).astype(bf16)
    qkv = qkv.reshape(slots, rows // slots, 3 * width).transpose(0, 2, 1)
    mixed_out, d_mixed, dqkv, sums, g_out, g_in, g_back = middle(
        jnp.broadcast_to(mol_len[:, None], (slots, 128)),
        qkv,
        (tokens, tokens),
        (cotangent, cotangent),
        full_out,
        full_in,
        full_back,
        lines,
        False,
    )
    g_qkv = jnp.einsum("rf,dr->fd", normed, dqkv, preferred_element_type=f32)
    d_normed = jnp.einsum("dr,fd->rf", dqkv, full_qkv, preferred_element_type=f32)
    totals = jnp.sum(dqkv.astype(f32), axis=1)
    small = [jnp.sum(d_normed * unit, axis=0), jnp.sum(d_normed, axis=0)]
    small += [totals[:width], totals[2 * width :]]
    small += [jnp.sum(sums[i], axis=0) for i in range(5)]
    share = norm_backward(d_normed, lines[0], unit, factor)
    token_grad = (d_mixed + share).astype(bf16)

    def scatter_sum(array, axis):
        return lax.psum_scatter(array, "fsdp", scatter_dimension=axis, tiled=True)

    small = scatter_sum(jnp.stack(small), 1)
    return (
        mixed_out,
        token_grad,
        [small[i] for i in range(9)],
        *(scatter_sum(g, 0) for g in (g_qkv, g_out, g_in, g_back)),
    )


def per_device(
    devices,
    tokens,
    mol_len,
    cotangent,
    ln1_gain,
    ln1_bias,
    w_qkv,
    q_bias,
    v_bias,
    w_out,
    out_bias,
    ln2_gain,
    ln2_bias,
    w_in,
    in_bias,
    w_back,
    back_bias,
):
    vectors = [
        ln1_gain,
        ln1_bias,
        q_bias,
        v_bias,
        out_bias,
        ln2_gain,
        ln2_bias,
        in_bias,
        back_bias,
    ]
    known = devices == DEVICES and w_qkv.shape[0] == SHARD
    plan = on_one_plan if known else on_any_plan
    mixed_out, token_grad, small, g_qkv, g_out, g_in, g_back = plan(
        tokens, mol_len, cotangent, vectors, w_qkv, w_out, w_in, w_back
    )
    return (
        mixed_out,
        token_grad,
        small[0],
        small[1],
        g_qkv,
        small[2],
        small[3],
        g_out,
        small[4],
        small[5],
        small[6],
        g_in,
        small[7],
        g_back,
        small[8],
    )


def solution(mesh):
    line, matrix = P("fsdp"), P("fsdp", None)
    return jax.shard_map(
        functools.partial(per_device, mesh.shape["fsdp"]),
        mesh=mesh,
        in_specs=(
            matrix,
            line,
            matrix,
            line,
            line,
            matrix,
            line,
            line,
            matrix,
            line,
            line,
            line,
            matrix,
            line,
            matrix,
            line,
        ),
        out_specs=(
            matrix,
            matrix,
            line,
            line,
            matrix,
            line,
            line,
            matrix,
            line,
            line,
            line,
            matrix,
            line,
            matrix,
            line,
        ),
        check_vma=False,
    )
```

```python
import functools

import jax
import jax.numpy as jnp
from jax import lax
from jax.experimental import pallas as pl
from jax.experimental.pallas import tpu as pltpu
from jax.sharding import PartitionSpec as P

HEADS = 32

bf16 = jnp.bfloat16
f32 = jnp.float32
eps = 1e-05
masked_score = -1e30
log2_e = 1.4426950408889634
MESH = pl.DeviceIdType.MESH
MIB = 1 << 20

PLANES = 4
CHIPS = 4 * PLANES
DEVICES = 2 * CHIPS
SHARD = 24
VECTORS = 9
COPIES = 8


def dot(left, right, left_dim, right_dim):
    return lax.dot_general(
        left, right, (((left_dim,), (right_dim,)), ((), ())), preferred_element_type=f32
    )


def normalize(values):
    centred = values - jnp.mean(values, axis=-1, keepdims=True)
    factor = lax.rsqrt(jnp.mean(centred * centred, axis=-1, keepdims=True) + eps)
    return centred * factor, factor


def norm_backward(d_normed, gain, unit, factor):
    e = d_normed * gain
    inner = jnp.mean(e * unit, axis=-1, keepdims=True)
    return factor * (e - jnp.mean(e, axis=-1, keepdims=True) - unit * inner)


def fold_rows(values):
    rows, columns = values.shape
    return jnp.sum(values.reshape(rows // 8, 8, columns), axis=0)


class Place:
    def __init__(self):
        me = lax.axis_index("fsdp")
        self.me = me
        self.c = lax.rem(me, 2)
        self.x = lax.rem(me // 2, 2)
        self.y = lax.rem(me // 4, 2)
        self.z = me // 8
        self.sib = me + 1 - 2 * self.c
        self.xn = me + 2 - 4 * self.x
        self.yn = me + 4 - 8 * self.y

    def block(self, c, z, y, x):
        return ((c * PLANES + z) * 2 + y) * 2 + x

    def greet(self):
        sem = pltpu.get_barrier_semaphore()

        def signal(device):
            pl.semaphore_signal(sem, inc=1, device_id=(device,), device_id_type=MESH)

        for device in (self.sib, self.xn, self.yn):
            signal(device)
        for distance in range(1, PLANES):
            signal(lax.rem(self.me + 8 * distance, DEVICES))

    def await_all(self):
        pl.semaphore_wait(pltpu.get_barrier_semaphore(), 2 + PLANES)


def gather_kernel(
    len_ref,
    *refs,
):
    lines, refs = refs[:VECTORS], refs[VECTORS:]
    gather_body(len_ref, lines, *refs)


def gather_body(
    len_ref,
    lines,
    wq_ref,
    wo_ref,
    wi_ref,
    wb_ref,
    tok_ref,
    cot_hbm,
    qkv_hbm,
    unit_hbm,
    fq_hbm,
    fo_hbm,
    fi_hbm,
    fb_hbm,
    tok_hbm,
    cot_out,
    vec_ref,
    work_ref,
    gq,
    gr,
    fq,
    fo,
    fi,
    fb,
    fq_t,
    unit,
    unit_t,
    qkv,
    bias,
    tok_odd,
    cot_odd,
    len_send,
    len_recv,
    send_sem,
    recv_sem,
    swap_send,
    swap_recv,
    copy_sem,
):
    at = Place()
    at.greet()
    width = tok_ref.shape[1]
    slots, _, block = qkv.shape
    shared = slots // 2
    half_q = 3 * width // 2
    half = width // 2
    own = at.block(at.c, at.z, at.y, at.x)
    mine, theirs = at.c * CHIPS, (1 - at.c) * CHIPS
    slabs = ((gq, 0, 384), (gq, 384, 384), (gq, 768, 512), (gr, 0, 640), (gr, 640, 512))

    small = [line[...].astype(f32).reshape(1, SHARD) for line in lines]
    small = jnp.concatenate(small + [jnp.zeros((2 * SHARD - VECTORS, SHARD), f32)], axis=0)
    small = jnp.concatenate([small, jnp.zeros((2 * SHARD, 128 - SHARD), f32)], axis=1).astype(bf16)
    gq[own] = jnp.concatenate(
        [
            jnp.concatenate([wq_ref[:, :half_q], wq_ref[:, half_q:]], axis=0),
            small,
        ],
        axis=1,
    )
    gr[own] = jnp.concatenate(
        [
            jnp.concatenate([wo_ref[...], wi_ref[...]], axis=0),
            jnp.concatenate([wb_ref[:, :half], wb_ref[:, half:]], axis=0),
        ],
        axis=1,
    )

    def view(k, first, count):
        slab, column, columns = slabs[k]
        return slab.at[pl.ds(first, count), :, pl.ds(column, columns)]

    def remote(k, first, target, sem, count=1):
        return pltpu.make_async_remote_copy(
            src_ref=view(k, first, count),
            dst_ref=view(k, first, count),
            send_sem=send_sem.at[k],
            recv_sem=recv_sem.at[k, sem],
            device_id=(target,),
            device_id_type=MESH,
        )

    def send(k, b, target):
        remote(k, b, target, lax.rem(b, CHIPS)).start()

    def to_sib(k, b):
        remote(k, b, at.sib, CHIPS).start()

    def arrived(k, b):
        remote(k, b, at.sib, lax.rem(b, CHIPS)).wait_recv()

    def at_level(shift, body):
        level = at.z + shift
        if shift == 0:
            body(level)
        else:
            pl.when((level >= 0) & (level <= PLANES - 1))(lambda: body(level))

    def both(s):
        return (0,) if s == 0 else (-s, s)

    def own_plane(k):
        send(k, own, at.xn)
        send(k, own, at.yn)

    def own_column(k):
        for s in range(1, PLANES):
            for shift in both(s):
                at_level(shift, lambda level, shift=shift: send(k, own, at.me + 8 * shift))
        to_sib(k, own)

    def column(k, s):
        def body(level):
            b = at.block(at.c, level, at.y, at.x)
            arrived(k, b)
            send(k, b, at.xn)
            send(k, b, at.yn)
            to_sib(k, b)

        for shift in both(s):
            at_level(shift, body)

    def plane(k, s):
        def body(level):
            even = lax.rem(level, 2) == 0
            b = at.block(at.c, level, at.y, 1 - at.x)
            arrived(k, b)
            pl.when(even)(lambda: send(k, b, at.yn))
            to_sib(k, b)
            d = at.block(at.c, level, 1 - at.y, at.x)
            arrived(k, d)
            pl.when(jnp.logical_not(even))(lambda: send(k, d, at.xn))
            to_sib(k, d)

        for shift in both(s):
            at_level(shift, body)

    def corner(k):
        for j in range(PLANES):
            b = at.block(at.c, j, 1 - at.y, 1 - at.x)
            arrived(k, b)
            to_sib(k, b)

    def others(k):
        remote(k, theirs, at.sib, CHIPS, CHIPS).wait_recv()

    def rows_of(i):
        return pl.ds(i * block, block)

    cot_in = [
        pltpu.make_async_copy(
            cot_hbm.at[rows_of(2 * i + 1)], cot_odd.at[rows_of(i)], swap_recv.at[6 + i]
        )
        for i in range(shared)
    ]

    def swap_copy(src, dst, send, recv):
        return pltpu.make_async_remote_copy(
            src_ref=src,
            dst_ref=dst,
            send_sem=swap_send.at[send],
            recv_sem=swap_recv.at[recv],
            device_id=(at.sib,),
            device_id_type=MESH,
        )

    def tok_copy(i):
        return swap_copy(tok_ref.at[rows_of(2 * i + 1)], tok_odd.at[rows_of(i)], 0, i)

    def swap_start():
        swap_copy(len_send, len_recv, 2, 5).start()
        for i in range(shared):
            tok_copy(i).start()
        for i in range(shared):
            cot_in[i].wait()
            swap_copy(cot_odd.at[rows_of(i)], cot_out.at[rows_of(i)], 1, 4).start()

    def swap_end():
        swap_copy(len_send, len_recv, 2, 5).wait()
        swap_copy(tok_odd, tok_odd, 0, 0).wait_send()
        swap_copy(cot_odd, cot_out, 1, 4).wait()
        place = lax.broadcasted_iota(jnp.int32, (shared, 128), 0)
        own_lengths = jnp.zeros((shared, 128), jnp.int32)
        odd_lengths = jnp.zeros((shared, 128), jnp.int32)
        for i in range(shared):
            own_lengths = jnp.where(place == i, len_send[2 * i : 2 * i + 1], own_lengths)
            odd_lengths = jnp.where(place == i, len_recv[2 * i + 1 : 2 * i + 2], odd_lengths)
        work_ref[:shared] = own_lengths
        work_ref[shared:] = odd_lengths

    for i in range(slots):
        len_send[i : i + 1] = jnp.full((1, 128), len_ref[i], jnp.int32)
    for copy in cot_in:
        copy.start()

    def norm_step(m):
        rows = rows_of(m)
        if m < shared:
            here = tok_ref[rows_of(2 * m)]
        else:
            tok_copy(m - shared).wait_recv()
            here = tok_odd[rows_of(m - shared)]
        size = block // 2
        for i in range(2):
            some = pl.ds(m * block + i * size, size)
            values, _ = normalize(here[i * size : (i + 1) * size].astype(f32))
            unit[some] = values
            unit_t[:, some] = values.astype(bf16).T

    def strip(i):
        return pl.ds(pl.multiple_of(i * 2 * SHARD, 2 * SHARD), 2 * SHARD)

    def stack(first, second):
        return jnp.concatenate([first, second], axis=0).astype(bf16)

    def build_q():
        def body(i, carry):
            first = gq[i].astype(f32)
            second = gq[CHIPS + i].astype(f32)
            fq[strip(i), :half_q] = stack(first[:SHARD, :half_q], second[:SHARD, :half_q])
            fq[strip(i), half_q:] = stack(first[SHARD:, :half_q], second[SHARD:, :half_q])
            return carry

        lax.fori_loop(0, CHIPS, body, 0)
        out(fq, fq_hbm)

    def build_r():
        def body(i, carry):
            first = gr[i].astype(f32)
            second = gr[CHIPS + i].astype(f32)
            fo[strip(i)] = stack(first[:SHARD, :width], second[:SHARD, :width])
            fi[strip(i)] = stack(first[SHARD:, :width], second[SHARD:, :width])
            fb[strip(i), :half] = stack(first[:SHARD, width:], second[:SHARD, width:])
            fb[strip(i), half:] = stack(first[SHARD:, width:], second[SHARD:, width:])
            return carry

        lax.fori_loop(0, CHIPS, body, 0)
        out(fo, fo_hbm)
        out(fi, fi_hbm)
        out(fb, fb_hbm)

    copies = []

    def out(src, dst):
        copy = pltpu.make_async_copy(src, dst, copy_sem.at[len(copies)])
        copy.start()
        copies.append(copy)

    def turn(part):
        columns = slice(part * width, (part + 1) * width)
        fq_t[columns] = fq[:, columns].T

    def spread_vectors():
        column_at = lax.broadcasted_iota(jnp.int32, (128, width), 1)
        entry = lax.broadcasted_iota(jnp.int32, (128, width), 0)
        spread = jnp.where(lax.rem(column_at, SHARD) == entry, 1.0, 0.0).astype(bf16)
        stacked = jnp.concatenate([gq[p, :16, half_q:] for p in range(DEVICES)], axis=0)
        wide = dot(stacked, spread, 1, 0)
        total = jnp.zeros((16, width), f32)
        column_at = lax.broadcasted_iota(jnp.int32, (16, width), 1)
        for p in range(DEVICES):
            first = SHARD * ((p % CHIPS) * 2 + p // CHIPS)
            here = (column_at >= first) & (column_at < first + SHARD)
            total = total + jnp.where(here, wide[16 * p : 16 * p + 16], 0.0)
        vec_ref[...] = total
        bias[:width] = jnp.broadcast_to(total[2:3], (128, width)).T
        bias[width : 2 * width] = jnp.zeros((width, 128), f32)
        bias[2 * width :] = jnp.broadcast_to(total[3:4], (128, width)).T

    def qkv_copy(m):
        return pltpu.make_async_copy(qkv.at[m], qkv_hbm.at[m], copy_sem.at[COPIES + m])

    def qkv_part(m, part):
        here = unit[pl.ds(pl.multiple_of(m * block, block), block)]
        normed = (here * vec_ref[0:1] + vec_ref[1:2]).astype(bf16)
        lines = pl.ds(pl.multiple_of(part * width, width), width)
        result = dot(fq_t[lines], normed, 1, 1)
        added = jnp.concatenate([bias[lines]] * (block // 128), axis=1)
        qkv[m, lines] = (result + added).astype(bf16)
        pl.when(part == 2)(lambda: qkv_copy(m).start())

    norm_step(0)
    norm_step(1)
    at.await_all()
    swap_start()
    own_column(0)
    own_column(1)
    own_plane(1)
    own_plane(2)
    norm_step(2)
    own_plane(4)
    own_plane(3)
    own_column(2)
    own_plane(0)
    column(0, 3)
    column(0, 2)
    plane(1, 0)
    column(0, 1)
    plane(0, 3)
    plane(0, 0)
    own_column(3)
    column(1, 3)
    own_column(4)
    column(1, 1)
    norm_step(3)
    norm_step(4)
    column(1, 2)
    plane(2, 0)
    plane(0, 1)
    plane(1, 3)
    norm_step(5)
    norm_step(6)
    column(2, 3)
    column(2, 1)
    column(2, 2)
    plane(1, 2)
    plane(1, 1)
    norm_step(7)
    plane(0, 2)
    plane(2, 1)
    plane(2, 3)
    plane(2, 2)
    corner(1)
    column(3, 3)
    corner(0)
    plane(3, 0)
    corner(2)
    column(3, 2)
    others(1)
    others(0)
    plane(4, 0)
    column(3, 1)
    others(2)
    column(4, 3)
    build_q()
    plane(3, 3)
    column(4, 1)
    turn(0)
    turn(1)
    turn(2)
    spread_vectors()
    column(4, 2)

    def beside_qkv_6():
        plane(3, 2)

    def beside_qkv_7():
        plane(3, 1)

    def beside_qkv_8():
        plane(4, 1)

    def beside_qkv_11():
        plane(4, 2)
        plane(4, 3)

    def beside_qkv_14():
        corner(3)

    def beside_qkv_19():
        corner(4)

    def beside_qkv_22():
        others(4)
        others(3)


    def beside_qkv_step(i, carry):
        qkv_part(i // 3, lax.rem(i, 3))
        pl.when(i == 6)(beside_qkv_6)
        pl.when(i == 7)(beside_qkv_7)
        pl.when(i == 8)(beside_qkv_8)
        pl.when(i == 11)(beside_qkv_11)
        pl.when(i == 14)(beside_qkv_14)
        pl.when(i == 19)(beside_qkv_19)
        pl.when(i == 22)(beside_qkv_22)
        return carry

    lax.fori_loop(0, 24, beside_qkv_step, 0)
    build_r()
    out(unit_t, unit_hbm)
    out(tok_odd, tok_hbm)
    swap_end()
    for k in range(len(slabs)):
        remote(k, 0, at.sib, 0, DEVICES - 1).wait_send()
    for copy in copies:
        copy.wait()
    for m in range(slots):
        qkv_copy(m).wait()


def gather_and_project(mol_len, vectors, w_qkv, w_out, w_in, w_back, tokens, cotangent):
    slots = mol_len.shape[0]
    rows, width = tokens.shape
    block = rows // slots
    wide = 3 * width
    vmem = pl.BlockSpec(memory_space=pltpu.VMEM)
    anywhere = pl.BlockSpec(memory_space=pl.ANY)
    square = (width, width)
    return pl.pallas_call(
        gather_kernel,
        out_shape=[
            jax.ShapeDtypeStruct((slots, wide, block), bf16),
            jax.ShapeDtypeStruct((width, rows), bf16),
            jax.ShapeDtypeStruct((width, wide), bf16),
            jax.ShapeDtypeStruct(square, bf16),
            jax.ShapeDtypeStruct(square, bf16),
            jax.ShapeDtypeStruct(square, bf16),
            jax.ShapeDtypeStruct((rows // 2, width), bf16),
            jax.ShapeDtypeStruct((rows // 2, width), bf16),
            jax.ShapeDtypeStruct((16, width), f32),
            jax.ShapeDtypeStruct((slots, 128), jnp.int32),
        ],
        in_specs=[pl.BlockSpec(memory_space=pltpu.SMEM)] + [vmem] * (VECTORS + 5) + [anywhere],
        out_specs=[anywhere] * 8 + [vmem] * 2,
        scratch_shapes=[
            pltpu.VMEM((DEVICES, 2 * SHARD, wide // 2 + 128), bf16),
            pltpu.VMEM((DEVICES, 2 * SHARD, wide // 2), bf16),
            pltpu.VMEM((width, wide), bf16),
            pltpu.VMEM(square, bf16),
            pltpu.VMEM(square, bf16),
            pltpu.VMEM(square, bf16),
            pltpu.VMEM((wide, width), bf16),
            pltpu.VMEM((rows, width), f32),
            pltpu.VMEM((width, rows), bf16),
            pltpu.VMEM((slots, wide, block), bf16),
            pltpu.VMEM((wide, 128), f32),
            pltpu.VMEM((rows // 2, width), bf16),
            pltpu.VMEM((rows // 2, width), bf16),
            pltpu.VMEM((slots, 128), jnp.int32),
            pltpu.VMEM((slots, 128), jnp.int32),
            pltpu.SemaphoreType.DMA((5,)),
            pltpu.SemaphoreType.DMA((5, CHIPS + 1)),
            pltpu.SemaphoreType.DMA((3,)),
            pltpu.SemaphoreType.DMA((6 + slots // 2,)),
            pltpu.SemaphoreType.DMA((COPIES + slots,)),
        ],
        compiler_params=pltpu.CompilerParams(
            collective_id=0, has_side_effects=True, vmem_limit_bytes=60 * MIB
        ),
    )(mol_len, *vectors, w_qkv, w_out, w_in, w_back, tokens, cotangent)


def middle_kernel(
    packed,
    head_dim,
    len_ref,
    qkv_ref,
    tok_first,
    tok_second,
    cot_first,
    cot_second,
    wout_ref,
    win_ref,
    wback_ref,
    vec_ref,
    mixed_out,
    dmix_ref,
    dqkv_ref,
    gvec_ref,
    *rest,
):
    if packed:
        mixed_odd, packed_ref, gout_ref, gin_ref, gback_ref, *rest = rest
    else:
        gout_ref, gin_ref, gback_ref, *rest = rest
    probs, ctx_s, linv_s, dctx_s, tok_ref, cot_ref, mixed_ref = rest
    step = pl.program_id(0)
    block, width = tok_ref.shape
    slot = 32
    group = 4
    heads = width // head_dim
    span = group * head_dim
    scale = head_dim ** (-0.5)
    length = len_ref[step, 0]
    first = step < pl.num_programs(0) // 2
    tok_ref[...] = jnp.where(first, tok_first[...], tok_second[...])
    cot_ref[...] = jnp.where(first, cot_first[...], cot_second[...])

    @pl.when(step == 0)
    def _():
        gout_ref[...] = jnp.zeros_like(gout_ref)
        gin_ref[...] = jnp.zeros_like(gin_ref)
        gback_ref[...] = jnp.zeros_like(gback_ref)
        gvec_ref[...] = jnp.zeros_like(gvec_ref)

    def run(size):
        extra = (slot - head_dim, size)
        sub = lax.broadcasted_iota(jnp.int32, extra, 0)
        lane = lax.broadcasted_iota(jnp.int32, extra, 1)
        one_row = jnp.where(sub == 0, 1.0, 0.0).astype(f32)
        two_rows = jnp.where(sub <= 1, 1.0, 0.0).astype(f32)
        mask_row = jnp.where((sub == 0) & (lane >= length), masked_score, 0.0).astype(f32)

        def group_rows(base, g):
            return slice(base + g * span, base + (g + 1) * span)

        def load(base, g):
            return qkv_ref[group_rows(base, g), :size].astype(f32)

        def place(j, rows):
            parts = []
            if j > 0:
                parts.append(jnp.zeros((slot * j, size), bf16))
            parts.append(rows)
            if j < group - 1:
                parts.append(jnp.zeros((slot * (group - 1 - j), size), bf16))
            return jnp.concatenate(parts, axis=0)

        def pieces(values):
            return [values[head_dim * j : head_dim * (j + 1)] for j in range(group)]

        def padded(values, tail):
            return [jnp.concatenate([p, tail], axis=0).astype(bf16) for p in pieces(values)]

        ahead = 3 if size > 128 else 6

        def forward():
            q, k, v, scores, weights, outs = {}, {}, {}, {}, {}, {}
            for t in range(heads + 2 * ahead):
                if t < heads:
                    g, j = divmod(t, group)
                    if j == 0:
                        q[g] = padded(load(0, g), one_row)
                        k[g] = jnp.concatenate(padded(load(width, g), mask_row), axis=0).T
                        v[g] = padded(load(2 * width, g), one_row)
                    scores[t] = dot(k[g], place(j, q[g][j]), 1, 0)
                h = t - ahead
                if 0 <= h < heads:
                    s = scores.pop(h)
                    peak = jnp.max(s, axis=0, keepdims=True)
                    weights[h] = jnp.exp2((s - peak) * (scale * log2_e)).astype(bf16)
                    probs[h, :size, :size] = weights[h]
                h = t - 2 * ahead
                if 0 <= h < heads:
                    g, j = divmod(h, group)
                    o = dot(v[g][j], weights.pop(h), 1, 0)
                    inverse = 1.0 / o[head_dim : head_dim + 1]
                    linv_s[h, :, :size] = jnp.broadcast_to(inverse, (8, size))
                    outs[h] = o[:head_dim] * inverse
                    if j == group - 1:
                        parts = [outs.pop(h - group + 1 + i) for i in range(group)]
                        ctx_s[group_rows(0, g), :size] = jnp.concatenate(parts, axis=0)

        forward()

        live = (lax.broadcasted_iota(jnp.int32, (size, 1), 0) < length).astype(f32)
        out_bias, gain, shift = vec_ref[4:5], vec_ref[5:6], vec_ref[6:7]
        in_bias, back_bias = vec_ref[7:8], vec_ref[8:9]

        strips = [slice(c, c + 256) for c in range(0, width, 256)]

        def row_mean(parts):
            return sum(jnp.sum(p, axis=1, keepdims=True) for p in parts) * (1.0 / width)

        def join(parts):
            return jnp.concatenate(parts, axis=1)

        d_ffn = cot_ref[:size].astype(f32) * live
        gvec_ref[4] += fold_rows(d_ffn)
        d_ffn = d_ffn.astype(bf16)
        ctx_t = ctx_s[:, :size].astype(bf16)
        ctx = ctx_t.T
        mixed = []
        for c in strips:
            attn = dot(ctx, wout_ref[:, c], 1, 0) + out_bias[:, c]
            mixed.append(tok_ref[:size, c].astype(f32) + live * attn)
        d_act = [dot(d_ffn, wback_ref[c], 1, 1) for c in strips[:1]]
        mean = row_mean(mixed)
        centred = [m - mean for m in mixed]
        factor = lax.rsqrt(row_mean([v * v for v in centred]) + eps)
        unit = [v * factor for v in centred]
        normed = join(
            [(u * gain[:, c] + shift[:, c]).astype(bf16) for u, c in zip(unit, strips)]
        )
        act, d_pre = [], []

        def project(c):
            return dot(normed, win_ref[:, c], 1, 0) + in_bias[:, c]

        ahead_pre = [project(strips[0])]
        for i, c in enumerate(strips):
            if i + 1 < len(strips):
                ahead_pre.append(project(strips[i + 1]))
                d_act.append(dot(d_ffn, wback_ref[strips[i + 1]], 1, 1))
            pre = ahead_pre[i]
            cdf = 0.5 * (1.0 + lax.erf(pre * 0.7071067811865476))
            act.append((pre * cdf).astype(bf16))
            slope = cdf + pre * jnp.exp(-0.5 * pre * pre) * 0.3989422804014327
            low = (d_act[i] * slope).astype(bf16)
            gvec_ref[3, :, c] += fold_rows(low.astype(f32))
            d_pre.append(low)
        act, d_pre = join(act), join(d_pre)
        d_normed = [dot(d_pre, win_ref[c], 1, 1) for c in strips]
        for m, c in zip(mixed, strips):
            branch = dot(act, wback_ref[:, c], 1, 0) + back_bias[:, c]
            mixed_ref[:size, c] = (m + live * branch).astype(bf16)
        act_t, normed_t = act.T, normed.T
        e = []
        for i, c in enumerate(strips):
            gback_ref[:, c] += dot(act_t, d_ffn[:, c], 1, 0)
            gvec_ref[1, :, c] += fold_rows(d_normed[i] * unit[i])
            gvec_ref[2, :, c] += fold_rows(d_normed[i])
            e.append(d_normed[i] * gain[:, c])
        mean = row_mean(e)
        inner = row_mean([v * u for v, u in zip(e, unit)])
        d_attn = []
        for i, c in enumerate(strips):
            gin_ref[:, c] += dot(normed_t, d_pre[:, c], 1, 0)
            d_mixed = cot_ref[:size, c].astype(f32) + factor * (e[i] - mean - unit[i] * inner)
            dmix_ref[:size, c] = d_mixed
            low = (live * d_mixed).astype(bf16)
            gvec_ref[0, :, c] += fold_rows(low.astype(f32))
            d_attn.append(low)
        d_attn = join(d_attn)
        for c in strips:
            dctx_s[c, :size] = dot(wout_ref[c], d_attn, 1, 1).astype(bf16)
        for c in strips:
            gout_ref[:, c] += dot(ctx_t, d_attn[:, c], 1, 0)

        behind = 3 if size > 128 else 6

        def backward():
            q, k, v, d, d_probs, d_scores = {}, {}, {}, {}, {}, {}
            d_q, d_k, d_v = {}, {}, {}
            for t in range(heads + 2 * behind):
                if t < heads:
                    g, j = divmod(t, group)
                    if j == 0:
                        q[g] = padded(load(0, g), one_row)
                        k[g] = padded(load(width, g), one_row)
                        v[g] = jnp.concatenate(padded(load(2 * width, g), two_rows), axis=0).T
                        d_out = pieces(dctx_s[group_rows(0, g), :size].astype(f32))
                        out = pieces(ctx_s[group_rows(0, g), :size])
                        for i in range(group):
                            here = d_out[i] * linv_s[g * group + i, :1, :size]
                            inner = -jnp.sum(here * out[i], axis=0, keepdims=True)
                            high = inner.astype(bf16).astype(f32)
                            blank = jnp.zeros((slot - head_dim - 2, size), f32)
                            tail = [here, high, inner - high, blank]
                            d[g * group + i] = jnp.concatenate(tail, axis=0).astype(bf16)
                    d_probs[t] = dot(v[g], place(j, d[t]), 1, 0)
                h = t - behind
                if 0 <= h < heads:
                    p = probs[h, :size, :size]
                    d_scores[h] = (p.astype(f32) * d_probs.pop(h)).astype(bf16)
                h = t - 2 * behind
                if 0 <= h < heads:
                    g, j = divmod(h, group)
                    ds = d_scores.pop(h)
                    d_v[h] = dot(d.pop(h), probs[h, :size, :size], 1, 1)[:head_dim]
                    d_q[h] = dot(k[g][j], ds, 1, 0)[:head_dim] * scale
                    d_k[h] = dot(q[g][j], ds, 1, 1)[:head_dim] * scale
                    if j == group - 1:
                        for base, parts in ((0, d_q), (width, d_k), (2 * width, d_v)):
                            some = [parts.pop(h - group + 1 + i) for i in range(group)]
                            dqkv_ref[group_rows(base, g), :size] = jnp.concatenate(
                                some, axis=0
                            ).astype(bf16)

        backward()

        if size < block:
            mixed_ref[size:] = tok_ref[size:]
            dmix_ref[size:] = cot_ref[size:].astype(f32)
            dqkv_ref[:, size:] = jnp.zeros((3 * width, block - size), bf16)

    half = block // 2

    @pl.when(length == 0)
    def _():
        mixed_ref[...] = tok_ref[...]
        dmix_ref[...] = cot_ref[...].astype(f32)
        dqkv_ref[...] = jnp.zeros_like(dqkv_ref)

    @pl.when((length > 0) & (length <= half))
    def _():
        run(half)

    @pl.when(length > half)
    def _():
        run(block)

    if packed:

        @pl.when(first)
        def _():
            mixed_out[...] = mixed_ref[...]

        @pl.when(jnp.logical_not(first))
        def _():
            mixed_odd[...] = mixed_ref[...]

    else:
        mixed_out[...] = mixed_ref[...]

    if packed:

        @pl.when(step == pl.num_programs(0) - 1)
        def _():
            columns = width // 2
            for i in range(DEVICES):
                p = (i % 2) * CHIPS + i // 2
                rows = slice(SHARD * i, SHARD * (i + 1))
                top = jnp.concatenate([gout_ref[rows], gback_ref[rows, :columns]], axis=1)
                bottom = jnp.concatenate([gin_ref[rows], gback_ref[rows, columns:]], axis=1)
                packed_ref[p] = jnp.concatenate([top, bottom], axis=0).astype(bf16)


def middle(lengths, qkv, tokens, cotangent, w_out, w_in, w_back, vectors, packed):
    slots, wide, block = qkv.shape
    rows, width = slots * block, wide // 3
    square = (width, width)
    shared = slots // 2

    def whole(shape):
        return pl.BlockSpec(shape, lambda m: (0,) * len(shape))

    by_rows = pl.BlockSpec((block, width), lambda m: (m, 0))
    if packed:
        first = pl.BlockSpec((block, width), lambda m: (2 * jnp.minimum(m, shared - 1), 0))
        second = pl.BlockSpec((block, width), lambda m: (jnp.maximum(m - shared, 0), 0))
    else:
        first = pl.BlockSpec((block, width), lambda m: (jnp.minimum(m, shared - 1), 0))
        second = pl.BlockSpec((block, width), lambda m: (jnp.maximum(m, shared), 0))
    out_specs = [
        by_rows,
        by_rows,
        pl.BlockSpec((3 * width, block), lambda m: (0, m)),
        whole((5, 8, width)),
    ]
    out_shape = [
        jax.ShapeDtypeStruct((rows, width), bf16),
        jax.ShapeDtypeStruct((rows, width), f32),
        jax.ShapeDtypeStruct((3 * width, rows), bf16),
        jax.ShapeDtypeStruct((5, 8, width), f32),
    ]
    scratch = [
        pltpu.VMEM((HEADS, block, block), bf16),
        pltpu.VMEM((width, block), f32),
        pltpu.VMEM((HEADS, 8, block), f32),
        pltpu.VMEM((width, block), bf16),
        pltpu.VMEM((block, width), bf16),
        pltpu.VMEM((block, width), bf16),
        pltpu.VMEM((block, width), bf16),
    ]
    if packed:
        shape = (DEVICES, 2 * SHARD, width + width // 2)
        out_specs[0] = first
        out_specs += [second, whole(shape)]
        out_shape.append(jax.ShapeDtypeStruct((rows // 2, width), bf16))
        out_shape.append(jax.ShapeDtypeStruct(shape, bf16))
        scratch = [pltpu.VMEM(square, f32)] * 3 + scratch
    else:
        out_specs += [whole(square)] * 3
        out_shape += [jax.ShapeDtypeStruct(square, f32)] * 3
    return pl.pallas_call(
        functools.partial(middle_kernel, packed, width // HEADS),
        grid=(slots,),
        in_specs=[
            pl.BlockSpec(memory_space=pltpu.SMEM),
            pl.BlockSpec((None, 3 * width, block), lambda m: (m, 0, 0)),
            first,
            second,
            first,
            second,
            whole(square),
            whole(square),
            whole(square),
            whole((16, width)),
        ],
        out_specs=out_specs,
        scratch_shapes=scratch,
        out_shape=out_shape,
        compiler_params=pltpu.CompilerParams(vmem_limit_bytes=58 * MIB),
    )(lengths, qkv, *tokens, *cotangent, w_out, w_in, w_back, vectors)


def scatter_kernel(
    sr_hbm,
    dqkv_hbm,
    unit_hbm,
    fq_hbm,
    tok_hbm,
    odd_hbm,
    dmix_hbm,
    mixed_hbm,
    vec_ref,
    gvec_ref,
    grad_hbm,
    grad_out,
    mixed_out,
    gq_ref,
    gr_ref,
    sq,
    sr,
    rq_sib,
    rr_sib,
    rq,
    rr,
    dqkv,
    unit_t,
    fq,
    tok,
    dmix,
    grad,
    mixed,
    gain_wide,
    shift_wide,
    small_wide,
    sums,
    result,
    send_sem,
    recv_sem,
    swap_send,
    swap_recv,
    copy_sem,
):
    at = Place()
    at.greet()
    rows, width = tok.shape
    wide = 3 * width
    half_q = wide // 2
    slots = 8
    block = rows // slots
    mine, theirs = at.c * CHIPS, (1 - at.c) * CHIPS
    own = at.block(at.c, at.z, at.y, at.x)
    level_rows = 8 * SHARD

    def local(src, dst, i):
        copy = pltpu.make_async_copy(src, dst, copy_sem.at[i])
        copy.start()
        return copy

    sr_in = local(sr_hbm, sr, 0)
    unit_in = local(unit_hbm, unit_t, 1)
    parts_in = []
    for part in range(3):
        some = pl.ds(part * width, width)
        parts_in.append(local(dqkv_hbm.at[some], dqkv.at[some], 2 + 2 * part))
        parts_in.append(local(fq_hbm.at[:, some], fq.at[:, some], 3 + 2 * part))

    def part_wait(part):
        for copy in parts_in[2 * part : 2 * part + 2]:
            copy.wait()

    shared = slots // 2

    def rows_of(i, count=1):
        return pl.ds(i * block, count * block)

    mixed_in = local(mixed_hbm, mixed, 8)
    late = [local(dmix_hbm, dmix, 9), local(odd_hbm, tok.at[rows_of(shared, shared)], 10)]
    for i in range(shared):
        late.append(local(tok_hbm.at[rows_of(2 * i)], tok.at[rows_of(i)], 11 + i))

    def swap_copy(src, dst, i):
        return pltpu.make_async_remote_copy(
            src_ref=src,
            dst_ref=dst,
            send_sem=swap_send.at[i],
            recv_sem=swap_recv.at[i],
            device_id=(at.sib,),
            device_id_type=MESH,
        )

    slabs = (
        (sq, rq_sib, rq, 0, 640),
        (sq, rq_sib, rq, 640, 640),
        (sr, rr_sib, rr, 0, 1152),
    )

    def cut(ref, k, first, count):
        return ref.at[pl.ds(first, count), :, pl.ds(slabs[k][3], slabs[k][4])]

    def piece(ref, k, p):
        _, _, _, column, columns = slabs[k]
        return ref[p, :, column : column + columns].astype(f32)

    def put(k, p, value):
        slab, _, _, column, columns = slabs[k]
        slab[p, :, column : column + columns] = value.astype(bf16)

    def remote(k, src, dst, target, sem):
        return pltpu.make_async_remote_copy(
            src_ref=src,
            dst_ref=dst,
            send_sem=send_sem.at[k],
            recv_sem=recv_sem.at[k, sem],
            device_id=(target,),
            device_id_type=MESH,
        )

    def x_type(j):
        return at.block(at.c, j, at.y, 1 - at.x)

    def y_type(j):
        return at.block(at.c, j, 1 - at.y, at.x)

    def corner_type(j):
        return at.block(at.c, j, 1 - at.y, 1 - at.x)

    def column_type(j):
        return at.block(at.c, j, at.y, at.x)

    def sib_copy(k, j):
        src = cut(slabs[k][0], k, theirs + 4 * j, 4)
        return remote(k, src, cut(slabs[k][1], k, 4 * j, 4), at.sib, j)

    def sib_send(k, j):
        sib_copy(k, j).start()

    def step_copy(k, src, slot, target):
        src = cut(slabs[k][0], k, src, 1)
        return remote(k, src, cut(slabs[k][2], k, slot, 1), target, PLANES + slot)

    def x_send(k, j):
        step_copy(k, x_type(j), 4 + j, at.xn).start()

    def y_send(k, j):
        step_copy(k, y_type(j), 8 + j, at.yn).start()

    def sib_add(k, j):
        sib_copy(k, j).wait_recv()

        def body(i, carry):
            p = mine + 4 * j + i
            put(k, p, piece(slabs[k][0], k, p) + piece(slabs[k][1], k, 4 * j + i))
            return carry

        lax.fori_loop(0, 4, body, 0)
        step_copy(k, corner_type(j), j, at.yn if j % 2 == 0 else at.xn).start()
        (y_send if j % 2 == 0 else x_send)(k, j)

    def corner_add(k, j):
        step_copy(k, own, j, at.sib).wait_recv()
        p = x_type(j) if j % 2 == 0 else y_type(j)
        put(k, p, piece(slabs[k][0], k, p) + piece(slabs[k][2], k, j))
        (x_send if j % 2 == 0 else y_send)(k, j)

    def plane_add(k, j):
        p = column_type(j)
        step_copy(k, own, 4 + j, at.sib).wait_recv()
        step_copy(k, own, 8 + j, at.sib).wait_recv()
        received = piece(slabs[k][2], k, 4 + j) + piece(slabs[k][2], k, 8 + j)
        put(k, p, piece(slabs[k][0], k, p) + received)

        @pl.when(at.z != j)
        def _():
            step_copy(k, p, 12 + at.z, at.me + 8 * (j - at.z)).start()

    def land(k):
        total = gq_ref if slabs[k][0] is sq else gr_ref
        columns = slice(slabs[k][3], slabs[k][3] + slabs[k][4])
        total[:, columns] = piece(slabs[k][0], k, own)
        for j in range(PLANES):

            @pl.when(at.z != j)
            def _():
                step_copy(k, own, 12 + j, at.sib).wait_recv()
                total[:, columns] += piece(slabs[k][2], k, 12 + j)

    def prepare(part):
        columns = slice(part * width, (part + 1) * width)
        sums[:, columns] = dot(jnp.ones((16, rows), bf16), dqkv[columns], 1, 1)[:8]
        if part == 0:
            gain_wide[...] = jnp.broadcast_to(vec_ref[0:1], (128, width)).T
            shift_wide[...] = jnp.broadcast_to(vec_ref[1:2], (128, width)).T
            small_wide[...] = jnp.zeros((width, 128), f32)
        if part == 2:
            lines = [jnp.zeros((2, width), f32), sums[0:1, :width], sums[0:1, 2 * width :]]
            lines += [jnp.sum(gvec_ref[i], axis=0, keepdims=True) for i in range(5)]
            lines.append(jnp.zeros((128 - VECTORS, width), f32))
            small_wide[...] += jnp.concatenate(lines, axis=0).T

    def weight_grad(j, part):
        lines = pl.ds(pl.multiple_of(j * level_rows, level_rows), level_rows)
        columns = pl.ds(pl.multiple_of(part * width, width), width)
        product = dot(unit_t[lines], dqkv[columns], 1, 1)
        weight = fq[lines, columns].astype(f32)
        line = sums[0:1, columns]
        gain_sum = jnp.sum(weight * product, axis=1, keepdims=True)
        shift_sum = jnp.sum(weight * line, axis=1, keepdims=True)
        lane = lax.broadcasted_iota(jnp.int32, (level_rows, 128), 1)
        small_wide[lines] += jnp.where(
            lane == 0, gain_sum, jnp.where(lane == 1, shift_sum, 0.0)
        )
        gain = jnp.concatenate([gain_wide[lines]] * (width // 128), axis=1)
        shift = jnp.concatenate([shift_wide[lines]] * (width // 128), axis=1)
        result[:, columns] = gain * product + shift * line

        @pl.when(part == 2)
        def _():
            small = small_wide[lines]
            blank = jnp.zeros((SHARD, 128), f32)
            for i in range(8):
                p = (i % 2) * CHIPS + 4 * j + i // 2
                some = slice(SHARD * i, SHARD * (i + 1))
                top = jnp.concatenate([result[some, :half_q], small[some]], axis=1)
                bottom = jnp.concatenate([result[some, half_q:], blank], axis=1)
                sq[p] = jnp.concatenate([top, bottom], axis=0).astype(bf16)

    def grad_rows(m):
        return pl.ds(pl.multiple_of(m * block, block), block)

    def grad_copy(m):
        return pltpu.make_async_copy(
            grad.at[grad_rows(m)], grad_hbm.at[grad_rows(m)], copy_sem.at[11 + shared + m]
        )

    def input_grad(m):
        some = grad_rows(m)
        d_normed = dot(fq[...], dqkv[:, some], 1, 0).T
        unit, factor = normalize(tok[some].astype(f32))
        share = norm_backward(d_normed, vec_ref[0:1], unit, factor)
        grad[some] = (dmix[some] + share).astype(bf16)

        @pl.when(m < shared)
        def _():
            grad_copy(m).start()

        @pl.when(m >= shared)
        def _():
            swap_copy(grad.at[some], grad_out.at[grad_rows(m - shared)], 0).start()

    def late_wait():
        for copy in late:
            copy.wait()

    sr_in.wait()
    at.await_all()
    sib_send(2, 2)
    sib_send(2, 1)
    sib_send(2, 0)
    sib_add(2, 2)
    sib_send(2, 3)
    sib_add(2, 1)
    unit_in.wait()
    part_wait(0)
    prepare(0)
    sib_add(2, 0)
    part_wait(1)
    sib_add(2, 3)
    prepare(1)

    def beside_weight_0():
        part_wait(2)
        prepare(2)

    def beside_weight_2():
        sib_send(1, 0)

    def beside_weight_4():
        corner_add(2, 0)
        corner_add(2, 1)
        sib_send(0, 0)

    def beside_weight_5():
        sib_send(0, 3)
        corner_add(2, 3)

    def beside_weight_6():
        corner_add(2, 2)

    def beside_weight_7():
        sib_add(0, 0)
        sib_add(0, 3)
        plane_add(2, 0)

    def beside_weight_8():
        sib_send(0, 1)
        sib_add(1, 0)
        plane_add(2, 3)

    def beside_weight_9():
        sib_add(0, 1)

    def beside_weight_10():
        corner_add(0, 3)
        sib_send(1, 3)


    def beside_weight_step(i, carry):
        turn = i // 3
        j = jnp.where(turn == 0, 0, jnp.where(turn == 1, 3, jnp.where(turn == 2, 1, 2)))
        weight_grad(j, lax.rem(i, 3))
        pl.when(i == 0)(beside_weight_0)
        pl.when(i == 2)(beside_weight_2)
        pl.when(i == 4)(beside_weight_4)
        pl.when(i == 5)(beside_weight_5)
        pl.when(i == 6)(beside_weight_6)
        pl.when(i == 7)(beside_weight_7)
        pl.when(i == 8)(beside_weight_8)
        pl.when(i == 9)(beside_weight_9)
        pl.when(i == 10)(beside_weight_10)
        return carry

    lax.fori_loop(0, 12, beside_weight_step, 0)
    corner_add(0, 0)
    sib_send(1, 2)
    plane_add(2, 2)
    sib_send(0, 2)
    corner_add(0, 1)
    plane_add(2, 1)
    sib_add(1, 3)
    sib_send(1, 1)
    mixed_in.wait()
    swap_copy(mixed, mixed_out, 1).start()
    late_wait()
    sib_add(1, 2)
    plane_add(0, 3)
    corner_add(1, 0)
    sib_add(0, 2)

    def beside_input_0():
        plane_add(0, 0)
        corner_add(1, 3)
        corner_add(1, 2)
        sib_add(1, 1)
        plane_add(0, 1)

    def beside_input_1():
        corner_add(0, 2)
        plane_add(1, 2)
        plane_add(1, 0)

    def beside_input_2():
        corner_add(1, 1)
        plane_add(1, 3)

    def beside_input_4():
        plane_add(0, 2)
        plane_add(1, 1)

    def beside_input_6():
        land(2)


    def beside_input_step(i, carry):
        input_grad(i)
        pl.when(i == 0)(beside_input_0)
        pl.when(i == 1)(beside_input_1)
        pl.when(i == 2)(beside_input_2)
        pl.when(i == 4)(beside_input_4)
        pl.when(i == 6)(beside_input_6)
        return carry

    lax.fori_loop(0, 8, beside_input_step, 0)
    land(0)
    land(1)
    for k in range(len(slabs)):
        every = cut(slabs[k][0], k, 0, DEVICES - 1)
        remote(k, every, every, at.sib, 0).wait_send()
    for m in range(shared):
        grad_copy(m).wait()
    swap_copy(grad.at[rows_of(shared, shared)], grad_out, 0).wait()
    swap_copy(mixed, mixed_out, 1).wait()


def scatter(packed, dqkv, unit_t, full_qkv, tokens, odd_tokens, d_mixed, mixed, vectors, sums):
    rows, width = tokens.shape
    wide = 3 * width
    vmem = pl.BlockSpec(memory_space=pltpu.VMEM)
    anywhere = pl.BlockSpec(memory_space=pl.ANY)
    tall = 2 * SHARD
    widths = (wide // 2 + 128, wide // 2)
    return pl.pallas_call(
        scatter_kernel,
        out_shape=[jax.ShapeDtypeStruct((rows // 2, width), bf16)] * 3
        + [jax.ShapeDtypeStruct((tall, w), f32) for w in widths],
        in_specs=[anywhere] * 8 + [vmem] * 2,
        out_specs=[anywhere] * 3 + [vmem] * 2,
        scratch_shapes=[pltpu.VMEM((DEVICES, tall, w), bf16) for w in widths]
        + [pltpu.VMEM((CHIPS, tall, w), bf16) for w in widths]
        + [pltpu.VMEM((4 * PLANES, tall, w), bf16) for w in widths]
        + [
            pltpu.VMEM((wide, rows), bf16),
            pltpu.VMEM((width, rows), bf16),
            pltpu.VMEM((width, wide), bf16),
            pltpu.VMEM((rows, width), bf16),
            pltpu.VMEM((rows, width), f32),
            pltpu.VMEM((rows, width), bf16),
            pltpu.VMEM((rows // 2, width), bf16),
            pltpu.VMEM((width, 128), f32),
            pltpu.VMEM((width, 128), f32),
            pltpu.VMEM((width, 128), f32),
            pltpu.VMEM((8, wide), f32),
            pltpu.VMEM((8 * SHARD, wide), f32),
            pltpu.SemaphoreType.DMA((3,)),
            pltpu.SemaphoreType.DMA((3, 5 * PLANES)),
            pltpu.SemaphoreType.DMA((2,)),
            pltpu.SemaphoreType.DMA((2,)),
            pltpu.SemaphoreType.DMA((19,)),
        ],
        compiler_params=pltpu.CompilerParams(
            collective_id=1, has_side_effects=True, vmem_limit_bytes=60 * MIB
        ),
    )(packed, dqkv, unit_t, full_qkv, tokens, odd_tokens, d_mixed, mixed, vectors, sums)


def finish_kernel(
    _, mixed_odd, grad_even, grad_odd, q_ref, r_ref, mixed, grad, g_qkv, g_out, g_in, g_back, *lines
):
    block = mixed_odd.shape[0]
    mixed[...] = mixed_odd[...]
    grad[:block] = grad_even[...]
    grad[block:] = grad_odd[...]

    @pl.when(pl.program_id(0) == 0)
    def _():
        width = g_out.shape[1]
        half_q = 3 * width // 2
        half = width // 2
        g_qkv[:, :half_q] = q_ref[:SHARD, :half_q]
        g_qkv[:, half_q:] = q_ref[SHARD:, :half_q]
        g_out[...] = r_ref[:SHARD, :width]
        g_in[...] = r_ref[SHARD:, :width]
        g_back[:, :half] = r_ref[:SHARD, width:]
        g_back[:, half:] = r_ref[SHARD:, width:]
        small = q_ref[:SHARD, half_q:].T
        for i, line in enumerate(lines):
            line[...] = small[i, :SHARD]


def finish(mixed, mixed_odd, grad, grad_odd, q_part, r_part, slots):
    rows, width = mixed.shape
    block = rows // slots
    single = pl.BlockSpec((block, width), lambda i: (i, 0))
    double = pl.BlockSpec((2 * block, width), lambda i: (i, 0))

    def whole(shape):
        return pl.BlockSpec(shape, lambda i: (0,) * len(shape))

    shapes = [(SHARD, 3 * width)] + [(SHARD, width)] * 3 + [(SHARD,)] * 9
    return pl.pallas_call(
        finish_kernel,
        grid=(slots // 2,),
        out_shape=[jax.ShapeDtypeStruct((rows, width), bf16)] * 2
        + [jax.ShapeDtypeStruct(s, f32) for s in shapes],
        in_specs=[pl.BlockSpec(memory_space=pl.ANY)]
        + [single] * 3
        + [whole(q_part.shape), whole(r_part.shape)],
        out_specs=[pl.BlockSpec((block, width), lambda i: (2 * i + 1, 0)), double]
        + [whole(s) for s in shapes],
        input_output_aliases={0: 0},
    )(mixed, mixed_odd, grad, grad_odd, q_part, r_part)


def on_one_plan(tokens, mol_len, cotangent, vectors, w_qkv, w_out, w_in, w_back):
    slots = mol_len.shape[0]
    (
        qkv,
        unit_t,
        full_qkv,
        full_out,
        full_in,
        full_back,
        odd_tokens,
        odd_cotangent,
        lines,
        lengths,
    ) = gather_and_project(mol_len, vectors, w_qkv, w_out, w_in, w_back, tokens, cotangent)
    mixed, d_mixed, dqkv, sums, mixed_sent, packed = middle(
        lengths,
        qkv,
        (tokens, odd_tokens),
        (cotangent, odd_cotangent),
        full_out,
        full_in,
        full_back,
        lines,
        True,
    )
    grad, grad_odd, mixed_odd, q_part, r_part = scatter(
        packed, dqkv, unit_t, full_qkv, tokens, odd_tokens, d_mixed, mixed_sent, lines, sums
    )
    mixed_out, token_grad, g_qkv, g_out, g_in, g_back, *small = finish(
        mixed, mixed_odd, grad, grad_odd, q_part, r_part, slots
    )
    return mixed_out, token_grad, small, g_qkv, g_out, g_in, g_back


def on_any_plan(tokens, mol_len, cotangent, vectors, w_qkv, w_out, w_in, w_back):
    slots = mol_len.shape[0]
    rows, width = tokens.shape

    def gather(array, axis):
        return lax.all_gather(array, "fsdp", axis=axis, tiled=True)

    lines = gather(jnp.stack(vectors), 1).astype(f32)
    lines = jnp.pad(lines, ((0, 16 - len(vectors)), (0, 0)))
    full_qkv, full_out, full_in, full_back = (
        gather(w, 0) for w in (w_qkv, w_out, w_in, w_back)
    )
    unit, factor = normalize(tokens.astype(f32))
    normed = (unit * lines[0] + lines[1]).astype(bf16)
    qkv = jnp.dot(normed, full_qkv, preferred_element_type=f32)
    qkv = (qkv + jnp.concatenate([lines[2], jnp.zeros_like(lines[2]), lines[3]])).astype(bf16)
    qkv = qkv.reshape(slots, rows // slots, 3 * width).transpose(0, 2, 1)
    mixed_out, d_mixed, dqkv, sums, g_out, g_in, g_back = middle(
        jnp.broadcast_to(mol_len[:, None], (slots, 128)),
        qkv,
        (tokens, tokens),
        (cotangent, cotangent),
        full_out,
        full_in,
        full_back,
        lines,
        False,
    )
    g_qkv = jnp.einsum("rf,dr->fd", normed, dqkv, preferred_element_type=f32)
    d_normed = jnp.einsum("dr,fd->rf", dqkv, full_qkv, preferred_element_type=f32)
    totals = jnp.sum(dqkv.astype(f32), axis=1)
    small = [jnp.sum(d_normed * unit, axis=0), jnp.sum(d_normed, axis=0)]
    small += [totals[:width], totals[2 * width :]]
    small += [jnp.sum(sums[i], axis=0) for i in range(5)]
    share = norm_backward(d_normed, lines[0], unit, factor)
    token_grad = (d_mixed + share).astype(bf16)

    def scatter_sum(array, axis):
        return lax.psum_scatter(array, "fsdp", scatter_dimension=axis, tiled=True)

    small = scatter_sum(jnp.stack(small), 1)
    return (
        mixed_out,
        token_grad,
        [small[i] for i in range(9)],
        *(scatter_sum(g, 0) for g in (g_qkv, g_out, g_in, g_back)),
    )


def per_device(
    devices,
    tokens,
    mol_len,
    cotangent,
    ln1_gain,
    ln1_bias,
    w_qkv,
    q_bias,
    v_bias,
    w_out,
    out_bias,
    ln2_gain,
    ln2_bias,
    w_in,
    in_bias,
    w_back,
    back_bias,
):
    vectors = [
        ln1_gain,
        ln1_bias,
        q_bias,
        v_bias,
        out_bias,
        ln2_gain,
        ln2_bias,
        in_bias,
        back_bias,
    ]
    known = devices == DEVICES and w_qkv.shape[0] == SHARD
    plan = on_one_plan if known else on_any_plan
    mixed_out, token_grad, small, g_qkv, g_out, g_in, g_back = plan(
        tokens, mol_len, cotangent, vectors, w_qkv, w_out, w_in, w_back
    )
    return (
        mixed_out,
        token_grad,
        small[0],
        small[1],
        g_qkv,
        small[2],
        small[3],
        g_out,
        small[4],
        small[5],
        small[6],
        g_in,
        small[7],
        g_back,
        small[8],
    )


def solution(mesh):
    line, matrix = P("fsdp"), P("fsdp", None)
    return jax.shard_map(
        functools.partial(per_device, mesh.shape["fsdp"]),
        mesh=mesh,
        in_specs=(
            matrix,
            line,
            matrix,
            line,
            line,
            matrix,
            line,
            line,
            matrix,
            line,
            line,
            line,
            matrix,
            line,
            matrix,
            line,
        ),
        out_specs=(
            matrix,
            matrix,
            line,
            line,
            matrix,
            line,
            line,
            matrix,
            line,
            line,
            line,
            matrix,
            line,
            matrix,
            line,
        ),
        check_vma=False,
    )
```

```python
import functools

import jax
import jax.numpy as jnp
from jax import lax
from jax.experimental import pallas as pl
from jax.experimental.pallas import tpu as pltpu
from jax.sharding import PartitionSpec as P

HEADS = 32

bf16 = jnp.bfloat16
f32 = jnp.float32
eps = 1e-05
masked_score = -1e30
log2_e = 1.4426950408889634
MESH = pl.DeviceIdType.MESH
MIB = 1 << 20

PLANES = 4
CHIPS = 4 * PLANES
DEVICES = 2 * CHIPS
SHARD = 24
VECTORS = 9
COPIES = 8


def dot(left, right, left_dim, right_dim):
    return lax.dot_general(
        left, right, (((left_dim,), (right_dim,)), ((), ())), preferred_element_type=f32
    )


def normalize(values):
    centred = values - jnp.mean(values, axis=-1, keepdims=True)
    factor = lax.rsqrt(jnp.mean(centred * centred, axis=-1, keepdims=True) + eps)
    return centred * factor, factor


def norm_backward(d_normed, gain, unit, factor):
    e = d_normed * gain
    inner = jnp.mean(e * unit, axis=-1, keepdims=True)
    return factor * (e - jnp.mean(e, axis=-1, keepdims=True) - unit * inner)


def fold_rows(values):
    rows, columns = values.shape
    return jnp.sum(values.reshape(rows // 8, 8, columns), axis=0)


class Place:
    def __init__(self):
        me = lax.axis_index("fsdp")
        self.me = me
        self.c = lax.rem(me, 2)
        self.x = lax.rem(me // 2, 2)
        self.y = lax.rem(me // 4, 2)
        self.z = me // 8
        self.sib = me + 1 - 2 * self.c
        self.xn = me + 2 - 4 * self.x
        self.yn = me + 4 - 8 * self.y

    def block(self, c, z, y, x):
        return ((c * PLANES + z) * 2 + y) * 2 + x

    def greet(self):
        sem = pltpu.get_barrier_semaphore()

        def signal(device):
            pl.semaphore_signal(sem, inc=1, device_id=(device,), device_id_type=MESH)

        for device in (self.sib, self.xn, self.yn):
            signal(device)
        for distance in range(1, PLANES):
            signal(lax.rem(self.me + 8 * distance, DEVICES))

    def await_all(self):
        pl.semaphore_wait(pltpu.get_barrier_semaphore(), 2 + PLANES)


def gather_kernel(
    len_ref,
    *refs,
):
    lines, refs = refs[:VECTORS], refs[VECTORS:]
    gather_body(len_ref, lines, *refs)


def gather_body(
    len_ref,
    lines,
    wq_ref,
    wo_ref,
    wi_ref,
    wb_ref,
    tok_ref,
    cot_hbm,
    qkv_hbm,
    unit_hbm,
    fq_hbm,
    fo_hbm,
    fi_hbm,
    fb_hbm,
    tok_hbm,
    cot_out,
    vec_ref,
    work_ref,
    gq,
    gr,
    fq,
    fo,
    fi,
    fb,
    fq_t,
    unit,
    unit_t,
    qkv,
    bias,
    tok_odd,
    cot_odd,
    len_send,
    len_recv,
    send_sem,
    recv_sem,
    swap_send,
    swap_recv,
    copy_sem,
):
    at = Place()
    at.greet()
    width = tok_ref.shape[1]
    slots, _, block = qkv.shape
    shared = slots // 2
    half_q = 3 * width // 2
    half = width // 2
    own = at.block(at.c, at.z, at.y, at.x)
    mine, theirs = at.c * CHIPS, (1 - at.c) * CHIPS
    slabs = ((gq, 0, 384), (gq, 384, 384), (gq, 768, 512), (gr, 0, 640), (gr, 640, 512))

    small = [line[...].astype(f32).reshape(1, SHARD) for line in lines]
    small = jnp.concatenate(small + [jnp.zeros((2 * SHARD - VECTORS, SHARD), f32)], axis=0)
    small = jnp.concatenate([small, jnp.zeros((2 * SHARD, 128 - SHARD), f32)], axis=1).astype(bf16)
    gq[own] = jnp.concatenate(
        [
            jnp.concatenate([wq_ref[:, :half_q], wq_ref[:, half_q:]], axis=0),
            small,
        ],
        axis=1,
    )
    gr[own] = jnp.concatenate(
        [
            jnp.concatenate([wo_ref[...], wi_ref[...]], axis=0),
            jnp.concatenate([wb_ref[:, :half], wb_ref[:, half:]], axis=0),
        ],
        axis=1,
    )

    def view(k, first, count):
        slab, column, columns = slabs[k]
        return slab.at[pl.ds(first, count), :, pl.ds(column, columns)]

    def remote(k, first, target, sem, count=1):
        return pltpu.make_async_remote_copy(
            src_ref=view(k, first, count),
            dst_ref=view(k, first, count),
            send_sem=send_sem.at[k],
            recv_sem=recv_sem.at[k, sem],
            device_id=(target,),
            device_id_type=MESH,
        )

    def send(k, b, target):
        remote(k, b, target, lax.rem(b, CHIPS)).start()

    def to_sib(k, b):
        remote(k, b, at.sib, CHIPS).start()

    def arrived(k, b):
        remote(k, b, at.sib, lax.rem(b, CHIPS)).wait_recv()

    def at_level(shift, body):
        level = at.z + shift
        if shift == 0:
            body(level)
        else:
            pl.when((level >= 0) & (level <= PLANES - 1))(lambda: body(level))

    def both(s):
        return (0,) if s == 0 else (-s, s)

    def own_plane(k):
        send(k, own, at.xn)
        send(k, own, at.yn)

    def own_column(k):
        for s in range(1, PLANES):
            for shift in both(s):
                at_level(shift, lambda level, shift=shift: send(k, own, at.me + 8 * shift))
        to_sib(k, own)

    def column(k, s):
        def body(level):
            b = at.block(at.c, level, at.y, at.x)
            arrived(k, b)
            send(k, b, at.xn)
            send(k, b, at.yn)
            to_sib(k, b)

        for shift in both(s):
            at_level(shift, body)

    def plane(k, s):
        def body(level):
            even = lax.rem(level, 2) == 0
            b = at.block(at.c, level, at.y, 1 - at.x)
            arrived(k, b)
            pl.when(even)(lambda: send(k, b, at.yn))
            to_sib(k, b)
            d = at.block(at.c, level, 1 - at.y, at.x)
            arrived(k, d)
            pl.when(jnp.logical_not(even))(lambda: send(k, d, at.xn))
            to_sib(k, d)

        for shift in both(s):
            at_level(shift, body)

    def corner(k):
        for j in range(PLANES):
            b = at.block(at.c, j, 1 - at.y, 1 - at.x)
            arrived(k, b)
            to_sib(k, b)

    def others(k):
        remote(k, theirs, at.sib, CHIPS, CHIPS).wait_recv()

    def rows_of(i):
        return pl.ds(i * block, block)

    cot_in = [
        pltpu.make_async_copy(
            cot_hbm.at[rows_of(2 * i + 1)], cot_odd.at[rows_of(i)], swap_recv.at[6 + i]
        )
        for i in range(shared)
    ]

    def swap_copy(src, dst, send, recv):
        return pltpu.make_async_remote_copy(
            src_ref=src,
            dst_ref=dst,
            send_sem=swap_send.at[send],
            recv_sem=swap_recv.at[recv],
            device_id=(at.sib,),
            device_id_type=MESH,
        )

    def tok_copy(i):
        return swap_copy(tok_ref.at[rows_of(2 * i + 1)], tok_odd.at[rows_of(i)], 0, i)

    def swap_start():
        swap_copy(len_send, len_recv, 2, 5).start()
        for i in range(shared):
            tok_copy(i).start()
        for i in range(shared):
            cot_in[i].wait()
            swap_copy(cot_odd.at[rows_of(i)], cot_out.at[rows_of(i)], 1, 4).start()

    def swap_end():
        swap_copy(len_send, len_recv, 2, 5).wait()
        swap_copy(tok_odd, tok_odd, 0, 0).wait_send()
        swap_copy(cot_odd, cot_out, 1, 4).wait()
        place = lax.broadcasted_iota(jnp.int32, (shared, 128), 0)
        own_lengths = jnp.zeros((shared, 128), jnp.int32)
        odd_lengths = jnp.zeros((shared, 128), jnp.int32)
        for i in range(shared):
            own_lengths = jnp.where(place == i, len_send[2 * i : 2 * i + 1], own_lengths)
            odd_lengths = jnp.where(place == i, len_recv[2 * i + 1 : 2 * i + 2], odd_lengths)
        work_ref[:shared] = own_lengths
        work_ref[shared:] = odd_lengths

    for i in range(slots):
        len_send[i : i + 1] = jnp.full((1, 128), len_ref[i], jnp.int32)
    for copy in cot_in:
        copy.start()

    def norm_step(m):
        rows = rows_of(m)
        if m < shared:
            here = tok_ref[rows_of(2 * m)]
        else:
            tok_copy(m - shared).wait_recv()
            here = tok_odd[rows_of(m - shared)]
        size = block // 2
        for i in range(2):
            some = pl.ds(m * block + i * size, size)
            values, _ = normalize(here[i * size : (i + 1) * size].astype(f32))
            unit[some] = values
            unit_t[:, some] = values.astype(bf16).T

    def strip(i):
        return pl.ds(pl.multiple_of(i * 2 * SHARD, 2 * SHARD), 2 * SHARD)

    def stack(first, second):
        return jnp.concatenate([first, second], axis=0).astype(bf16)

    def build_q():
        def body(i, carry):
            first = gq[i].astype(f32)
            second = gq[CHIPS + i].astype(f32)
            fq[strip(i), :half_q] = stack(first[:SHARD, :half_q], second[:SHARD, :half_q])
            fq[strip(i), half_q:] = stack(first[SHARD:, :half_q], second[SHARD:, :half_q])
            return carry

        lax.fori_loop(0, CHIPS, body, 0)
        out(fq, fq_hbm)

    def build_r():
        def body(i, carry):
            first = gr[i].astype(f32)
            second = gr[CHIPS + i].astype(f32)
            fo[strip(i)] = stack(first[:SHARD, :width], second[:SHARD, :width])
            fi[strip(i)] = stack(first[SHARD:, :width], second[SHARD:, :width])
            fb[strip(i), :half] = stack(first[:SHARD, width:], second[:SHARD, width:])
            fb[strip(i), half:] = stack(first[SHARD:, width:], second[SHARD:, width:])
            return carry

        lax.fori_loop(0, CHIPS, body, 0)
        out(fo, fo_hbm)
        out(fi, fi_hbm)
        out(fb, fb_hbm)

    copies = []

    def out(src, dst):
        copy = pltpu.make_async_copy(src, dst, copy_sem.at[len(copies)])
        copy.start()
        copies.append(copy)

    def turn(part):
        columns = slice(part * width, (part + 1) * width)
        fq_t[columns] = fq[:, columns].T

    def spread_vectors():
        column_at = lax.broadcasted_iota(jnp.int32, (128, width), 1)
        entry = lax.broadcasted_iota(jnp.int32, (128, width), 0)
        spread = jnp.where(lax.rem(column_at, SHARD) == entry, 1.0, 0.0).astype(bf16)
        stacked = jnp.concatenate([gq[p, :16, half_q:] for p in range(DEVICES)], axis=0)
        wide = dot(stacked, spread, 1, 0)
        total = jnp.zeros((16, width), f32)
        column_at = lax.broadcasted_iota(jnp.int32, (16, width), 1)
        for p in range(DEVICES):
            first = SHARD * ((p % CHIPS) * 2 + p // CHIPS)
            here = (column_at >= first) & (column_at < first + SHARD)
            total = total + jnp.where(here, wide[16 * p : 16 * p + 16], 0.0)
        vec_ref[...] = total
        bias[:width] = jnp.broadcast_to(total[2:3], (128, width)).T
        bias[width : 2 * width] = jnp.zeros((width, 128), f32)
        bias[2 * width :] = jnp.broadcast_to(total[3:4], (128, width)).T

    def qkv_copy(m):
        return pltpu.make_async_copy(qkv.at[m], qkv_hbm.at[m], copy_sem.at[COPIES + m])

    def qkv_part(m, part):
        here = unit[pl.ds(pl.multiple_of(m * block, block), block)]
        normed = (here * vec_ref[0:1] + vec_ref[1:2]).astype(bf16)
        lines = pl.ds(pl.multiple_of(part * width, width), width)
        result = dot(fq_t[lines], normed, 1, 1)
        added = jnp.concatenate([bias[lines]] * (block // 128), axis=1)
        qkv[m, lines] = (result + added).astype(bf16)
        pl.when(part == 2)(lambda: qkv_copy(m).start())

    norm_step(0)
    norm_step(1)
    at.await_all()
    swap_start()
    own_column(0)
    own_column(1)
    own_plane(1)
    own_plane(2)
    norm_step(2)
    own_plane(4)
    own_plane(3)
    own_column(2)
    own_plane(0)
    column(0, 3)
    column(0, 2)
    plane(1, 0)
    column(0, 1)
    plane(0, 3)
    plane(0, 0)
    own_column(3)
    column(1, 3)
    own_column(4)
    column(1, 1)
    norm_step(3)
    norm_step(4)
    column(1, 2)
    plane(2, 0)
    plane(0, 1)
    plane(1, 3)
    norm_step(5)
    norm_step(6)
    column(2, 3)
    column(2, 1)
    column(2, 2)
    plane(1, 2)
    plane(1, 1)
    norm_step(7)
    plane(0, 2)
    plane(2, 1)
    plane(2, 3)
    plane(2, 2)
    corner(1)
    column(3, 3)
    corner(0)
    plane(3, 0)
    corner(2)
    column(3, 2)
    others(1)
    others(0)
    plane(4, 0)
    column(3, 1)
    others(2)
    column(4, 3)
    build_q()
    plane(3, 3)
    column(4, 1)
    turn(0)
    turn(1)
    turn(2)
    spread_vectors()
    column(4, 2)

    def beside_qkv_6():
        plane(3, 2)

    def beside_qkv_7():
        plane(3, 1)

    def beside_qkv_8():
        plane(4, 1)

    def beside_qkv_11():
        plane(4, 2)
        plane(4, 3)

    def beside_qkv_14():
        corner(3)

    def beside_qkv_19():
        corner(4)

    def beside_qkv_22():
        others(4)
        others(3)


    def beside_qkv_step(i, carry):
        qkv_part(i // 3, lax.rem(i, 3))
        pl.when(i == 6)(beside_qkv_6)
        pl.when(i == 7)(beside_qkv_7)
        pl.when(i == 8)(beside_qkv_8)
        pl.when(i == 11)(beside_qkv_11)
        pl.when(i == 14)(beside_qkv_14)
        pl.when(i == 19)(beside_qkv_19)
        pl.when(i == 22)(beside_qkv_22)
        return carry

    lax.fori_loop(0, 24, beside_qkv_step, 0)
    build_r()
    out(unit_t, unit_hbm)
    out(tok_odd, tok_hbm)
    swap_end()
    for k in range(len(slabs)):
        remote(k, 0, at.sib, 0, DEVICES - 1).wait_send()
    for copy in copies:
        copy.wait()
    for m in range(slots):
        qkv_copy(m).wait()


def gather_and_project(mol_len, vectors, w_qkv, w_out, w_in, w_back, tokens, cotangent):
    slots = mol_len.shape[0]
    rows, width = tokens.shape
    block = rows // slots
    wide = 3 * width
    vmem = pl.BlockSpec(memory_space=pltpu.VMEM)
    anywhere = pl.BlockSpec(memory_space=pl.ANY)
    square = (width, width)
    return pl.pallas_call(
        gather_kernel,
        out_shape=[
            jax.ShapeDtypeStruct((slots, wide, block), bf16),
            jax.ShapeDtypeStruct((width, rows), bf16),
            jax.ShapeDtypeStruct((width, wide), bf16),
            jax.ShapeDtypeStruct(square, bf16),
            jax.ShapeDtypeStruct(square, bf16),
            jax.ShapeDtypeStruct(square, bf16),
            jax.ShapeDtypeStruct((rows // 2, width), bf16),
            jax.ShapeDtypeStruct((rows // 2, width), bf16),
            jax.ShapeDtypeStruct((16, width), f32),
            jax.ShapeDtypeStruct((slots, 128), jnp.int32),
        ],
        in_specs=[pl.BlockSpec(memory_space=pltpu.SMEM)] + [vmem] * (VECTORS + 5) + [anywhere],
        out_specs=[anywhere] * 8 + [vmem] * 2,
        scratch_shapes=[
            pltpu.VMEM((DEVICES, 2 * SHARD, wide // 2 + 128), bf16),
            pltpu.VMEM((DEVICES, 2 * SHARD, wide // 2), bf16),
            pltpu.VMEM((width, wide), bf16),
            pltpu.VMEM(square, bf16),
            pltpu.VMEM(square, bf16),
            pltpu.VMEM(square, bf16),
            pltpu.VMEM((wide, width), bf16),
            pltpu.VMEM((rows, width), f32),
            pltpu.VMEM((width, rows), bf16),
            pltpu.VMEM((slots, wide, block), bf16),
            pltpu.VMEM((wide, 128), f32),
            pltpu.VMEM((rows // 2, width), bf16),
            pltpu.VMEM((rows // 2, width), bf16),
            pltpu.VMEM((slots, 128), jnp.int32),
            pltpu.VMEM((slots, 128), jnp.int32),
            pltpu.SemaphoreType.DMA((5,)),
            pltpu.SemaphoreType.DMA((5, CHIPS + 1)),
            pltpu.SemaphoreType.DMA((3,)),
            pltpu.SemaphoreType.DMA((6 + slots // 2,)),
            pltpu.SemaphoreType.DMA((COPIES + slots,)),
        ],
        compiler_params=pltpu.CompilerParams(
            collective_id=0, has_side_effects=True, vmem_limit_bytes=60 * MIB
        ),
    )(mol_len, *vectors, w_qkv, w_out, w_in, w_back, tokens, cotangent)


def middle_kernel(
    packed,
    head_dim,
    len_ref,
    qkv_ref,
    tok_first,
    tok_second,
    cot_first,
    cot_second,
    wout_ref,
    win_ref,
    wback_ref,
    vec_ref,
    mixed_out,
    dmix_ref,
    dqkv_ref,
    gvec_ref,
    *rest,
):
    if packed:
        mixed_odd, packed_ref, gout_ref, gin_ref, gback_ref, *rest = rest
    else:
        gout_ref, gin_ref, gback_ref, *rest = rest
    probs, ctx_s, linv_s, dctx_s, tok_ref, cot_ref, mixed_ref = rest
    step = pl.program_id(0)
    block, width = tok_ref.shape
    slot = 32
    group = 4
    heads = width // head_dim
    span = group * head_dim
    scale = head_dim ** (-0.5)
    length = len_ref[step, 0]
    first = step < pl.num_programs(0) // 2
    tok_ref[...] = jnp.where(first, tok_first[...], tok_second[...])
    cot_ref[...] = jnp.where(first, cot_first[...], cot_second[...])

    @pl.when(step == 0)
    def _():
        gout_ref[...] = jnp.zeros_like(gout_ref)
        gin_ref[...] = jnp.zeros_like(gin_ref)
        gback_ref[...] = jnp.zeros_like(gback_ref)
        gvec_ref[...] = jnp.zeros_like(gvec_ref)

    def run(size, keys):
        extra = (slot - head_dim, size)
        sub = lax.broadcasted_iota(jnp.int32, extra, 0)
        lane = lax.broadcasted_iota(jnp.int32, extra, 1)
        one_row = jnp.where(sub == 0, 1.0, 0.0).astype(f32)
        two_rows = jnp.where(sub <= 1, 1.0, 0.0).astype(f32)
        mask_row = jnp.where((sub == 0) & (lane >= length), masked_score, 0.0).astype(f32)

        def group_rows(base, g):
            return slice(base + g * span, base + (g + 1) * span)

        def load(base, g):
            return qkv_ref[group_rows(base, g), :size].astype(f32)

        def place(j, rows):
            parts = []
            if j > 0:
                parts.append(jnp.zeros((slot * j, size), bf16))
            parts.append(rows)
            if j < group - 1:
                parts.append(jnp.zeros((slot * (group - 1 - j), size), bf16))
            return jnp.concatenate(parts, axis=0)

        def pieces(values):
            return [values[head_dim * j : head_dim * (j + 1)] for j in range(group)]

        def padded(values, tail):
            return [jnp.concatenate([p, tail], axis=0).astype(bf16) for p in pieces(values)]

        together = 1 if size == block else 2
        units = heads // together
        ahead = 3 if size == block else 6

        def beside(parts):
            return parts[0] if together == 1 else jnp.concatenate(parts, axis=1)

        def below(parts):
            return parts[0] if together == 1 else jnp.concatenate(parts, axis=0)

        def stacked(pair):
            return below([pair[:, i * size : (i + 1) * size] for i in range(together)])

        def own_part(value, i, n):
            return value[slot * i : slot * i + head_dim, i * n : (i + 1) * n]

        def all_keys(value):
            if keys == size:
                return value
            return jnp.concatenate([value, jnp.zeros((value.shape[0], size - keys), f32)], axis=1)

        def members(u):
            g, first = divmod(u * together, group)
            return g, range(first, first + together)

        def forward():
            q, k, v, scores, weights, outs = {}, {}, {}, {}, {}, {}
            for t in range(units + 2 * ahead):
                if t < units:
                    g, js = members(t)
                    if js[0] == 0:
                        q[g] = padded(load(0, g), one_row)
                        k[g] = jnp.concatenate(padded(load(width, g), mask_row), axis=0).T[:keys]
                        v[g] = padded(load(2 * width, g), one_row)
                    scores[t] = dot(k[g], beside([place(j, q[g][j]) for j in js]), 1, 0)
                u = t - ahead
                if 0 <= u < units:
                    s = scores.pop(u)
                    peak = jnp.max(s, axis=0, keepdims=True)
                    weights[u] = jnp.exp2((s - peak) * (scale * log2_e)).astype(bf16)
                    probs[u, :keys, : together * size] = weights[u]
                u = t - 2 * ahead
                if 0 <= u < units:
                    g, js = members(u)
                    o = dot(below([v[g][j] for j in js])[:, :keys], weights.pop(u), 1, 0)
                    for i, j in enumerate(js):
                        total = slot * i + head_dim
                        inverse = 1.0 / o[total : total + 1, i * size : (i + 1) * size]
                        linv_s[g * group + j, :, :size] = jnp.broadcast_to(inverse, (8, size))
                        outs[j] = own_part(o, i, size) * inverse
                    if js[-1] == group - 1:
                        parts = [outs.pop(j) for j in range(group)]
                        ctx_s[group_rows(0, g), :size] = jnp.concatenate(parts, axis=0)

        forward()

        live = (lax.broadcasted_iota(jnp.int32, (keys, 1), 0) < length).astype(f32)
        out_bias, gain, shift = vec_ref[4:5], vec_ref[5:6], vec_ref[6:7]
        in_bias, back_bias = vec_ref[7:8], vec_ref[8:9]

        strips = [slice(c, c + 256) for c in range(0, width, 256)]

        def row_mean(parts):
            return sum(jnp.sum(p, axis=1, keepdims=True) for p in parts) * (1.0 / width)

        def join(parts):
            return jnp.concatenate(parts, axis=1)

        d_ffn = cot_ref[:keys].astype(f32) * live
        gvec_ref[4] += fold_rows(d_ffn)
        d_ffn = d_ffn.astype(bf16)
        ctx_t = ctx_s[:, :size].astype(bf16)
        ctx = ctx_t.T[:keys]
        mixed = []
        for c in strips:
            attn = dot(ctx, wout_ref[:, c], 1, 0) + out_bias[:, c]
            mixed.append(tok_ref[:keys, c].astype(f32) + live * attn)
        d_act = [dot(d_ffn, wback_ref[c], 1, 1) for c in strips[:1]]
        mean = row_mean(mixed)
        centred = [m - mean for m in mixed]
        factor = lax.rsqrt(row_mean([v * v for v in centred]) + eps)
        unit = [v * factor for v in centred]
        normed = join(
            [(u * gain[:, c] + shift[:, c]).astype(bf16) for u, c in zip(unit, strips)]
        )
        act, d_pre = [], []

        def project(c):
            return dot(normed, win_ref[:, c], 1, 0) + in_bias[:, c]

        ahead_pre = [project(strips[0])]
        for i, c in enumerate(strips):
            if i + 1 < len(strips):
                ahead_pre.append(project(strips[i + 1]))
                d_act.append(dot(d_ffn, wback_ref[strips[i + 1]], 1, 1))
            pre = ahead_pre[i]
            cdf = 0.5 * (1.0 + lax.erf(pre * 0.7071067811865476))
            act.append((pre * cdf).astype(bf16))
            slope = cdf + pre * jnp.exp(-0.5 * pre * pre) * 0.3989422804014327
            low = (d_act[i] * slope).astype(bf16)
            gvec_ref[3, :, c] += fold_rows(low.astype(f32))
            d_pre.append(low)
        act, d_pre = join(act), join(d_pre)
        d_normed = [dot(d_pre, win_ref[c], 1, 1) for c in strips]
        for m, c in zip(mixed, strips):
            branch = dot(act, wback_ref[:, c], 1, 0) + back_bias[:, c]
            mixed_ref[:keys, c] = (m + live * branch).astype(bf16)
        act_t, normed_t = act.T, normed.T
        e = []
        for i, c in enumerate(strips):
            gback_ref[:, c] += dot(act_t, d_ffn[:, c], 1, 0)
            gvec_ref[1, :, c] += fold_rows(d_normed[i] * unit[i])
            gvec_ref[2, :, c] += fold_rows(d_normed[i])
            e.append(d_normed[i] * gain[:, c])
        mean = row_mean(e)
        inner = row_mean([v * u for v, u in zip(e, unit)])
        d_attn = []
        for i, c in enumerate(strips):
            gin_ref[:, c] += dot(normed_t, d_pre[:, c], 1, 0)
            d_mixed = cot_ref[:keys, c].astype(f32) + factor * (e[i] - mean - unit[i] * inner)
            dmix_ref[:keys, c] = d_mixed
            low = (live * d_mixed).astype(bf16)
            gvec_ref[0, :, c] += fold_rows(low.astype(f32))
            d_attn.append(low)
        d_attn = join(d_attn)
        for c in strips:
            d_ctx = dot(wout_ref[c], d_attn, 1, 1)
            dctx_s[c, :size] = all_keys(d_ctx).astype(bf16)
        for c in strips:
            gout_ref[:, c] += dot(ctx_t[:, :keys], d_attn[:, c], 1, 0)

        behind = 3 if size == block else 4

        def backward():
            q, k, v, d, d_probs, d_scores = {}, {}, {}, {}, {}, {}
            d_q, d_k, d_v = {}, {}, {}
            for t in range(units + 2 * behind):
                if t < units:
                    g, js = members(t)
                    if js[0] == 0:
                        q[g] = padded(load(0, g), one_row)
                        k[g] = padded(load(width, g), one_row)
                        v[g] = jnp.concatenate(padded(load(2 * width, g), two_rows), axis=0).T[:keys]
                        d_out = pieces(dctx_s[group_rows(0, g), :size].astype(f32))
                        out = pieces(ctx_s[group_rows(0, g), :size])
                        d[g] = []
                        for i in range(group):
                            scaled = d_out[i] * linv_s[g * group + i, :1, :size]
                            inner = -jnp.sum(scaled * out[i], axis=0, keepdims=True)
                            high = inner.astype(bf16).astype(f32)
                            blank = jnp.zeros((slot - head_dim - 2, size), f32)
                            tail = [scaled, high, inner - high, blank]
                            d[g].append(jnp.concatenate(tail, axis=0).astype(bf16))
                    d_probs[t] = dot(v[g], beside([place(j, d[g][j]) for j in js]), 1, 0)
                u = t - behind
                if 0 <= u < units:
                    p = probs[u, :keys, : together * size]
                    d_scores[u] = (p.astype(f32) * d_probs.pop(u)).astype(bf16)
                u = t - 2 * behind
                if 0 <= u < units:
                    g, js = members(u)
                    ds = d_scores.pop(u)
                    p = stacked(probs[u, :keys, : together * size])
                    to_v = dot(below([d[g][j] for j in js]), p, 1, 1)
                    to_q = dot(below([k[g][j] for j in js])[:, :keys], ds, 1, 0)
                    to_k = dot(below([q[g][j] for j in js]), stacked(ds), 1, 1)
                    for i, j in enumerate(js):
                        d_v[j] = all_keys(own_part(to_v, i, keys))
                        d_q[j] = own_part(to_q, i, size) * scale
                        d_k[j] = all_keys(own_part(to_k, i, keys) * scale)
                    if js[-1] == group - 1:
                        for base, parts in ((0, d_q), (width, d_k), (2 * width, d_v)):
                            some = [parts.pop(j) for j in range(group)]
                            dqkv_ref[group_rows(base, g), :size] = jnp.concatenate(
                                some, axis=0
                            ).astype(bf16)

        backward()

        if keys < block:
            mixed_ref[keys:] = tok_ref[keys:]
            dmix_ref[keys:] = cot_ref[keys:].astype(f32)
        if size < block:
            dqkv_ref[:, size:] = jnp.zeros((3 * width, block - size), bf16)

    half = block // 2

    @pl.when(length == 0)
    def _():
        mixed_ref[...] = tok_ref[...]
        dmix_ref[...] = cot_ref[...].astype(f32)
        dqkv_ref[...] = jnp.zeros_like(dqkv_ref)

    @pl.when((length > 0) & (length <= half))
    def _():
        run(half, half)

    more = half + half // 2

    @pl.when((length > half) & (length <= more))
    def _():
        run(block, more)

    @pl.when(length > more)
    def _():
        run(block, block)

    if packed:

        @pl.when(first)
        def _():
            mixed_out[...] = mixed_ref[...]

        @pl.when(jnp.logical_not(first))
        def _():
            mixed_odd[...] = mixed_ref[...]

    else:
        mixed_out[...] = mixed_ref[...]

    if packed:

        @pl.when(step == pl.num_programs(0) - 1)
        def _():
            columns = width // 2
            for i in range(DEVICES):
                p = (i % 2) * CHIPS + i // 2
                rows = slice(SHARD * i, SHARD * (i + 1))
                top = jnp.concatenate([gout_ref[rows], gback_ref[rows, :columns]], axis=1)
                bottom = jnp.concatenate([gin_ref[rows], gback_ref[rows, columns:]], axis=1)
                packed_ref[p] = jnp.concatenate([top, bottom], axis=0).astype(bf16)


def middle(lengths, qkv, tokens, cotangent, w_out, w_in, w_back, vectors, packed):
    slots, wide, block = qkv.shape
    rows, width = slots * block, wide // 3
    square = (width, width)
    shared = slots // 2

    def whole(shape):
        return pl.BlockSpec(shape, lambda m: (0,) * len(shape))

    by_rows = pl.BlockSpec((block, width), lambda m: (m, 0))
    if packed:
        first = pl.BlockSpec((block, width), lambda m: (2 * jnp.minimum(m, shared - 1), 0))
        second = pl.BlockSpec((block, width), lambda m: (jnp.maximum(m - shared, 0), 0))
    else:
        first = pl.BlockSpec((block, width), lambda m: (jnp.minimum(m, shared - 1), 0))
        second = pl.BlockSpec((block, width), lambda m: (jnp.maximum(m, shared), 0))
    out_specs = [
        by_rows,
        by_rows,
        pl.BlockSpec((3 * width, block), lambda m: (0, m)),
        whole((5, 8, width)),
    ]
    out_shape = [
        jax.ShapeDtypeStruct((rows, width), bf16),
        jax.ShapeDtypeStruct((rows, width), f32),
        jax.ShapeDtypeStruct((3 * width, rows), bf16),
        jax.ShapeDtypeStruct((5, 8, width), f32),
    ]
    scratch = [
        pltpu.VMEM((HEADS, block, block), bf16),
        pltpu.VMEM((width, block), f32),
        pltpu.VMEM((HEADS, 8, block), f32),
        pltpu.VMEM((width, block), bf16),
        pltpu.VMEM((block, width), bf16),
        pltpu.VMEM((block, width), bf16),
        pltpu.VMEM((block, width), bf16),
    ]
    if packed:
        shape = (DEVICES, 2 * SHARD, width + width // 2)
        out_specs[0] = first
        out_specs += [second, whole(shape)]
        out_shape.append(jax.ShapeDtypeStruct((rows // 2, width), bf16))
        out_shape.append(jax.ShapeDtypeStruct(shape, bf16))
        scratch = [pltpu.VMEM(square, f32)] * 3 + scratch
    else:
        out_specs += [whole(square)] * 3
        out_shape += [jax.ShapeDtypeStruct(square, f32)] * 3
    return pl.pallas_call(
        functools.partial(middle_kernel, packed, width // HEADS),
        grid=(slots,),
        in_specs=[
            pl.BlockSpec(memory_space=pltpu.SMEM),
            pl.BlockSpec((None, 3 * width, block), lambda m: (m, 0, 0)),
            first,
            second,
            first,
            second,
            whole(square),
            whole(square),
            whole(square),
            whole((16, width)),
        ],
        out_specs=out_specs,
        scratch_shapes=scratch,
        out_shape=out_shape,
        compiler_params=pltpu.CompilerParams(vmem_limit_bytes=58 * MIB),
    )(lengths, qkv, *tokens, *cotangent, w_out, w_in, w_back, vectors)


def scatter_kernel(
    sr_hbm,
    dqkv_hbm,
    unit_hbm,
    fq_hbm,
    tok_hbm,
    odd_hbm,
    dmix_hbm,
    mixed_hbm,
    vec_ref,
    gvec_ref,
    grad_hbm,
    grad_out,
    mixed_out,
    gq_ref,
    gr_ref,
    sq,
    sr,
    rq_sib,
    rr_sib,
    rq,
    rr,
    dqkv,
    unit_t,
    fq,
    tok,
    dmix,
    grad,
    mixed,
    gain_wide,
    shift_wide,
    small_wide,
    sums,
    result,
    send_sem,
    recv_sem,
    swap_send,
    swap_recv,
    copy_sem,
):
    at = Place()
    at.greet()
    rows, width = tok.shape
    wide = 3 * width
    half_q = wide // 2
    slots = 8
    block = rows // slots
    mine, theirs = at.c * CHIPS, (1 - at.c) * CHIPS
    own = at.block(at.c, at.z, at.y, at.x)
    level_rows = 8 * SHARD

    def local(src, dst, i):
        copy = pltpu.make_async_copy(src, dst, copy_sem.at[i])
        copy.start()
        return copy

    sr_in = local(sr_hbm, sr, 0)
    unit_in = local(unit_hbm, unit_t, 1)
    parts_in = []
    for part in range(3):
        some = pl.ds(part * width, width)
        parts_in.append(local(dqkv_hbm.at[some], dqkv.at[some], 2 + 2 * part))
        parts_in.append(local(fq_hbm.at[:, some], fq.at[:, some], 3 + 2 * part))

    def part_wait(part):
        for copy in parts_in[2 * part : 2 * part + 2]:
            copy.wait()

    shared = slots // 2

    def rows_of(i, count=1):
        return pl.ds(i * block, count * block)

    mixed_in = local(mixed_hbm, mixed, 8)
    late = [local(dmix_hbm, dmix, 9), local(odd_hbm, tok.at[rows_of(shared, shared)], 10)]
    for i in range(shared):
        late.append(local(tok_hbm.at[rows_of(2 * i)], tok.at[rows_of(i)], 11 + i))

    def swap_copy(src, dst, i):
        return pltpu.make_async_remote_copy(
            src_ref=src,
            dst_ref=dst,
            send_sem=swap_send.at[i],
            recv_sem=swap_recv.at[i],
            device_id=(at.sib,),
            device_id_type=MESH,
        )

    slabs = (
        (sq, rq_sib, rq, 0, 640),
        (sq, rq_sib, rq, 640, 640),
        (sr, rr_sib, rr, 0, 1152),
    )

    def cut(ref, k, first, count):
        return ref.at[pl.ds(first, count), :, pl.ds(slabs[k][3], slabs[k][4])]

    def piece(ref, k, p):
        _, _, _, column, columns = slabs[k]
        return ref[p, :, column : column + columns].astype(f32)

    def put(k, p, value):
        slab, _, _, column, columns = slabs[k]
        slab[p, :, column : column + columns] = value.astype(bf16)

    def remote(k, src, dst, target, sem):
        return pltpu.make_async_remote_copy(
            src_ref=src,
            dst_ref=dst,
            send_sem=send_sem.at[k],
            recv_sem=recv_sem.at[k, sem],
            device_id=(target,),
            device_id_type=MESH,
        )

    def x_type(j):
        return at.block(at.c, j, at.y, 1 - at.x)

    def y_type(j):
        return at.block(at.c, j, 1 - at.y, at.x)

    def corner_type(j):
        return at.block(at.c, j, 1 - at.y, 1 - at.x)

    def column_type(j):
        return at.block(at.c, j, at.y, at.x)

    def sib_copy(k, j):
        src = cut(slabs[k][0], k, theirs + 4 * j, 4)
        return remote(k, src, cut(slabs[k][1], k, 4 * j, 4), at.sib, j)

    def sib_send(k, j):
        sib_copy(k, j).start()

    def step_copy(k, src, slot, target):
        src = cut(slabs[k][0], k, src, 1)
        return remote(k, src, cut(slabs[k][2], k, slot, 1), target, PLANES + slot)

    def x_send(k, j):
        step_copy(k, x_type(j), 4 + j, at.xn).start()

    def y_send(k, j):
        step_copy(k, y_type(j), 8 + j, at.yn).start()

    def sib_add(k, j):
        sib_copy(k, j).wait_recv()

        def body(i, carry):
            p = mine + 4 * j + i
            put(k, p, piece(slabs[k][0], k, p) + piece(slabs[k][1], k, 4 * j + i))
            return carry

        lax.fori_loop(0, 4, body, 0)
        step_copy(k, corner_type(j), j, at.yn if j % 2 == 0 else at.xn).start()
        (y_send if j % 2 == 0 else x_send)(k, j)

    def corner_add(k, j):
        step_copy(k, own, j, at.sib).wait_recv()
        p = x_type(j) if j % 2 == 0 else y_type(j)
        put(k, p, piece(slabs[k][0], k, p) + piece(slabs[k][2], k, j))
        (x_send if j % 2 == 0 else y_send)(k, j)

    def plane_add(k, j):
        p = column_type(j)
        step_copy(k, own, 4 + j, at.sib).wait_recv()
        step_copy(k, own, 8 + j, at.sib).wait_recv()
        received = piece(slabs[k][2], k, 4 + j) + piece(slabs[k][2], k, 8 + j)
        put(k, p, piece(slabs[k][0], k, p) + received)

        @pl.when(at.z != j)
        def _():
            step_copy(k, p, 12 + at.z, at.me + 8 * (j - at.z)).start()

    def land(k):
        total = gq_ref if slabs[k][0] is sq else gr_ref
        columns = slice(slabs[k][3], slabs[k][3] + slabs[k][4])
        total[:, columns] = piece(slabs[k][0], k, own)
        for j in range(PLANES):

            @pl.when(at.z != j)
            def _():
                step_copy(k, own, 12 + j, at.sib).wait_recv()
                total[:, columns] += piece(slabs[k][2], k, 12 + j)

    def prepare(part):
        columns = slice(part * width, (part + 1) * width)
        sums[:, columns] = dot(jnp.ones((16, rows), bf16), dqkv[columns], 1, 1)[:8]
        if part == 0:
            gain_wide[...] = jnp.broadcast_to(vec_ref[0:1], (128, width)).T
            shift_wide[...] = jnp.broadcast_to(vec_ref[1:2], (128, width)).T
            small_wide[...] = jnp.zeros((width, 128), f32)
        if part == 2:
            lines = [jnp.zeros((2, width), f32), sums[0:1, :width], sums[0:1, 2 * width :]]
            lines += [jnp.sum(gvec_ref[i], axis=0, keepdims=True) for i in range(5)]
            lines.append(jnp.zeros((128 - VECTORS, width), f32))
            small_wide[...] += jnp.concatenate(lines, axis=0).T

    def weight_grad(j, part):
        lines = pl.ds(pl.multiple_of(j * level_rows, level_rows), level_rows)
        columns = pl.ds(pl.multiple_of(part * width, width), width)
        product = dot(unit_t[lines], dqkv[columns], 1, 1)
        weight = fq[lines, columns].astype(f32)
        line = sums[0:1, columns]
        gain_sum = jnp.sum(weight * product, axis=1, keepdims=True)
        shift_sum = jnp.sum(weight * line, axis=1, keepdims=True)
        lane = lax.broadcasted_iota(jnp.int32, (level_rows, 128), 1)
        small_wide[lines] += jnp.where(
            lane == 0, gain_sum, jnp.where(lane == 1, shift_sum, 0.0)
        )
        gain = jnp.concatenate([gain_wide[lines]] * (width // 128), axis=1)
        shift = jnp.concatenate([shift_wide[lines]] * (width // 128), axis=1)
        result[:, columns] = gain * product + shift * line

        @pl.when(part == 2)
        def _():
            small = small_wide[lines]
            blank = jnp.zeros((SHARD, 128), f32)
            for i in range(8):
                p = (i % 2) * CHIPS + 4 * j + i // 2
                some = slice(SHARD * i, SHARD * (i + 1))
                top = jnp.concatenate([result[some, :half_q], small[some]], axis=1)
                bottom = jnp.concatenate([result[some, half_q:], blank], axis=1)
                sq[p] = jnp.concatenate([top, bottom], axis=0).astype(bf16)

    def grad_rows(m):
        return pl.ds(pl.multiple_of(m * block, block), block)

    def grad_copy(m):
        return pltpu.make_async_copy(
            grad.at[grad_rows(m)], grad_hbm.at[grad_rows(m)], copy_sem.at[11 + shared + m]
        )

    def input_grad(m):
        some = grad_rows(m)
        d_normed = dot(fq[...], dqkv[:, some], 1, 0).T
        unit, factor = normalize(tok[some].astype(f32))
        share = norm_backward(d_normed, vec_ref[0:1], unit, factor)
        grad[some] = (dmix[some] + share).astype(bf16)

        @pl.when(m < shared)
        def _():
            grad_copy(m).start()

        @pl.when(m >= shared)
        def _():
            swap_copy(grad.at[some], grad_out.at[grad_rows(m - shared)], 0).start()

    def late_wait():
        for copy in late:
            copy.wait()

    sr_in.wait()
    at.await_all()
    sib_send(2, 2)
    sib_send(2, 1)
    sib_send(2, 0)
    sib_add(2, 2)
    sib_send(2, 3)
    sib_add(2, 1)
    unit_in.wait()
    part_wait(0)
    prepare(0)
    sib_add(2, 0)
    part_wait(1)
    sib_add(2, 3)
    prepare(1)

    def beside_weight_0():
        part_wait(2)
        prepare(2)

    def beside_weight_2():
        sib_send(1, 0)

    def beside_weight_4():
        corner_add(2, 0)
        corner_add(2, 1)
        sib_send(0, 0)

    def beside_weight_5():
        sib_send(0, 3)
        corner_add(2, 3)

    def beside_weight_6():
        corner_add(2, 2)

    def beside_weight_7():
        sib_add(0, 0)
        sib_add(0, 3)
        plane_add(2, 0)

    def beside_weight_8():
        sib_send(0, 1)
        sib_add(1, 0)
        plane_add(2, 3)

    def beside_weight_9():
        sib_add(0, 1)

    def beside_weight_10():
        corner_add(0, 3)
        sib_send(1, 3)


    def beside_weight_step(i, carry):
        turn = i // 3
        j = jnp.where(turn == 0, 0, jnp.where(turn == 1, 3, jnp.where(turn == 2, 1, 2)))
        weight_grad(j, lax.rem(i, 3))
        pl.when(i == 0)(beside_weight_0)
        pl.when(i == 2)(beside_weight_2)
        pl.when(i == 4)(beside_weight_4)
        pl.when(i == 5)(beside_weight_5)
        pl.when(i == 6)(beside_weight_6)
        pl.when(i == 7)(beside_weight_7)
        pl.when(i == 8)(beside_weight_8)
        pl.when(i == 9)(beside_weight_9)
        pl.when(i == 10)(beside_weight_10)
        return carry

    lax.fori_loop(0, 12, beside_weight_step, 0)
    corner_add(0, 0)
    sib_send(1, 2)
    plane_add(2, 2)
    sib_send(0, 2)
    corner_add(0, 1)
    plane_add(2, 1)
    sib_add(1, 3)
    sib_send(1, 1)
    mixed_in.wait()
    swap_copy(mixed, mixed_out, 1).start()
    late_wait()
    sib_add(1, 2)
    plane_add(0, 3)
    corner_add(1, 0)
    sib_add(0, 2)

    def beside_input_0():
        plane_add(0, 0)
        corner_add(1, 3)
        corner_add(1, 2)
        sib_add(1, 1)
        plane_add(0, 1)

    def beside_input_1():
        corner_add(0, 2)
        plane_add(1, 2)
        plane_add(1, 0)

    def beside_input_2():
        corner_add(1, 1)
        plane_add(1, 3)

    def beside_input_4():
        plane_add(0, 2)
        plane_add(1, 1)

    def beside_input_6():
        land(2)


    def beside_input_step(i, carry):
        input_grad(i)
        pl.when(i == 0)(beside_input_0)
        pl.when(i == 1)(beside_input_1)
        pl.when(i == 2)(beside_input_2)
        pl.when(i == 4)(beside_input_4)
        pl.when(i == 6)(beside_input_6)
        return carry

    lax.fori_loop(0, 8, beside_input_step, 0)
    land(0)
    land(1)
    for k in range(len(slabs)):
        every = cut(slabs[k][0], k, 0, DEVICES - 1)
        remote(k, every, every, at.sib, 0).wait_send()
    for m in range(shared):
        grad_copy(m).wait()
    swap_copy(grad.at[rows_of(shared, shared)], grad_out, 0).wait()
    swap_copy(mixed, mixed_out, 1).wait()


def scatter(packed, dqkv, unit_t, full_qkv, tokens, odd_tokens, d_mixed, mixed, vectors, sums):
    rows, width = tokens.shape
    wide = 3 * width
    vmem = pl.BlockSpec(memory_space=pltpu.VMEM)
    anywhere = pl.BlockSpec(memory_space=pl.ANY)
    tall = 2 * SHARD
    widths = (wide // 2 + 128, wide // 2)
    return pl.pallas_call(
        scatter_kernel,
        out_shape=[jax.ShapeDtypeStruct((rows // 2, width), bf16)] * 3
        + [jax.ShapeDtypeStruct((tall, w), f32) for w in widths],
        in_specs=[anywhere] * 8 + [vmem] * 2,
        out_specs=[anywhere] * 3 + [vmem] * 2,
        scratch_shapes=[pltpu.VMEM((DEVICES, tall, w), bf16) for w in widths]
        + [pltpu.VMEM((CHIPS, tall, w), bf16) for w in widths]
        + [pltpu.VMEM((4 * PLANES, tall, w), bf16) for w in widths]
        + [
            pltpu.VMEM((wide, rows), bf16),
            pltpu.VMEM((width, rows), bf16),
            pltpu.VMEM((width, wide), bf16),
            pltpu.VMEM((rows, width), bf16),
            pltpu.VMEM((rows, width), f32),
            pltpu.VMEM((rows, width), bf16),
            pltpu.VMEM((rows // 2, width), bf16),
            pltpu.VMEM((width, 128), f32),
            pltpu.VMEM((width, 128), f32),
            pltpu.VMEM((width, 128), f32),
            pltpu.VMEM((8, wide), f32),
            pltpu.VMEM((8 * SHARD, wide), f32),
            pltpu.SemaphoreType.DMA((3,)),
            pltpu.SemaphoreType.DMA((3, 5 * PLANES)),
            pltpu.SemaphoreType.DMA((2,)),
            pltpu.SemaphoreType.DMA((2,)),
            pltpu.SemaphoreType.DMA((19,)),
        ],
        compiler_params=pltpu.CompilerParams(
            collective_id=1, has_side_effects=True, vmem_limit_bytes=60 * MIB
        ),
    )(packed, dqkv, unit_t, full_qkv, tokens, odd_tokens, d_mixed, mixed, vectors, sums)


def finish_kernel(
    _, mixed_odd, grad_even, grad_odd, q_ref, r_ref, mixed, grad, g_qkv, g_out, g_in, g_back, *lines
):
    block = mixed_odd.shape[0]
    mixed[...] = mixed_odd[...]
    grad[:block] = grad_even[...]
    grad[block:] = grad_odd[...]

    @pl.when(pl.program_id(0) == 0)
    def _():
        width = g_out.shape[1]
        half_q = 3 * width // 2
        half = width // 2
        g_qkv[:, :half_q] = q_ref[:SHARD, :half_q]
        g_qkv[:, half_q:] = q_ref[SHARD:, :half_q]
        g_out[...] = r_ref[:SHARD, :width]
        g_in[...] = r_ref[SHARD:, :width]
        g_back[:, :half] = r_ref[:SHARD, width:]
        g_back[:, half:] = r_ref[SHARD:, width:]
        small = q_ref[:SHARD, half_q:].T
        for i, line in enumerate(lines):
            line[...] = small[i, :SHARD]


def finish(mixed, mixed_odd, grad, grad_odd, q_part, r_part, slots):
    rows, width = mixed.shape
    block = rows // slots
    single = pl.BlockSpec((block, width), lambda i: (i, 0))
    double = pl.BlockSpec((2 * block, width), lambda i: (i, 0))

    def whole(shape):
        return pl.BlockSpec(shape, lambda i: (0,) * len(shape))

    shapes = [(SHARD, 3 * width)] + [(SHARD, width)] * 3 + [(SHARD,)] * 9
    return pl.pallas_call(
        finish_kernel,
        grid=(slots // 2,),
        out_shape=[jax.ShapeDtypeStruct((rows, width), bf16)] * 2
        + [jax.ShapeDtypeStruct(s, f32) for s in shapes],
        in_specs=[pl.BlockSpec(memory_space=pl.ANY)]
        + [single] * 3
        + [whole(q_part.shape), whole(r_part.shape)],
        out_specs=[pl.BlockSpec((block, width), lambda i: (2 * i + 1, 0)), double]
        + [whole(s) for s in shapes],
        input_output_aliases={0: 0},
    )(mixed, mixed_odd, grad, grad_odd, q_part, r_part)


def on_one_plan(tokens, mol_len, cotangent, vectors, w_qkv, w_out, w_in, w_back):
    slots = mol_len.shape[0]
    (
        qkv,
        unit_t,
        full_qkv,
        full_out,
        full_in,
        full_back,
        odd_tokens,
        odd_cotangent,
        lines,
        lengths,
    ) = gather_and_project(mol_len, vectors, w_qkv, w_out, w_in, w_back, tokens, cotangent)
    mixed, d_mixed, dqkv, sums, mixed_sent, packed = middle(
        lengths,
        qkv,
        (tokens, odd_tokens),
        (cotangent, odd_cotangent),
        full_out,
        full_in,
        full_back,
        lines,
        True,
    )
    grad, grad_odd, mixed_odd, q_part, r_part = scatter(
        packed, dqkv, unit_t, full_qkv, tokens, odd_tokens, d_mixed, mixed_sent, lines, sums
    )
    mixed_out, token_grad, g_qkv, g_out, g_in, g_back, *small = finish(
        mixed, mixed_odd, grad, grad_odd, q_part, r_part, slots
    )
    return mixed_out, token_grad, small, g_qkv, g_out, g_in, g_back


def on_any_plan(tokens, mol_len, cotangent, vectors, w_qkv, w_out, w_in, w_back):
    slots = mol_len.shape[0]
    rows, width = tokens.shape

    def gather(array, axis):
        return lax.all_gather(array, "fsdp", axis=axis, tiled=True)

    lines = gather(jnp.stack(vectors), 1).astype(f32)
    lines = jnp.pad(lines, ((0, 16 - len(vectors)), (0, 0)))
    full_qkv, full_out, full_in, full_back = (
        gather(w, 0) for w in (w_qkv, w_out, w_in, w_back)
    )
    unit, factor = normalize(tokens.astype(f32))
    normed = (unit * lines[0] + lines[1]).astype(bf16)
    qkv = jnp.dot(normed, full_qkv, preferred_element_type=f32)
    qkv = (qkv + jnp.concatenate([lines[2], jnp.zeros_like(lines[2]), lines[3]])).astype(bf16)
    qkv = qkv.reshape(slots, rows // slots, 3 * width).transpose(0, 2, 1)
    mixed_out, d_mixed, dqkv, sums, g_out, g_in, g_back = middle(
        jnp.broadcast_to(mol_len[:, None], (slots, 128)),
        qkv,
        (tokens, tokens),
        (cotangent, cotangent),
        full_out,
        full_in,
        full_back,
        lines,
        False,
    )
    g_qkv = jnp.einsum("rf,dr->fd", normed, dqkv, preferred_element_type=f32)
    d_normed = jnp.einsum("dr,fd->rf", dqkv, full_qkv, preferred_element_type=f32)
    totals = jnp.sum(dqkv.astype(f32), axis=1)
    small = [jnp.sum(d_normed * unit, axis=0), jnp.sum(d_normed, axis=0)]
    small += [totals[:width], totals[2 * width :]]
    small += [jnp.sum(sums[i], axis=0) for i in range(5)]
    share = norm_backward(d_normed, lines[0], unit, factor)
    token_grad = (d_mixed + share).astype(bf16)

    def scatter_sum(array, axis):
        return lax.psum_scatter(array, "fsdp", scatter_dimension=axis, tiled=True)

    small = scatter_sum(jnp.stack(small), 1)
    return (
        mixed_out,
        token_grad,
        [small[i] for i in range(9)],
        *(scatter_sum(g, 0) for g in (g_qkv, g_out, g_in, g_back)),
    )


def per_device(
    devices,
    tokens,
    mol_len,
    cotangent,
    ln1_gain,
    ln1_bias,
    w_qkv,
    q_bias,
    v_bias,
    w_out,
    out_bias,
    ln2_gain,
    ln2_bias,
    w_in,
    in_bias,
    w_back,
    back_bias,
):
    vectors = [
        ln1_gain,
        ln1_bias,
        q_bias,
        v_bias,
        out_bias,
        ln2_gain,
        ln2_bias,
        in_bias,
        back_bias,
    ]
    known = devices == DEVICES and w_qkv.shape[0] == SHARD
    plan = on_one_plan if known else on_any_plan
    mixed_out, token_grad, small, g_qkv, g_out, g_in, g_back = plan(
        tokens, mol_len, cotangent, vectors, w_qkv, w_out, w_in, w_back
    )
    return (
        mixed_out,
        token_grad,
        small[0],
        small[1],
        g_qkv,
        small[2],
        small[3],
        g_out,
        small[4],
        small[5],
        small[6],
        g_in,
        small[7],
        g_back,
        small[8],
    )


def solution(mesh):
    line, matrix = P("fsdp"), P("fsdp", None)
    return jax.shard_map(
        functools.partial(per_device, mesh.shape["fsdp"]),
        mesh=mesh,
        in_specs=(
            matrix,
            line,
            matrix,
            line,
            line,
            matrix,
            line,
            line,
            matrix,
            line,
            line,
            line,
            matrix,
            line,
            matrix,
            line,
        ),
        out_specs=(
            matrix,
            matrix,
            line,
            line,
            matrix,
            line,
            line,
            matrix,
            line,
            line,
            line,
            matrix,
            line,
            matrix,
            line,
        ),
        check_vma=False,
    )
```

```python
import functools

import jax
import jax.numpy as jnp
from jax import lax
from jax.experimental import pallas as pl
from jax.experimental.pallas import tpu as pltpu
from jax.sharding import PartitionSpec as P

HEADS = 32

bf16 = jnp.bfloat16
f32 = jnp.float32
eps = 1e-05
masked_score = -1e30
log2_e = 1.4426950408889634
MESH = pl.DeviceIdType.MESH
MIB = 1 << 20

PLANES = 4
CHIPS = 4 * PLANES
DEVICES = 2 * CHIPS
SHARD = 24
VECTORS = 9
COPIES = 8


def dot(left, right, left_dim, right_dim):
    return lax.dot_general(
        left, right, (((left_dim,), (right_dim,)), ((), ())), preferred_element_type=f32
    )


def normalize(values):
    centred = values - jnp.mean(values, axis=-1, keepdims=True)
    factor = lax.rsqrt(jnp.mean(centred * centred, axis=-1, keepdims=True) + eps)
    return centred * factor, factor


def norm_backward(d_normed, gain, unit, factor):
    e = d_normed * gain
    inner = jnp.mean(e * unit, axis=-1, keepdims=True)
    return factor * (e - jnp.mean(e, axis=-1, keepdims=True) - unit * inner)


def fold_rows(values):
    rows, columns = values.shape
    return jnp.sum(values.reshape(rows // 8, 8, columns), axis=0)


class Place:
    def __init__(self):
        me = lax.axis_index("fsdp")
        self.me = me
        self.c = lax.rem(me, 2)
        self.x = lax.rem(me // 2, 2)
        self.y = lax.rem(me // 4, 2)
        self.z = me // 8
        self.sib = me + 1 - 2 * self.c
        self.xn = me + 2 - 4 * self.x
        self.yn = me + 4 - 8 * self.y

    def block(self, c, z, y, x):
        return ((c * PLANES + z) * 2 + y) * 2 + x

    def greet(self):
        sem = pltpu.get_barrier_semaphore()

        def signal(device):
            pl.semaphore_signal(sem, inc=1, device_id=(device,), device_id_type=MESH)

        for device in (self.sib, self.xn, self.yn):
            signal(device)
        for distance in range(1, PLANES):
            signal(lax.rem(self.me + 8 * distance, DEVICES))

    def await_all(self):
        pl.semaphore_wait(pltpu.get_barrier_semaphore(), 2 + PLANES)


def gather_kernel(
    len_ref,
    *refs,
):
    lines, refs = refs[:VECTORS], refs[VECTORS:]
    gather_body(len_ref, lines, *refs)


def gather_body(
    len_ref,
    lines,
    wq_ref,
    wo_ref,
    wi_ref,
    wb_ref,
    tok_in,
    cot_hbm,
    qkv_hbm,
    unit_hbm,
    fq_hbm,
    fo_hbm,
    fi_hbm,
    fb_hbm,
    tok_hbm,
    cot_out,
    vec_ref,
    work_ref,
    gq,
    gr,
    fq,
    fo,
    fi,
    fb,
    fq_t,
    unit,
    unit_t,
    qkv,
    bias,
    tok_ref,
    tok_odd,
    cot_odd,
    len_send,
    len_recv,
    send_sem,
    recv_sem,
    swap_send,
    swap_recv,
    slot_sem,
    copy_sem,
):
    at = Place()
    at.greet()
    width = tok_ref.shape[1]
    slots, _, block = qkv.shape
    slot_in = [
        pltpu.make_async_copy(
            tok_in.at[pl.ds(i * block, block)], tok_ref.at[pl.ds(i * block, block)], slot_sem.at[i]
        )
        for i in range(slots)
    ]
    for i in [0, 2] + list(range(1, slots, 2)) + list(range(4, slots, 2)):
        slot_in[i].start()
    shared = slots // 2
    half_q = 3 * width // 2
    half = width // 2
    own = at.block(at.c, at.z, at.y, at.x)
    mine, theirs = at.c * CHIPS, (1 - at.c) * CHIPS
    slabs = ((gq, 0, 384), (gq, 384, 384), (gq, 768, 512), (gr, 0, 640), (gr, 640, 512))

    small = [line[...].astype(f32).reshape(1, SHARD) for line in lines]
    small = jnp.concatenate(small + [jnp.zeros((2 * SHARD - VECTORS, SHARD), f32)], axis=0)
    small = jnp.concatenate([small, jnp.zeros((2 * SHARD, 128 - SHARD), f32)], axis=1).astype(bf16)
    gq[own] = jnp.concatenate(
        [
            jnp.concatenate([wq_ref[:, :half_q], wq_ref[:, half_q:]], axis=0),
            small,
        ],
        axis=1,
    )
    gr[own] = jnp.concatenate(
        [
            jnp.concatenate([wo_ref[...], wi_ref[...]], axis=0),
            jnp.concatenate([wb_ref[:, :half], wb_ref[:, half:]], axis=0),
        ],
        axis=1,
    )

    def view(k, first, count):
        slab, column, columns = slabs[k]
        return slab.at[pl.ds(first, count), :, pl.ds(column, columns)]

    def remote(k, first, target, sem, count=1):
        return pltpu.make_async_remote_copy(
            src_ref=view(k, first, count),
            dst_ref=view(k, first, count),
            send_sem=send_sem.at[k],
            recv_sem=recv_sem.at[k, sem],
            device_id=(target,),
            device_id_type=MESH,
        )

    def send(k, b, target):
        remote(k, b, target, lax.rem(b, CHIPS)).start()

    def to_sib(k, b):
        remote(k, b, at.sib, CHIPS).start()

    def arrived(k, b):
        remote(k, b, at.sib, lax.rem(b, CHIPS)).wait_recv()

    def at_level(shift, body):
        level = at.z + shift
        if shift == 0:
            body(level)
        else:
            pl.when((level >= 0) & (level <= PLANES - 1))(lambda: body(level))

    def both(s):
        return (0,) if s == 0 else (-s, s)

    def own_plane(k):
        send(k, own, at.xn)
        send(k, own, at.yn)

    def own_column(k):
        for s in range(1, PLANES):
            for shift in both(s):
                at_level(shift, lambda level, shift=shift: send(k, own, at.me + 8 * shift))
        to_sib(k, own)

    def column(k, s):
        def body(level):
            b = at.block(at.c, level, at.y, at.x)
            arrived(k, b)
            send(k, b, at.xn)
            send(k, b, at.yn)
            to_sib(k, b)

        for shift in both(s):
            at_level(shift, body)

    def plane(k, s):
        def body(level):
            even = lax.rem(level, 2) == 0
            b = at.block(at.c, level, at.y, 1 - at.x)
            arrived(k, b)
            pl.when(even)(lambda: send(k, b, at.yn))
            to_sib(k, b)
            d = at.block(at.c, level, 1 - at.y, at.x)
            arrived(k, d)
            pl.when(jnp.logical_not(even))(lambda: send(k, d, at.xn))
            to_sib(k, d)

        for shift in both(s):
            at_level(shift, body)

    def corner(k):
        for j in range(PLANES):
            b = at.block(at.c, j, 1 - at.y, 1 - at.x)
            arrived(k, b)
            to_sib(k, b)

    def others(k):
        remote(k, theirs, at.sib, CHIPS, CHIPS).wait_recv()

    def rows_of(i):
        return pl.ds(i * block, block)

    cot_in = [
        pltpu.make_async_copy(
            cot_hbm.at[rows_of(2 * i + 1)], cot_odd.at[rows_of(i)], swap_recv.at[6 + i]
        )
        for i in range(shared)
    ]

    def swap_copy(src, dst, send, recv):
        return pltpu.make_async_remote_copy(
            src_ref=src,
            dst_ref=dst,
            send_sem=swap_send.at[send],
            recv_sem=swap_recv.at[recv],
            device_id=(at.sib,),
            device_id_type=MESH,
        )

    def tok_copy(i):
        return swap_copy(tok_ref.at[rows_of(2 * i + 1)], tok_odd.at[rows_of(i)], 0, i)

    def swap_start():
        swap_copy(len_send, len_recv, 2, 5).start()
        for i in range(shared):
            slot_in[2 * i + 1].wait()
            tok_copy(i).start()
        for i in range(shared):
            cot_in[i].wait()
            swap_copy(cot_odd.at[rows_of(i)], cot_out.at[rows_of(i)], 1, 4).start()

    def swap_end():
        swap_copy(len_send, len_recv, 2, 5).wait()
        swap_copy(tok_odd, tok_odd, 0, 0).wait_send()
        swap_copy(cot_odd, cot_out, 1, 4).wait()
        place = lax.broadcasted_iota(jnp.int32, (shared, 128), 0)
        own_lengths = jnp.zeros((shared, 128), jnp.int32)
        odd_lengths = jnp.zeros((shared, 128), jnp.int32)
        for i in range(shared):
            own_lengths = jnp.where(place == i, len_send[2 * i : 2 * i + 1], own_lengths)
            odd_lengths = jnp.where(place == i, len_recv[2 * i + 1 : 2 * i + 2], odd_lengths)
        work_ref[:shared] = own_lengths
        work_ref[shared:] = odd_lengths

    for i in range(slots):
        len_send[i : i + 1] = jnp.full((1, 128), len_ref[i], jnp.int32)
    for copy in cot_in:
        copy.start()

    def norm_step(m):
        rows = rows_of(m)
        if m < shared:
            slot_in[2 * m].wait()
            here = tok_ref[rows_of(2 * m)]
        else:
            tok_copy(m - shared).wait_recv()
            here = tok_odd[rows_of(m - shared)]
        size = block // 2
        for i in range(2):
            some = pl.ds(m * block + i * size, size)
            values, _ = normalize(here[i * size : (i + 1) * size].astype(f32))
            unit[some] = values
            unit_t[:, some] = values.astype(bf16).T

    def strip(i):
        return pl.ds(pl.multiple_of(i * 2 * SHARD, 2 * SHARD), 2 * SHARD)

    def stack(first, second):
        return jnp.concatenate([first, second], axis=0).astype(bf16)

    def build_q():
        def body(i, carry):
            first = gq[i].astype(f32)
            second = gq[CHIPS + i].astype(f32)
            fq[strip(i), :half_q] = stack(first[:SHARD, :half_q], second[:SHARD, :half_q])
            fq[strip(i), half_q:] = stack(first[SHARD:, :half_q], second[SHARD:, :half_q])
            return carry

        lax.fori_loop(0, CHIPS, body, 0)
        out(fq, fq_hbm)

    def build_r():
        def body(i, carry):
            first = gr[i].astype(f32)
            second = gr[CHIPS + i].astype(f32)
            fo[strip(i)] = stack(first[:SHARD, :width], second[:SHARD, :width])
            fi[strip(i)] = stack(first[SHARD:, :width], second[SHARD:, :width])
            fb[strip(i), :half] = stack(first[:SHARD, width:], second[:SHARD, width:])
            fb[strip(i), half:] = stack(first[SHARD:, width:], second[SHARD:, width:])
            return carry

        lax.fori_loop(0, CHIPS, body, 0)
        out(fo, fo_hbm)
        out(fi, fi_hbm)
        out(fb, fb_hbm)

    copies = []

    def out(src, dst):
        copy = pltpu.make_async_copy(src, dst, copy_sem.at[len(copies)])
        copy.start()
        copies.append(copy)

    def turn(part):
        columns = slice(part * width, (part + 1) * width)
        fq_t[columns] = fq[:, columns].T

    def spread_vectors():
        column_at = lax.broadcasted_iota(jnp.int32, (128, width), 1)
        entry = lax.broadcasted_iota(jnp.int32, (128, width), 0)
        spread = jnp.where(lax.rem(column_at, SHARD) == entry, 1.0, 0.0).astype(bf16)
        stacked = jnp.concatenate([gq[p, :16, half_q:] for p in range(DEVICES)], axis=0)
        wide = dot(stacked, spread, 1, 0)
        total = jnp.zeros((16, width), f32)
        column_at = lax.broadcasted_iota(jnp.int32, (16, width), 1)
        for p in range(DEVICES):
            first = SHARD * ((p % CHIPS) * 2 + p // CHIPS)
            here = (column_at >= first) & (column_at < first + SHARD)
            total = total + jnp.where(here, wide[16 * p : 16 * p + 16], 0.0)
        vec_ref[...] = total
        bias[:width] = jnp.broadcast_to(total[2:3], (128, width)).T
        bias[width : 2 * width] = jnp.zeros((width, 128), f32)
        bias[2 * width :] = jnp.broadcast_to(total[3:4], (128, width)).T

    def qkv_copy(m):
        return pltpu.make_async_copy(qkv.at[m], qkv_hbm.at[m], copy_sem.at[COPIES + m])

    def qkv_part(m, part):
        here = unit[pl.ds(pl.multiple_of(m * block, block), block)]
        normed = (here * vec_ref[0:1] + vec_ref[1:2]).astype(bf16)
        lines = pl.ds(pl.multiple_of(part * width, width), width)
        result = dot(fq_t[lines], normed, 1, 1)
        added = jnp.concatenate([bias[lines]] * (block // 128), axis=1)
        qkv[m, lines] = (result + added).astype(bf16)
        pl.when(part == 2)(lambda: qkv_copy(m).start())

    norm_step(0)
    norm_step(1)
    at.await_all()
    own_column(0)
    own_column(1)
    own_plane(1)
    own_plane(2)
    norm_step(2)
    own_plane(4)
    own_plane(3)
    swap_start()
    own_column(2)
    own_plane(0)
    column(0, 3)
    column(0, 2)
    plane(1, 0)
    column(0, 1)
    plane(0, 3)
    plane(0, 0)
    own_column(3)
    column(1, 3)
    own_column(4)
    column(1, 1)
    norm_step(3)
    norm_step(4)
    column(1, 2)
    plane(2, 0)
    plane(0, 1)
    plane(1, 3)
    norm_step(5)
    norm_step(6)
    column(2, 3)
    column(2, 1)
    column(2, 2)
    plane(1, 2)
    plane(1, 1)
    norm_step(7)
    plane(0, 2)
    plane(2, 1)
    plane(2, 3)
    plane(2, 2)
    corner(1)
    column(3, 3)
    corner(0)
    plane(3, 0)
    corner(2)
    column(3, 2)
    others(1)
    others(0)
    plane(4, 0)
    column(3, 1)
    others(2)
    column(4, 3)
    build_q()
    plane(3, 3)
    column(4, 1)
    turn(0)
    turn(1)
    turn(2)
    spread_vectors()
    column(4, 2)

    def beside_qkv_6():
        plane(3, 2)

    def beside_qkv_7():
        plane(3, 1)

    def beside_qkv_8():
        plane(4, 1)

    def beside_qkv_11():
        plane(4, 2)
        plane(4, 3)

    def beside_qkv_14():
        corner(3)

    def beside_qkv_19():
        corner(4)

    def beside_qkv_22():
        others(4)
        others(3)


    def beside_qkv_step(i, carry):
        qkv_part(i // 3, lax.rem(i, 3))
        pl.when(i == 6)(beside_qkv_6)
        pl.when(i == 7)(beside_qkv_7)
        pl.when(i == 8)(beside_qkv_8)
        pl.when(i == 11)(beside_qkv_11)
        pl.when(i == 14)(beside_qkv_14)
        pl.when(i == 19)(beside_qkv_19)
        pl.when(i == 22)(beside_qkv_22)
        return carry

    lax.fori_loop(0, 24, beside_qkv_step, 0)
    build_r()
    out(unit_t, unit_hbm)
    out(tok_odd, tok_hbm)
    swap_end()
    for k in range(len(slabs)):
        remote(k, 0, at.sib, 0, DEVICES - 1).wait_send()
    for copy in copies:
        copy.wait()
    for m in range(slots):
        qkv_copy(m).wait()


def gather_and_project(mol_len, vectors, w_qkv, w_out, w_in, w_back, tokens, cotangent):
    slots = mol_len.shape[0]
    rows, width = tokens.shape
    block = rows // slots
    wide = 3 * width
    vmem = pl.BlockSpec(memory_space=pltpu.VMEM)
    anywhere = pl.BlockSpec(memory_space=pl.ANY)
    square = (width, width)
    return pl.pallas_call(
        gather_kernel,
        out_shape=[
            jax.ShapeDtypeStruct((slots, wide, block), bf16),
            jax.ShapeDtypeStruct((width, rows), bf16),
            jax.ShapeDtypeStruct((width, wide), bf16),
            jax.ShapeDtypeStruct(square, bf16),
            jax.ShapeDtypeStruct(square, bf16),
            jax.ShapeDtypeStruct(square, bf16),
            jax.ShapeDtypeStruct((rows // 2, width), bf16),
            jax.ShapeDtypeStruct((rows // 2, width), bf16),
            jax.ShapeDtypeStruct((16, width), f32),
            jax.ShapeDtypeStruct((slots, 128), jnp.int32),
        ],
        in_specs=[pl.BlockSpec(memory_space=pltpu.SMEM)] + [vmem] * (VECTORS + 4) + [anywhere] * 2,
        out_specs=[anywhere] * 8 + [vmem] * 2,
        scratch_shapes=[
            pltpu.VMEM((DEVICES, 2 * SHARD, wide // 2 + 128), bf16),
            pltpu.VMEM((DEVICES, 2 * SHARD, wide // 2), bf16),
            pltpu.VMEM((width, wide), bf16),
            pltpu.VMEM(square, bf16),
            pltpu.VMEM(square, bf16),
            pltpu.VMEM(square, bf16),
            pltpu.VMEM((wide, width), bf16),
            pltpu.VMEM((rows, width), f32),
            pltpu.VMEM((width, rows), bf16),
            pltpu.VMEM((slots, wide, block), bf16),
            pltpu.VMEM((wide, 128), f32),
            pltpu.VMEM((rows, width), bf16),
            pltpu.VMEM((rows // 2, width), bf16),
            pltpu.VMEM((rows // 2, width), bf16),
            pltpu.VMEM((slots, 128), jnp.int32),
            pltpu.VMEM((slots, 128), jnp.int32),
            pltpu.SemaphoreType.DMA((5,)),
            pltpu.SemaphoreType.DMA((5, CHIPS + 1)),
            pltpu.SemaphoreType.DMA((3,)),
            pltpu.SemaphoreType.DMA((6 + slots // 2,)),
            pltpu.SemaphoreType.DMA((slots,)),
            pltpu.SemaphoreType.DMA((COPIES + slots,)),
        ],
        compiler_params=pltpu.CompilerParams(
            collective_id=0, has_side_effects=True, vmem_limit_bytes=60 * MIB
        ),
    )(mol_len, *vectors, w_qkv, w_out, w_in, w_back, tokens, cotangent)


def middle_kernel(
    packed,
    head_dim,
    len_ref,
    qkv_ref,
    tok_first,
    tok_second,
    cot_first,
    cot_second,
    wout_hbm,
    win_hbm,
    wback_hbm,
    vec_ref,
    mixed_out,
    dmix_ref,
    dqkv_ref,
    gvec_ref,
    *rest,
):
    if packed:
        mixed_odd, packed_ref, gout_ref, gin_ref, gback_ref, *rest = rest
    else:
        gout_ref, gin_ref, gback_ref, *rest = rest
    probs, ctx_s, linv_s, dctx_s, tok_ref, cot_ref, mixed_ref, *rest = rest
    wout_ref, win_ref, wback_ref, weight_sem = rest
    step = pl.program_id(0)
    block, width = tok_ref.shape
    slot = 32
    group = 4
    heads = width // head_dim
    span = group * head_dim
    scale = head_dim ** (-0.5)
    length = len_ref[step, 0]
    first = step < pl.num_programs(0) // 2
    tok_ref[...] = jnp.where(first, tok_first[...], tok_second[...])
    cot_ref[...] = jnp.where(first, cot_first[...], cot_second[...])

    weight_copies = [
        pltpu.make_async_copy(src, dst, weight_sem.at[i])
        for i, (src, dst) in enumerate(
            ((wout_hbm, wout_ref), (win_hbm, win_ref), (wback_hbm, wback_ref))
        )
    ]

    def await_weights():
        for copy in weight_copies:
            copy.wait()

    @pl.when(step == 0)
    def _():
        for copy in weight_copies:
            copy.start()
        gout_ref[...] = jnp.zeros_like(gout_ref)
        gin_ref[...] = jnp.zeros_like(gin_ref)
        gback_ref[...] = jnp.zeros_like(gback_ref)
        gvec_ref[...] = jnp.zeros_like(gvec_ref)

    def run(size, keys):
        extra = (slot - head_dim, size)
        sub = lax.broadcasted_iota(jnp.int32, extra, 0)
        lane = lax.broadcasted_iota(jnp.int32, extra, 1)
        one_row = jnp.where(sub == 0, 1.0, 0.0).astype(f32)
        two_rows = jnp.where(sub <= 1, 1.0, 0.0).astype(f32)
        mask_row = jnp.where((sub == 0) & (lane >= length), masked_score, 0.0).astype(f32)

        def group_rows(base, g):
            return slice(base + g * span, base + (g + 1) * span)

        def load(base, g):
            return qkv_ref[group_rows(base, g), :size].astype(f32)

        def place(j, rows):
            parts = []
            if j > 0:
                parts.append(jnp.zeros((slot * j, size), bf16))
            parts.append(rows)
            if j < group - 1:
                parts.append(jnp.zeros((slot * (group - 1 - j), size), bf16))
            return jnp.concatenate(parts, axis=0)

        def pieces(values):
            return [values[head_dim * j : head_dim * (j + 1)] for j in range(group)]

        def padded(values, tail):
            return [jnp.concatenate([p, tail], axis=0).astype(bf16) for p in pieces(values)]

        together = 1 if size == block else 2
        units = heads // together
        ahead = 3 if size == block else 6

        def beside(parts):
            return parts[0] if together == 1 else jnp.concatenate(parts, axis=1)

        def below(parts):
            return parts[0] if together == 1 else jnp.concatenate(parts, axis=0)

        def stacked(pair):
            return below([pair[:, i * size : (i + 1) * size] for i in range(together)])

        def own_part(value, i, n):
            return value[slot * i : slot * i + head_dim, i * n : (i + 1) * n]

        def all_keys(value):
            if keys == size:
                return value
            return jnp.concatenate([value, jnp.zeros((value.shape[0], size - keys), f32)], axis=1)

        def members(u):
            g, first = divmod(u * together, group)
            return g, range(first, first + together)

        def forward():
            q, k, v, scores, weights, outs = {}, {}, {}, {}, {}, {}
            for t in range(units + 2 * ahead):
                if t < units:
                    g, js = members(t)
                    if js[0] == 0:
                        q[g] = padded(load(0, g), one_row)
                        k[g] = jnp.concatenate(padded(load(width, g), mask_row), axis=0).T[:keys]
                        v[g] = padded(load(2 * width, g), one_row)
                    scores[t] = dot(k[g], beside([place(j, q[g][j]) for j in js]), 1, 0)
                u = t - ahead
                if 0 <= u < units:
                    s = scores.pop(u)
                    peak = jnp.max(s, axis=0, keepdims=True)
                    weights[u] = jnp.exp2((s - peak) * (scale * log2_e)).astype(bf16)
                    probs[u, :keys, : together * size] = weights[u]
                u = t - 2 * ahead
                if 0 <= u < units:
                    g, js = members(u)
                    o = dot(below([v[g][j] for j in js])[:, :keys], weights.pop(u), 1, 0)
                    for i, j in enumerate(js):
                        total = slot * i + head_dim
                        inverse = 1.0 / o[total : total + 1, i * size : (i + 1) * size]
                        linv_s[g * group + j, :, :size] = jnp.broadcast_to(inverse, (8, size))
                        outs[j] = own_part(o, i, size) * inverse
                    if js[-1] == group - 1:
                        parts = [outs.pop(j) for j in range(group)]
                        ctx_s[group_rows(0, g), :size] = jnp.concatenate(parts, axis=0)

        forward()

        pl.when(step == 0)(await_weights)
        live = (lax.broadcasted_iota(jnp.int32, (keys, 1), 0) < length).astype(f32)
        out_bias, gain, shift = vec_ref[4:5], vec_ref[5:6], vec_ref[6:7]
        in_bias, back_bias = vec_ref[7:8], vec_ref[8:9]

        strips = [slice(c, c + 256) for c in range(0, width, 256)]

        def row_mean(parts):
            return sum(jnp.sum(p, axis=1, keepdims=True) for p in parts) * (1.0 / width)

        def join(parts):
            return jnp.concatenate(parts, axis=1)

        d_ffn = cot_ref[:keys].astype(f32) * live
        gvec_ref[4] += fold_rows(d_ffn)
        d_ffn = d_ffn.astype(bf16)
        ctx_t = ctx_s[:, :size].astype(bf16)
        ctx = ctx_t.T[:keys]
        mixed = []
        for c in strips:
            attn = dot(ctx, wout_ref[:, c], 1, 0) + out_bias[:, c]
            mixed.append(tok_ref[:keys, c].astype(f32) + live * attn)
        d_act = [dot(d_ffn, wback_ref[c], 1, 1) for c in strips[:1]]
        mean = row_mean(mixed)
        centred = [m - mean for m in mixed]
        factor = lax.rsqrt(row_mean([v * v for v in centred]) + eps)
        unit = [v * factor for v in centred]
        normed = join(
            [(u * gain[:, c] + shift[:, c]).astype(bf16) for u, c in zip(unit, strips)]
        )
        act, d_pre = [], []

        def project(c):
            return dot(normed, win_ref[:, c], 1, 0) + in_bias[:, c]

        ahead_pre = [project(strips[0])]
        for i, c in enumerate(strips):
            if i + 1 < len(strips):
                ahead_pre.append(project(strips[i + 1]))
                d_act.append(dot(d_ffn, wback_ref[strips[i + 1]], 1, 1))
            pre = ahead_pre[i]
            cdf = 0.5 * (1.0 + lax.erf(pre * 0.7071067811865476))
            act.append((pre * cdf).astype(bf16))
            slope = cdf + pre * jnp.exp(-0.5 * pre * pre) * 0.3989422804014327
            low = (d_act[i] * slope).astype(bf16)
            gvec_ref[3, :, c] += fold_rows(low.astype(f32))
            d_pre.append(low)
        act, d_pre = join(act), join(d_pre)
        d_normed = [dot(d_pre, win_ref[c], 1, 1) for c in strips]
        for m, c in zip(mixed, strips):
            branch = dot(act, wback_ref[:, c], 1, 0) + back_bias[:, c]
            mixed_ref[:keys, c] = (m + live * branch).astype(bf16)
        act_t, normed_t = act.T, normed.T
        e = []
        for i, c in enumerate(strips):
            gback_ref[:, c] += dot(act_t, d_ffn[:, c], 1, 0)
            gvec_ref[1, :, c] += fold_rows(d_normed[i] * unit[i])
            gvec_ref[2, :, c] += fold_rows(d_normed[i])
            e.append(d_normed[i] * gain[:, c])
        mean = row_mean(e)
        inner = row_mean([v * u for v, u in zip(e, unit)])
        d_attn = []
        for i, c in enumerate(strips):
            gin_ref[:, c] += dot(normed_t, d_pre[:, c], 1, 0)
            d_mixed = cot_ref[:keys, c].astype(f32) + factor * (e[i] - mean - unit[i] * inner)
            dmix_ref[:keys, c] = d_mixed
            low = (live * d_mixed).astype(bf16)
            gvec_ref[0, :, c] += fold_rows(low.astype(f32))
            d_attn.append(low)
        d_attn = join(d_attn)
        for c in strips:
            d_ctx = dot(wout_ref[c], d_attn, 1, 1)
            dctx_s[c, :size] = all_keys(d_ctx).astype(bf16)
        for c in strips:
            gout_ref[:, c] += dot(ctx_t[:, :keys], d_attn[:, c], 1, 0)

        behind = 3 if size == block else 4

        def backward():
            q, k, v, d, d_probs, d_scores = {}, {}, {}, {}, {}, {}
            d_q, d_k, d_v = {}, {}, {}
            for t in range(units + 2 * behind):
                if t < units:
                    g, js = members(t)
                    if js[0] == 0:
                        q[g] = padded(load(0, g), one_row)
                        k[g] = padded(load(width, g), one_row)
                        v[g] = jnp.concatenate(padded(load(2 * width, g), two_rows), axis=0).T[:keys]
                        d_out = pieces(dctx_s[group_rows(0, g), :size].astype(f32))
                        out = pieces(ctx_s[group_rows(0, g), :size])
                        d[g] = []
                        for i in range(group):
                            scaled = d_out[i] * linv_s[g * group + i, :1, :size]
                            inner = -jnp.sum(scaled * out[i], axis=0, keepdims=True)
                            high = inner.astype(bf16).astype(f32)
                            blank = jnp.zeros((slot - head_dim - 2, size), f32)
                            tail = [scaled, high, inner - high, blank]
                            d[g].append(jnp.concatenate(tail, axis=0).astype(bf16))
                    d_probs[t] = dot(v[g], beside([place(j, d[g][j]) for j in js]), 1, 0)
                u = t - behind
                if 0 <= u < units:
                    p = probs[u, :keys, : together * size]
                    d_scores[u] = (p.astype(f32) * d_probs.pop(u)).astype(bf16)
                u = t - 2 * behind
                if 0 <= u < units:
                    g, js = members(u)
                    ds = d_scores.pop(u)
                    p = stacked(probs[u, :keys, : together * size])
                    to_v = dot(below([d[g][j] for j in js]), p, 1, 1)
                    to_q = dot(below([k[g][j] for j in js])[:, :keys], ds, 1, 0)
                    to_k = dot(below([q[g][j] for j in js]), stacked(ds), 1, 1)
                    for i, j in enumerate(js):
                        d_v[j] = all_keys(own_part(to_v, i, keys))
                        d_q[j] = own_part(to_q, i, size) * scale
                        d_k[j] = all_keys(own_part(to_k, i, keys) * scale)
                    if js[-1] == group - 1:
                        for base, parts in ((0, d_q), (width, d_k), (2 * width, d_v)):
                            some = [parts.pop(j) for j in range(group)]
                            dqkv_ref[group_rows(base, g), :size] = jnp.concatenate(
                                some, axis=0
                            ).astype(bf16)

        backward()

        if keys < block:
            mixed_ref[keys:] = tok_ref[keys:]
            dmix_ref[keys:] = cot_ref[keys:].astype(f32)
        if size < block:
            dqkv_ref[:, size:] = jnp.zeros((3 * width, block - size), bf16)

    half = block // 2

    pl.when((step == 0) & (length == 0))(await_weights)

    @pl.when(length == 0)
    def _():
        mixed_ref[...] = tok_ref[...]
        dmix_ref[...] = cot_ref[...].astype(f32)
        dqkv_ref[...] = jnp.zeros_like(dqkv_ref)

    @pl.when((length > 0) & (length <= half))
    def _():
        run(half, half)

    more = half + half // 2

    @pl.when((length > half) & (length <= more))
    def _():
        run(block, more)

    @pl.when(length > more)
    def _():
        run(block, block)

    if packed:

        @pl.when(first)
        def _():
            mixed_out[...] = mixed_ref[...]

        @pl.when(jnp.logical_not(first))
        def _():
            mixed_odd[...] = mixed_ref[...]

    else:
        mixed_out[...] = mixed_ref[...]

    if packed:

        @pl.when(step == pl.num_programs(0) - 1)
        def _():
            columns = width // 2
            for i in range(DEVICES):
                p = (i % 2) * CHIPS + i // 2
                rows = slice(SHARD * i, SHARD * (i + 1))
                top = jnp.concatenate([gout_ref[rows], gback_ref[rows, :columns]], axis=1)
                bottom = jnp.concatenate([gin_ref[rows], gback_ref[rows, columns:]], axis=1)
                packed_ref[p] = jnp.concatenate([top, bottom], axis=0).astype(bf16)


def middle(lengths, qkv, tokens, cotangent, w_out, w_in, w_back, vectors, packed):
    slots, wide, block = qkv.shape
    rows, width = slots * block, wide // 3
    square = (width, width)
    shared = slots // 2

    def whole(shape):
        return pl.BlockSpec(shape, lambda m: (0,) * len(shape))

    by_rows = pl.BlockSpec((block, width), lambda m: (m, 0))
    if packed:
        first = pl.BlockSpec((block, width), lambda m: (2 * jnp.minimum(m, shared - 1), 0))
        second = pl.BlockSpec((block, width), lambda m: (jnp.maximum(m - shared, 0), 0))
    else:
        first = pl.BlockSpec((block, width), lambda m: (jnp.minimum(m, shared - 1), 0))
        second = pl.BlockSpec((block, width), lambda m: (jnp.maximum(m, shared), 0))
    out_specs = [
        by_rows,
        by_rows,
        pl.BlockSpec((3 * width, block), lambda m: (0, m)),
        whole((5, 8, width)),
    ]
    out_shape = [
        jax.ShapeDtypeStruct((rows, width), bf16),
        jax.ShapeDtypeStruct((rows, width), f32),
        jax.ShapeDtypeStruct((3 * width, rows), bf16),
        jax.ShapeDtypeStruct((5, 8, width), f32),
    ]
    scratch = [
        pltpu.VMEM((HEADS, block, block), bf16),
        pltpu.VMEM((width, block), f32),
        pltpu.VMEM((HEADS, 8, block), f32),
        pltpu.VMEM((width, block), bf16),
        pltpu.VMEM((block, width), bf16),
        pltpu.VMEM((block, width), bf16),
        pltpu.VMEM((block, width), bf16),
    ]
    if packed:
        shape = (DEVICES, 2 * SHARD, width + width // 2)
        out_specs[0] = first
        out_specs += [second, whole(shape)]
        out_shape.append(jax.ShapeDtypeStruct((rows // 2, width), bf16))
        out_shape.append(jax.ShapeDtypeStruct(shape, bf16))
        scratch = [pltpu.VMEM(square, f32)] * 3 + scratch
    else:
        out_specs += [whole(square)] * 3
        out_shape += [jax.ShapeDtypeStruct(square, f32)] * 3
    scratch += [pltpu.VMEM(square, bf16)] * 3 + [pltpu.SemaphoreType.DMA((3,))]
    return pl.pallas_call(
        functools.partial(middle_kernel, packed, width // HEADS),
        grid=(slots,),
        in_specs=[
            pl.BlockSpec(memory_space=pltpu.SMEM),
            pl.BlockSpec((None, 3 * width, block), lambda m: (m, 0, 0)),
            first,
            second,
            first,
            second,
            pl.BlockSpec(memory_space=pl.ANY),
            pl.BlockSpec(memory_space=pl.ANY),
            pl.BlockSpec(memory_space=pl.ANY),
            whole((16, width)),
        ],
        out_specs=out_specs,
        scratch_shapes=scratch,
        out_shape=out_shape,
        compiler_params=pltpu.CompilerParams(vmem_limit_bytes=58 * MIB),
    )(lengths, qkv, *tokens, *cotangent, w_out, w_in, w_back, vectors)


def scatter_kernel(
    sr_hbm,
    dqkv_hbm,
    unit_hbm,
    fq_hbm,
    tok_hbm,
    odd_hbm,
    dmix_hbm,
    mixed_hbm,
    vec_ref,
    gvec_ref,
    grad_hbm,
    grad_out,
    mixed_out,
    gq_ref,
    gr_ref,
    sq,
    sr,
    rq_sib,
    rr_sib,
    rq,
    rr,
    dqkv,
    unit_t,
    fq,
    tok,
    dmix,
    grad,
    mixed,
    gain_wide,
    shift_wide,
    small_wide,
    sums,
    result,
    send_sem,
    recv_sem,
    swap_send,
    swap_recv,
    copy_sem,
):
    at = Place()
    at.greet()
    rows, width = tok.shape
    wide = 3 * width
    half_q = wide // 2
    slots = 8
    block = rows // slots
    mine, theirs = at.c * CHIPS, (1 - at.c) * CHIPS
    own = at.block(at.c, at.z, at.y, at.x)
    level_rows = 8 * SHARD

    def local(src, dst, i):
        copy = pltpu.make_async_copy(src, dst, copy_sem.at[i])
        copy.start()
        return copy

    sr_in = local(sr_hbm, sr, 0)
    unit_in = local(unit_hbm, unit_t, 1)
    parts_in = []
    for part in range(3):
        some = pl.ds(part * width, width)
        parts_in.append(local(dqkv_hbm.at[some], dqkv.at[some], 2 + 2 * part))
        parts_in.append(local(fq_hbm.at[:, some], fq.at[:, some], 3 + 2 * part))

    def part_wait(part):
        for copy in parts_in[2 * part : 2 * part + 2]:
            copy.wait()

    shared = slots // 2

    def rows_of(i, count=1):
        return pl.ds(i * block, count * block)

    mixed_in = local(mixed_hbm, mixed, 8)
    late = [local(dmix_hbm, dmix, 9), local(odd_hbm, tok.at[rows_of(shared, shared)], 10)]
    for i in range(shared):
        late.append(local(tok_hbm.at[rows_of(2 * i)], tok.at[rows_of(i)], 11 + i))

    def swap_copy(src, dst, i):
        return pltpu.make_async_remote_copy(
            src_ref=src,
            dst_ref=dst,
            send_sem=swap_send.at[i],
            recv_sem=swap_recv.at[i],
            device_id=(at.sib,),
            device_id_type=MESH,
        )

    slabs = (
        (sq, rq_sib, rq, 0, 640),
        (sq, rq_sib, rq, 640, 640),
        (sr, rr_sib, rr, 0, 1152),
    )

    def cut(ref, k, first, count):
        return ref.at[pl.ds(first, count), :, pl.ds(slabs[k][3], slabs[k][4])]

    def piece(ref, k, p):
        _, _, _, column, columns = slabs[k]
        return ref[p, :, column : column + columns].astype(f32)

    def put(k, p, value):
        slab, _, _, column, columns = slabs[k]
        slab[p, :, column : column + columns] = value.astype(bf16)

    def remote(k, src, dst, target, sem):
        return pltpu.make_async_remote_copy(
            src_ref=src,
            dst_ref=dst,
            send_sem=send_sem.at[k],
            recv_sem=recv_sem.at[k, sem],
            device_id=(target,),
            device_id_type=MESH,
        )

    def x_type(j):
        return at.block(at.c, j, at.y, 1 - at.x)

    def y_type(j):
        return at.block(at.c, j, 1 - at.y, at.x)

    def corner_type(j):
        return at.block(at.c, j, 1 - at.y, 1 - at.x)

    def column_type(j):
        return at.block(at.c, j, at.y, at.x)

    def sib_copy(k, j):
        src = cut(slabs[k][0], k, theirs + 4 * j, 4)
        return remote(k, src, cut(slabs[k][1], k, 4 * j, 4), at.sib, j)

    def sib_send(k, j):
        sib_copy(k, j).start()

    def step_copy(k, src, slot, target):
        src = cut(slabs[k][0], k, src, 1)
        return remote(k, src, cut(slabs[k][2], k, slot, 1), target, PLANES + slot)

    def x_send(k, j):
        step_copy(k, x_type(j), 4 + j, at.xn).start()

    def y_send(k, j):
        step_copy(k, y_type(j), 8 + j, at.yn).start()

    def sib_add(k, j):
        sib_copy(k, j).wait_recv()

        def body(i, carry):
            p = mine + 4 * j + i
            put(k, p, piece(slabs[k][0], k, p) + piece(slabs[k][1], k, 4 * j + i))
            return carry

        lax.fori_loop(0, 4, body, 0)
        step_copy(k, corner_type(j), j, at.yn if j % 2 == 0 else at.xn).start()
        (y_send if j % 2 == 0 else x_send)(k, j)

    def corner_add(k, j):
        step_copy(k, own, j, at.sib).wait_recv()
        p = x_type(j) if j % 2 == 0 else y_type(j)
        put(k, p, piece(slabs[k][0], k, p) + piece(slabs[k][2], k, j))
        (x_send if j % 2 == 0 else y_send)(k, j)

    def plane_add(k, j):
        p = column_type(j)
        step_copy(k, own, 4 + j, at.sib).wait_recv()
        step_copy(k, own, 8 + j, at.sib).wait_recv()
        received = piece(slabs[k][2], k, 4 + j) + piece(slabs[k][2], k, 8 + j)
        put(k, p, piece(slabs[k][0], k, p) + received)

        @pl.when(at.z != j)
        def _():
            step_copy(k, p, 12 + at.z, at.me + 8 * (j - at.z)).start()

    def land(k):
        total = gq_ref if slabs[k][0] is sq else gr_ref
        columns = slice(slabs[k][3], slabs[k][3] + slabs[k][4])
        total[:, columns] = piece(slabs[k][0], k, own)
        for j in range(PLANES):

            @pl.when(at.z != j)
            def _():
                step_copy(k, own, 12 + j, at.sib).wait_recv()
                total[:, columns] += piece(slabs[k][2], k, 12 + j)

    def prepare(part):
        columns = slice(part * width, (part + 1) * width)
        sums[:, columns] = dot(jnp.ones((16, rows), bf16), dqkv[columns], 1, 1)[:8]
        if part == 0:
            gain_wide[...] = jnp.broadcast_to(vec_ref[0:1], (128, width)).T
            shift_wide[...] = jnp.broadcast_to(vec_ref[1:2], (128, width)).T
            small_wide[...] = jnp.zeros((width, 128), f32)
        if part == 2:
            lines = [jnp.zeros((2, width), f32), sums[0:1, :width], sums[0:1, 2 * width :]]
            lines += [jnp.sum(gvec_ref[i], axis=0, keepdims=True) for i in range(5)]
            lines.append(jnp.zeros((128 - VECTORS, width), f32))
            small_wide[...] += jnp.concatenate(lines, axis=0).T

    def weight_grad(j, part):
        lines = pl.ds(pl.multiple_of(j * level_rows, level_rows), level_rows)
        columns = pl.ds(pl.multiple_of(part * width, width), width)
        product = dot(unit_t[lines], dqkv[columns], 1, 1)
        weight = fq[lines, columns].astype(f32)
        line = sums[0:1, columns]
        gain_sum = jnp.sum(weight * product, axis=1, keepdims=True)
        shift_sum = jnp.sum(weight * line, axis=1, keepdims=True)
        lane = lax.broadcasted_iota(jnp.int32, (level_rows, 128), 1)
        small_wide[lines] += jnp.where(
            lane == 0, gain_sum, jnp.where(lane == 1, shift_sum, 0.0)
        )
        gain = jnp.concatenate([gain_wide[lines]] * (width // 128), axis=1)
        shift = jnp.concatenate([shift_wide[lines]] * (width // 128), axis=1)
        result[:, columns] = gain * product + shift * line

        @pl.when(part == 2)
        def _():
            small = small_wide[lines]
            blank = jnp.zeros((SHARD, 128), f32)
            for i in range(8):
                p = (i % 2) * CHIPS + 4 * j + i // 2
                some = slice(SHARD * i, SHARD * (i + 1))
                top = jnp.concatenate([result[some, :half_q], small[some]], axis=1)
                bottom = jnp.concatenate([result[some, half_q:], blank], axis=1)
                sq[p] = jnp.concatenate([top, bottom], axis=0).astype(bf16)

    def grad_rows(m):
        return pl.ds(pl.multiple_of(m * block, block), block)

    def grad_copy(m):
        return pltpu.make_async_copy(
            grad.at[grad_rows(m)], grad_hbm.at[grad_rows(m)], copy_sem.at[11 + shared + m]
        )

    def input_grad(m):
        some = grad_rows(m)
        d_normed = dot(fq[...], dqkv[:, some], 1, 0).T
        unit, factor = normalize(tok[some].astype(f32))
        share = norm_backward(d_normed, vec_ref[0:1], unit, factor)
        grad[some] = (dmix[some] + share).astype(bf16)

        @pl.when(m < shared)
        def _():
            grad_copy(m).start()

        @pl.when(m >= shared)
        def _():
            swap_copy(grad.at[some], grad_out.at[grad_rows(m - shared)], 0).start()

    def late_wait():
        for copy in late:
            copy.wait()

    sr_in.wait()
    at.await_all()
    sib_send(2, 2)
    sib_send(2, 1)
    sib_send(2, 0)
    sib_add(2, 2)
    sib_send(2, 3)
    sib_add(2, 1)
    unit_in.wait()
    part_wait(0)
    prepare(0)
    sib_add(2, 0)
    part_wait(1)
    sib_add(2, 3)
    prepare(1)

    def beside_weight_0():
        part_wait(2)
        prepare(2)

    def beside_weight_2():
        sib_send(1, 0)

    def beside_weight_4():
        corner_add(2, 0)
        corner_add(2, 1)
        sib_send(0, 0)

    def beside_weight_5():
        sib_send(0, 3)
        corner_add(2, 3)

    def beside_weight_6():
        corner_add(2, 2)

    def beside_weight_7():
        sib_add(0, 0)
        sib_add(0, 3)
        plane_add(2, 0)

    def beside_weight_8():
        sib_send(0, 1)
        sib_add(1, 0)
        plane_add(2, 3)

    def beside_weight_9():
        sib_add(0, 1)

    def beside_weight_10():
        corner_add(0, 3)
        sib_send(1, 3)


    def beside_weight_step(i, carry):
        turn = i // 3
        j = jnp.where(turn == 0, 0, jnp.where(turn == 1, 3, jnp.where(turn == 2, 1, 2)))
        weight_grad(j, lax.rem(i, 3))
        pl.when(i == 0)(beside_weight_0)
        pl.when(i == 2)(beside_weight_2)
        pl.when(i == 4)(beside_weight_4)
        pl.when(i == 5)(beside_weight_5)
        pl.when(i == 6)(beside_weight_6)
        pl.when(i == 7)(beside_weight_7)
        pl.when(i == 8)(beside_weight_8)
        pl.when(i == 9)(beside_weight_9)
        pl.when(i == 10)(beside_weight_10)
        return carry

    lax.fori_loop(0, 12, beside_weight_step, 0)
    corner_add(0, 0)
    sib_send(1, 2)
    plane_add(2, 2)
    sib_send(0, 2)
    corner_add(0, 1)
    plane_add(2, 1)
    sib_add(1, 3)
    sib_send(1, 1)
    mixed_in.wait()
    swap_copy(mixed, mixed_out, 1).start()
    late_wait()
    sib_add(1, 2)
    plane_add(0, 3)
    corner_add(1, 0)
    sib_add(0, 2)

    def beside_input_0():
        plane_add(0, 0)
        corner_add(1, 3)
        corner_add(1, 2)
        sib_add(1, 1)
        plane_add(0, 1)

    def beside_input_1():
        corner_add(0, 2)
        plane_add(1, 2)
        plane_add(1, 0)

    def beside_input_2():
        corner_add(1, 1)
        plane_add(1, 3)

    def beside_input_4():
        plane_add(0, 2)
        plane_add(1, 1)

    def beside_input_6():
        land(2)


    def beside_input_step(i, carry):
        input_grad(i)
        pl.when(i == 0)(beside_input_0)
        pl.when(i == 1)(beside_input_1)
        pl.when(i == 2)(beside_input_2)
        pl.when(i == 4)(beside_input_4)
        pl.when(i == 6)(beside_input_6)
        return carry

    lax.fori_loop(0, 8, beside_input_step, 0)
    land(0)
    land(1)
    for k in range(len(slabs)):
        every = cut(slabs[k][0], k, 0, DEVICES - 1)
        remote(k, every, every, at.sib, 0).wait_send()
    for m in range(shared):
        grad_copy(m).wait()
    swap_copy(grad.at[rows_of(shared, shared)], grad_out, 0).wait()
    swap_copy(mixed, mixed_out, 1).wait()


def scatter(packed, dqkv, unit_t, full_qkv, tokens, odd_tokens, d_mixed, mixed, vectors, sums):
    rows, width = tokens.shape
    wide = 3 * width
    vmem = pl.BlockSpec(memory_space=pltpu.VMEM)
    anywhere = pl.BlockSpec(memory_space=pl.ANY)
    tall = 2 * SHARD
    widths = (wide // 2 + 128, wide // 2)
    return pl.pallas_call(
        scatter_kernel,
        out_shape=[jax.ShapeDtypeStruct((rows // 2, width), bf16)] * 3
        + [jax.ShapeDtypeStruct((tall, w), f32) for w in widths],
        in_specs=[anywhere] * 8 + [vmem] * 2,
        out_specs=[anywhere] * 3 + [vmem] * 2,
        scratch_shapes=[pltpu.VMEM((DEVICES, tall, w), bf16) for w in widths]
        + [pltpu.VMEM((CHIPS, tall, w), bf16) for w in widths]
        + [pltpu.VMEM((4 * PLANES, tall, w), bf16) for w in widths]
        + [
            pltpu.VMEM((wide, rows), bf16),
            pltpu.VMEM((width, rows), bf16),
            pltpu.VMEM((width, wide), bf16),
            pltpu.VMEM((rows, width), bf16),
            pltpu.VMEM((rows, width), f32),
            pltpu.VMEM((rows, width), bf16),
            pltpu.VMEM((rows // 2, width), bf16),
            pltpu.VMEM((width, 128), f32),
            pltpu.VMEM((width, 128), f32),
            pltpu.VMEM((width, 128), f32),
            pltpu.VMEM((8, wide), f32),
            pltpu.VMEM((8 * SHARD, wide), f32),
            pltpu.SemaphoreType.DMA((3,)),
            pltpu.SemaphoreType.DMA((3, 5 * PLANES)),
            pltpu.SemaphoreType.DMA((2,)),
            pltpu.SemaphoreType.DMA((2,)),
            pltpu.SemaphoreType.DMA((19,)),
        ],
        compiler_params=pltpu.CompilerParams(
            collective_id=1, has_side_effects=True, vmem_limit_bytes=60 * MIB
        ),
    )(packed, dqkv, unit_t, full_qkv, tokens, odd_tokens, d_mixed, mixed, vectors, sums)


def finish_kernel(
    _, mixed_odd, grad_even, grad_odd, q_ref, r_ref, mixed, grad, g_qkv, g_out, g_in, g_back, *lines
):
    block = mixed_odd.shape[0]
    mixed[...] = mixed_odd[...]
    grad[:block] = grad_even[...]
    grad[block:] = grad_odd[...]

    @pl.when(pl.program_id(0) == 0)
    def _():
        width = g_out.shape[1]
        half_q = 3 * width // 2
        half = width // 2
        g_qkv[:, :half_q] = q_ref[:SHARD, :half_q]
        g_qkv[:, half_q:] = q_ref[SHARD:, :half_q]
        g_out[...] = r_ref[:SHARD, :width]
        g_in[...] = r_ref[SHARD:, :width]
        g_back[:, :half] = r_ref[:SHARD, width:]
        g_back[:, half:] = r_ref[SHARD:, width:]
        small = q_ref[:SHARD, half_q:].T
        for i, line in enumerate(lines):
            line[...] = small[i, :SHARD]


def finish(mixed, mixed_odd, grad, grad_odd, q_part, r_part, slots):
    rows, width = mixed.shape
    block = rows // slots
    single = pl.BlockSpec((block, width), lambda i: (i, 0))
    double = pl.BlockSpec((2 * block, width), lambda i: (i, 0))

    def whole(shape):
        return pl.BlockSpec(shape, lambda i: (0,) * len(shape))

    shapes = [(SHARD, 3 * width)] + [(SHARD, width)] * 3 + [(SHARD,)] * 9
    return pl.pallas_call(
        finish_kernel,
        grid=(slots // 2,),
        out_shape=[jax.ShapeDtypeStruct((rows, width), bf16)] * 2
        + [jax.ShapeDtypeStruct(s, f32) for s in shapes],
        in_specs=[pl.BlockSpec(memory_space=pl.ANY)]
        + [single] * 3
        + [whole(q_part.shape), whole(r_part.shape)],
        out_specs=[pl.BlockSpec((block, width), lambda i: (2 * i + 1, 0)), double]
        + [whole(s) for s in shapes],
        input_output_aliases={0: 0},
    )(mixed, mixed_odd, grad, grad_odd, q_part, r_part)


def on_one_plan(tokens, mol_len, cotangent, vectors, w_qkv, w_out, w_in, w_back):
    slots = mol_len.shape[0]
    (
        qkv,
        unit_t,
        full_qkv,
        full_out,
        full_in,
        full_back,
        odd_tokens,
        odd_cotangent,
        lines,
        lengths,
    ) = gather_and_project(mol_len, vectors, w_qkv, w_out, w_in, w_back, tokens, cotangent)
    mixed, d_mixed, dqkv, sums, mixed_sent, packed = middle(
        lengths,
        qkv,
        (tokens, odd_tokens),
        (cotangent, odd_cotangent),
        full_out,
        full_in,
        full_back,
        lines,
        True,
    )
    grad, grad_odd, mixed_odd, q_part, r_part = scatter(
        packed, dqkv, unit_t, full_qkv, tokens, odd_tokens, d_mixed, mixed_sent, lines, sums
    )
    mixed_out, token_grad, g_qkv, g_out, g_in, g_back, *small = finish(
        mixed, mixed_odd, grad, grad_odd, q_part, r_part, slots
    )
    return mixed_out, token_grad, small, g_qkv, g_out, g_in, g_back


def on_any_plan(tokens, mol_len, cotangent, vectors, w_qkv, w_out, w_in, w_back):
    slots = mol_len.shape[0]
    rows, width = tokens.shape

    def gather(array, axis):
        return lax.all_gather(array, "fsdp", axis=axis, tiled=True)

    lines = gather(jnp.stack(vectors), 1).astype(f32)
    lines = jnp.pad(lines, ((0, 16 - len(vectors)), (0, 0)))
    full_qkv, full_out, full_in, full_back = (
        gather(w, 0) for w in (w_qkv, w_out, w_in, w_back)
    )
    unit, factor = normalize(tokens.astype(f32))
    normed = (unit * lines[0] + lines[1]).astype(bf16)
    qkv = jnp.dot(normed, full_qkv, preferred_element_type=f32)
    qkv = (qkv + jnp.concatenate([lines[2], jnp.zeros_like(lines[2]), lines[3]])).astype(bf16)
    qkv = qkv.reshape(slots, rows // slots, 3 * width).transpose(0, 2, 1)
    mixed_out, d_mixed, dqkv, sums, g_out, g_in, g_back = middle(
        jnp.broadcast_to(mol_len[:, None], (slots, 128)),
        qkv,
        (tokens, tokens),
        (cotangent, cotangent),
        full_out,
        full_in,
        full_back,
        lines,
        False,
    )
    g_qkv = jnp.einsum("rf,dr->fd", normed, dqkv, preferred_element_type=f32)
    d_normed = jnp.einsum("dr,fd->rf", dqkv, full_qkv, preferred_element_type=f32)
    totals = jnp.sum(dqkv.astype(f32), axis=1)
    small = [jnp.sum(d_normed * unit, axis=0), jnp.sum(d_normed, axis=0)]
    small += [totals[:width], totals[2 * width :]]
    small += [jnp.sum(sums[i], axis=0) for i in range(5)]
    share = norm_backward(d_normed, lines[0], unit, factor)
    token_grad = (d_mixed + share).astype(bf16)

    def scatter_sum(array, axis):
        return lax.psum_scatter(array, "fsdp", scatter_dimension=axis, tiled=True)

    small = scatter_sum(jnp.stack(small), 1)
    return (
        mixed_out,
        token_grad,
        [small[i] for i in range(9)],
        *(scatter_sum(g, 0) for g in (g_qkv, g_out, g_in, g_back)),
    )


def per_device(
    devices,
    tokens,
    mol_len,
    cotangent,
    ln1_gain,
    ln1_bias,
    w_qkv,
    q_bias,
    v_bias,
    w_out,
    out_bias,
    ln2_gain,
    ln2_bias,
    w_in,
    in_bias,
    w_back,
    back_bias,
):
    vectors = [
        ln1_gain,
        ln1_bias,
        q_bias,
        v_bias,
        out_bias,
        ln2_gain,
        ln2_bias,
        in_bias,
        back_bias,
    ]
    known = devices == DEVICES and w_qkv.shape[0] == SHARD
    plan = on_one_plan if known else on_any_plan
    mixed_out, token_grad, small, g_qkv, g_out, g_in, g_back = plan(
        tokens, mol_len, cotangent, vectors, w_qkv, w_out, w_in, w_back
    )
    return (
        mixed_out,
        token_grad,
        small[0],
        small[1],
        g_qkv,
        small[2],
        small[3],
        g_out,
        small[4],
        small[5],
        small[6],
        g_in,
        small[7],
        g_back,
        small[8],
    )


def solution(mesh):
    line, matrix = P("fsdp"), P("fsdp", None)
    return jax.shard_map(
        functools.partial(per_device, mesh.shape["fsdp"]),
        mesh=mesh,
        in_specs=(
            matrix,
            line,
            matrix,
            line,
            line,
            matrix,
            line,
            line,
            matrix,
            line,
            line,
            line,
            matrix,
            line,
            matrix,
            line,
        ),
        out_specs=(
            matrix,
            matrix,
            line,
            line,
            matrix,
            line,
            line,
            matrix,
            line,
            line,
            line,
            matrix,
            line,
            matrix,
            line,
        ),
        check_vma=False,
    )
```
